32 devices in a mesh: dp: 8 (over z, y), fsdp: 4 (over x, core).
Axes of the slice: x: 2, y: 2, z: 4, core: 2. Of those that a mesh axis runs over, the one named last changes fastest.
Arguments:
- tokens: bfloat16 [32, 1024, 768], P(('dp', 'fsdp')), may hold values from -6 to 6
- lengths: int32 [32, 16], P(('dp', 'fsdp')), may hold values from 1 to 512, 1024 in all within a row
- cotangent: bfloat16 [32, 1024, 768], P(('dp', 'fsdp')), may hold values from -6 to 6
- w_query: bfloat16 [768, 768], P(('dp', 'fsdp')), may hold values from -0.21875 to 0.21875
- w_key: bfloat16 [768, 768], P(('dp', 'fsdp')), may hold values from -0.21875 to 0.21875
- w_value: bfloat16 [768, 768], P(('dp', 'fsdp')), may hold values from -0.21875 to 0.21875
- w_out: bfloat16 [768, 768], P(('dp', 'fsdp')), may hold values from -0.875 to 0.875
- b_query: bfloat16 [768], P(('dp', 'fsdp')), may hold values from -3 to 3
- b_value: bfloat16 [768], P(('dp', 'fsdp')), may hold values from -3 to 3
- b_out: bfloat16 [768], P(('dp', 'fsdp')), may hold values from -3 to 3
- norm1_gain: bfloat16 [768], P(('dp', 'fsdp')), may hold values from 0.099609375 to 1.8984375
- norm1_shift: bfloat16 [768], P(('dp', 'fsdp')), may hold values from -3 to 3
- w_in: bfloat16 [768, 3072], P(('dp', 'fsdp')), may hold values from -0.21875 to 0.21875
- w_back: bfloat16 [3072, 768], P(('dp', 'fsdp')), may hold values from -0.109375 to 0.109375
- b_in: bfloat16 [3072], P(('dp', 'fsdp')), may hold values from -3 to 3
- b_back: bfloat16 [768], P(('dp', 'fsdp')), may hold values from -3 to 3
- norm2_gain: bfloat16 [768], P(('dp', 'fsdp')), may hold values from 0.099609375 to 1.8984375
- norm2_shift: bfloat16 [768], P(('dp', 'fsdp')), may hold values from -3 to 3
Outputs:
- mixed: bfloat16 [32, 1024, 768], P(('dp', 'fsdp'))
- grad_tokens: float32 [32, 1024, 768], P(('dp', 'fsdp'))
- grad_w_query: float32 [768, 768], P(('dp', 'fsdp'))
- grad_w_key: float32 [768, 768], P(('dp', 'fsdp'))
- grad_w_value: float32 [768, 768], P(('dp', 'fsdp'))
- grad_w_out: float32 [768, 768], P(('dp', 'fsdp'))
- grad_b_query: float32 [768], P(('dp', 'fsdp'))
- grad_b_value: float32 [768], P(('dp', 'fsdp'))
- grad_b_out: float32 [768], P(('dp', 'fsdp'))
- grad_norm1_gain: float32 [768], P(('dp', 'fsdp'))
- grad_norm1_shift: float32 [768], P(('dp', 'fsdp'))
- grad_w_in: float32 [768, 3072], P(('dp', 'fsdp'))
- grad_w_back: float32 [3072, 768], P(('dp', 'fsdp'))
- grad_b_in: float32 [3072], P(('dp', 'fsdp'))
- grad_b_back: float32 [768], P(('dp', 'fsdp'))
- grad_norm2_gain: float32 [768], P(('dp', 'fsdp'))
- grad_norm2_shift: float32 [768], P(('dp', 'fsdp'))
The draws below stay inside these ranges and needn't reach their ends.
Inputs may be any that keep to these rules, and one draw needn't show every extreme that they name: Each row's 16 passage lengths sum to 1024; exactly one of them is 512.
All inputs are finite; a program needn't handle non-finite values.
Results may differ from the reference program's by a relative error of at most 0.014.
Values may be sent and summed in bfloat16 or wider, within the bound.
No kernel may reach another device: no remote copies, remote signals or barrier semaphores. Data moves between devices by JAX's collectives and lax.ppermute only.
A program may use at most 192 MiB of HBM per device.

```python
import math
import jax
import jax.numpy as jnp
import numpy as np
from jax import lax

D = 768
HEADS = 12
HEAD_DIM = 64
FF = 3072
SEQ = 1024
NSEG = 16
LONGEST = 512
ROWS = 32


def strengthened(entries, stream_key, source, target, shards_of, factor):
    def block_of(dim):
        return (jnp.arange(entries.shape[dim]) // (entries.shape[dim] // shards_of)).reshape((-1,) + (1,) * (entries.ndim - 1 - dim))

    near = jax.random.permutation(stream_key, shards_of)[block_of(target)]
    far = (block_of(target) + shards_of // 2) % shards_of
    return jnp.where((block_of(source) == near) | (block_of(source) == far), factor * entries, entries)


def block_scale(stream_key, extent, pieces, least, largest):
    def one(dim, parts):
        steps = jax.random.uniform(jax.random.fold_in(jax.random.fold_in(stream_key, 6), dim), (parts,), jnp.float32, least / len(pieces), largest / len(pieces))
        return jnp.repeat(jnp.exp(steps), extent[dim] // parts).reshape((-1,) + (1,) * (len(extent) - dim - 1))

    factor_of = one(*pieces[0])
    for cut in pieces[1:]:
        factor_of = factor_of * one(*cut)
    return factor_of


def length_profile(count, total, most, skew):
    portions = [(1 << 20) // math.isqrt(rank ** skew) + 1 for rank in range(2, count + 1)]
    spare, counts = total - most - (count - 1), [1] * (count - 1)
    while spare > 0:
        movable = [i for i in range(count - 1) if counts[i] < most]
        whole, budget = sum([portions[i] for i in movable]), spare
        for i in movable:
            addition = min(most - counts[i], max(1, budget * portions[i] // whole), spare)
            counts[i] = counts[i] + addition
            spare = spare - addition
    return np.array([most] + counts)


def ragged_sizes(key, number_of, total, most, lean):
    if number_of == 2:
        one = jax.random.randint(key, (), max(1, total - most), min(most, total - 1) + 1)
        return jnp.stack([one, total - one])
    sizes = jnp.asarray(length_profile(number_of, total, most, lean), jnp.int32)
    twos = (number_of - 1) // 2
    source_of, sink = sizes[1:1 + 2 * twos:2], sizes[2:2 + 2 * twos:2]
    margin = jnp.minimum(source_of - 1, most - sink)
    moved = jax.random.randint(jax.random.fold_in(key, 1), (twos,), 0, 1 << 20) % (margin + 1)
    sizes = sizes.at[1:1 + 2 * twos:2].set(source_of - moved).at[2:2 + 2 * twos:2].set(sink + moved)
    return sizes[jax.random.permutation(jax.random.fold_in(key, 2), number_of)]


def gaussian(key, dims, spread, reach, pieces=(), held_as=jnp.bfloat16):
    values = spread * jax.random.normal(key, dims, jnp.float32)
    if pieces:
        values = values * block_scale(key, dims, pieces, -0.22, 0.18)
    return jnp.clip(values, -reach, reach).astype(held_as)


def bell_draw_with(own_key, extent, scale, limit, cuts, heavy, held_as=jnp.bfloat16):
    array = scale * jax.random.normal(own_key, extent, jnp.float32)
    if cuts:
        array = array * block_scale(own_key, extent, cuts, -0.22, 0.18)
    return jnp.clip(strengthened(array, jax.random.fold_in(own_key, 3), *heavy), -limit, limit).astype(held_as)


def setup_inputs(seed: int = 0) -> dict:
    key_list = jax.random.split(jax.random.key(seed), 19)
    tokens = bell_draw_with(key_list[0], (ROWS, SEQ, D), 1.0, 6.0, ((0, 32),), (0, 2, 32, 2.75))
    lengths = jax.vmap(lambda own: ragged_sizes(own, NSEG, SEQ, LONGEST, 2))(jax.random.split(key_list[1], ROWS)).reshape((ROWS, NSEG)).astype(jnp.int32)
    cotangent = gaussian(key_list[2], (ROWS, SEQ, D), 1.0, 6.0, ((0, 32),))
    w_query = gaussian(key_list[3], (D, D), D ** -0.5, 0.21875, ((0, 32),))
    w_key = gaussian(key_list[4], (D, D), D ** -0.5, 0.21875, ((0, 32),))
    w_value = gaussian(key_list[5], (D, D), D ** -0.5, 0.21875, ((0, 32),))
    w_out = gaussian(key_list[6], (D, D), (D // 16) ** -0.5, 0.875, ((0, 32),))
    b_query = gaussian(key_list[7], (D,), 0.5, 3.0, ((0, 32),))
    b_value = gaussian(key_list[8], (D,), 0.5, 3.0, ((0, 32),))
    b_out = gaussian(key_list[9], (D,), 0.5, 3.0, ((0, 32),))
    norm1_gain = jnp.clip(1.0 + 0.18 * jax.random.normal(key_list[10], (D,), jnp.float32), 0.099609375, 1.8984375).astype(jnp.bfloat16)
    norm1_shift = gaussian(key_list[11], (D,), 0.5, 3.0, ((0, 32),))
    w_in = gaussian(key_list[12], (D, FF), D ** -0.5, 0.21875, ((0, 32),))
    w_back = gaussian(key_list[13], (FF, D), FF ** -0.5, 0.109375, ((0, 32),))
    b_in = gaussian(key_list[14], (FF,), 0.5, 3.0, ((0, 32),))
    b_back = gaussian(key_list[15], (D,), 0.5, 3.0, ((0, 32),))
    norm2_gain = jnp.clip(1.0 + 0.18 * jax.random.normal(key_list[16], (D,), jnp.float32), 0.099609375, 1.8984375).astype(jnp.bfloat16)
    norm2_shift = gaussian(key_list[17], (D,), 0.5, 3.0, ((0, 32),))
    return {"tokens": tokens, "lengths": lengths, "cotangent": cotangent, "w_query": w_query, "w_key": w_key, "w_value": w_value, "w_out": w_out, "b_query": b_query, "b_value": b_value, "b_out": b_out, "norm1_gain": norm1_gain, "norm1_shift": norm1_shift, "w_in": w_in, "w_back": w_back, "b_in": b_in, "b_back": b_back, "norm2_gain": norm2_gain, "norm2_shift": norm2_shift}


@jax.custom_vjp
def low(v):
    return lax.optimization_barrier(v.astype(jnp.bfloat16)).astype(jnp.float32)

@jax.custom_vjp
def low_back(v):
    return v

def low_keep(v):
    return (low(v), None)

def low_pass(kept, grad):
    return (grad,)

def back_keep(v):
    return (v, None)

def back_low(kept, grad):
    return (low(grad),)
low.defvjp(low_keep, low_pass)
low_back.defvjp(back_keep, back_low)

def layer_norm(value, gain_vec, shift_vec):
    centre = value - lax.optimization_barrier(jnp.mean(value, axis=-1, keepdims=True))
    variance = lax.optimization_barrier(jnp.mean(centre * centre, axis=-1, keepdims=True))
    return centre * lax.rsqrt(variance + 1e-06) * gain_vec + shift_vec

def segment_ids(length_row, seq_len):
    boundary = jnp.cumsum(length_row.astype(jnp.int32)).astype(jnp.int32)
    position = jnp.arange(seq_len, dtype=jnp.int32)
    return lax.optimization_barrier(jnp.sum((position[:, None] >= boundary[None, :]).astype(jnp.int32), axis=1)).astype(jnp.int32)

def row_layer(row_tokens, row_segments, params):
    w_query, w_key, w_value, w_out, b_query, b_value, b_out, gain_one, shift_one, w_in, w_back, b_in, b_back, gain_two, shift_two = params
    highest = lax.Precision.HIGHEST
    seq_len = row_tokens.shape[0]
    query = low_back(low(jnp.dot(row_tokens, w_query, precision=highest) + b_query))
    keys = low_back(low(jnp.dot(row_tokens, w_key, precision=highest)))
    values = low_back(low(jnp.dot(row_tokens, w_value, precision=highest) + b_value))
    shaped_query = query.reshape(seq_len, HEADS, HEAD_DIM)
    shaped_keys = keys.reshape(seq_len, HEADS, HEAD_DIM)
    shaped_values = values.reshape(seq_len, HEADS, HEAD_DIM)
    raw_scores = jnp.einsum('qhd,khd->hqk', shaped_query, shaped_keys, precision=highest)
    same_doc = row_segments[:, None] == row_segments[None, :]
    scores = low_back(jnp.where(same_doc[None], raw_scores * HEAD_DIM ** (-0.5), -1e+30))
    attn_prob = low(jax.nn.softmax(scores, axis=-1))
    attended = jnp.einsum('hqk,khd->qhd', attn_prob, shaped_values, precision=highest)
    attended = low_back(low(attended.reshape(seq_len, HEADS * HEAD_DIM)))
    branch = low_back(jnp.dot(attended, w_out, precision=highest) + b_out)
    normed_one = layer_norm(row_tokens + branch, gain_one, shift_one)
    hidden_pre = low_back(jnp.dot(low(normed_one), w_in, precision=highest) + b_in)
    hidden = low(jax.nn.gelu(hidden_pre, approximate=False))
    branch_two = low_back(jnp.dot(hidden, w_back, precision=highest) + b_back)
    return layer_norm(normed_one + branch_two, gain_two, shift_two)

def reference(tokens, lengths, cotangent, w_query, w_key, w_value, w_out, b_query, b_value, b_out, norm1_gain, norm1_shift, w_in, w_back, b_in, b_back, norm2_gain, norm2_shift):
    params = tuple((param_item.astype(jnp.float32) for param_item in (w_query, w_key, w_value, w_out, b_query, b_value, b_out, norm1_gain, norm1_shift, w_in, w_back, b_in, b_back, norm2_gain, norm2_shift)))
    segments = jax.vmap(lambda length_row: segment_ids(length_row, SEQ))(lengths)

    def forward(inputs, layer_params):

        def row_step(scan_carry, row_pair):
            return (scan_carry, jax.checkpoint(row_layer)(row_pair[0], row_pair[1], layer_params))
        _, outputs = lax.scan(row_step, jnp.zeros((), jnp.float32), (inputs, segments))
        return outputs
    outputs, pullback = jax.vjp(forward, tokens.astype(jnp.float32), params)
    grad_tokens, grads = pullback(cotangent.astype(jnp.float32))
    return (outputs.astype(jnp.bfloat16), grad_tokens, grads[0], grads[1], grads[2], grads[3], grads[4], grads[5], grads[6], grads[7], grads[8], grads[9], grads[10], grads[11], grads[12], grads[13], grads[14])
```

```python
import functools

import jax
import jax.numpy as jnp
from jax import lax
from jax.experimental import pallas as pl
from jax.experimental.pallas import tpu as pltpu
from jax.sharding import PartitionSpec as P

HEAD_DIM = 64
MASKED = -1e30
AXES = ("dp", "fsdp")
f32 = jnp.float32
bf16 = jnp.bfloat16
NN = (((1,), (0,)), ((), ()))
NT = (((1,), (1,)), ((), ()))
TN = (((0,), (0,)), ((), ()))
PARAMS = pltpu.CompilerParams(vmem_limit_bytes=56 << 20)


def dot(left, right, dims=NN):
    return lax.dot_general(left, right, dims, preferred_element_type=f32)


def shape_of(shape, dtype=f32):
    return jax.ShapeDtypeStruct(shape, dtype)


def whole(array):
    return pl.BlockSpec(array.shape, lambda i: (0,) * array.ndim)


def attend_kernel(
    x_ref, wq_ref, wk_ref, wv_ref, bq_ref, bv_ref, seg_row_ref, seg_col_ref,
    q_ref, k_ref, v_ref, o_ref, lse_ref, bias_ref,
):
    half = x_ref.shape[0] // 2
    width = wq_ref.shape[1]

    @pl.when(pl.program_id(0) == 0)
    def _():
        bias_ref[...] = jnp.where(seg_col_ref[...] == seg_row_ref[...], 0.0, MASKED)

    x = x_ref[...]
    query = (dot(x, wq_ref[...]) + bq_ref[...]).astype(bf16)
    q_ref[...] = query * jnp.asarray(HEAD_DIM**-0.5, bf16)
    k_ref[...] = dot(x, wk_ref[...]).astype(bf16)
    v_ref[...] = (dot(x, wv_ref[...]) + bv_ref[...]).astype(bf16)
    for part in range(2):
        rows = slice(part * half, (part + 1) * half)
        for pair in range(width // 128):
            cols = slice(pair * 128, (pair + 1) * 128)
            keys = k_ref[rows, cols]
            values_t = v_ref[rows, cols].T
            queries = q_ref[rows, cols]
            lane = lax.broadcasted_iota(jnp.int32, queries.shape, 1)
            outs = []
            for h in range(2):
                mine = (lane < HEAD_DIM) if h == 0 else (lane >= HEAD_DIM)
                scores = dot(keys, jnp.where(mine, queries, jnp.zeros_like(queries)), NT)
                if part == 1:
                    scores = scores + bias_ref[...]
                top = jnp.max(scores, axis=0, keepdims=True)
                terms = jnp.exp(scores - top)
                total = jnp.sum(terms, axis=0, keepdims=True)
                mixed = dot(values_t[h * HEAD_DIM : (h + 1) * HEAD_DIM, :], terms.astype(bf16))
                outs.append(mixed / total)
                lse_ref[0, pair * 2 + h : pair * 2 + h + 1, rows] = top + jnp.log(total)
            o_ref[rows, cols] = jnp.concatenate(outs, 0).T.astype(bf16)


def attend(x, wq, wk, wv, bq, bv, seg_row, seg_col, width=256):
    n, d = x.shape
    groups = d // width
    weight = pl.BlockSpec((d, width), lambda i: (0, i))
    bias = pl.BlockSpec((1, width), lambda i: (0, i))
    act = pl.BlockSpec((n, width), lambda i: (0, i))
    heads = width // HEAD_DIM
    return pl.pallas_call(
        attend_kernel,
        grid=(groups,),
        in_specs=[whole(x), weight, weight, weight, bias, bias, whole(seg_row), whole(seg_col)],
        out_specs=[act, act, act, act, pl.BlockSpec((1, heads, n), lambda i: (i, 0, 0))],
        out_shape=[shape_of((n, d), bf16)] * 4 + [shape_of((groups, heads, n))],
        scratch_shapes=[pltpu.VMEM((n // 2, n // 2), f32)],
        compiler_params=PARAMS,
        name="attend",
    )(x, wq, wk, wv, bq, bv, seg_row, seg_col)


def attend_back_kernel(
    q_ref, k_ref, v_ref, do_ref, lse_ref, seg_row_ref, seg_col_ref, grads_ref, bias_ref
):
    n, width = q_ref.shape
    half = n // 2

    @pl.when(pl.program_id(0) == 0)
    def _():
        bias_ref[...] = jnp.where(seg_col_ref[...] == seg_row_ref[...], 0.0, MASKED)

    for part in range(2):
        rows = slice(part * half, (part + 1) * half)
        for pair in range(width // 128):
            cols = slice(pair * 128, (pair + 1) * 128)
            keys, values = k_ref[rows, cols], v_ref[rows, cols]
            queries, grads = q_ref[rows, cols], do_ref[rows, cols]
            keys_t = keys.T
            lane = lax.broadcasted_iota(jnp.int32, queries.shape, 1)
            dqs = []
            dk = dv = None
            for h in range(2):
                mine = (lane < HEAD_DIM) if h == 0 else (lane >= HEAD_DIM)
                query = jnp.where(mine, queries, jnp.zeros_like(queries))
                grad = jnp.where(mine, grads, jnp.zeros_like(grads))
                scores = dot(keys, query, NT)
                if part == 1:
                    scores = scores + bias_ref[...]
                prob = jnp.exp(scores - lse_ref[0, pair * 2 + h : pair * 2 + h + 1, rows])
                prob_grad = dot(values, grad, NT)
                delta = jnp.sum(prob * prob_grad, axis=0, keepdims=True)
                score_grad = (prob * (prob_grad - delta)).astype(bf16)
                dv_h = dot(prob.astype(bf16), grad)
                dk_h = dot(score_grad, query)
                dv = dv_h if h == 0 else dv + dv_h
                dk = dk_h if h == 0 else dk + dk_h
                dqs.append(dot(keys_t[h * HEAD_DIM : (h + 1) * HEAD_DIM, :], score_grad))
            dq = jnp.concatenate(dqs, 0).T * HEAD_DIM**-0.5
            grads_ref[0, rows, cols] = dq.astype(bf16)
            grads_ref[1, rows, cols] = dk.astype(bf16)
            grads_ref[2, rows, cols] = dv.astype(bf16)


def attend_back(q, k, v, do, lse, seg_row, seg_col, width=256):
    n, d = q.shape
    act = pl.BlockSpec((n, width), lambda i: (0, i))
    heads = width // HEAD_DIM
    return pl.pallas_call(
        attend_back_kernel,
        grid=(d // width,),
        in_specs=[
            act, act, act, act, pl.BlockSpec((1, heads, n), lambda i: (i, 0, 0)),
            whole(seg_row), whole(seg_col),
        ],
        out_specs=pl.BlockSpec((3, n, width), lambda i: (0, 0, i)),
        out_shape=shape_of((3, n, d), bf16),
        scratch_shapes=[pltpu.VMEM((n // 2, n // 2), f32)],
        compiler_params=PARAMS,
        name="attend_back",
    )(q, k, v, do, lse, seg_row, seg_col)


def gelu_and_slope(u):
    size = jnp.abs(u)
    t = 1.0 / (1.0 + (0.3275911 * 0.7071067811865476) * size)
    bell = jnp.exp(-0.5 * u * u)
    series = t * (
        0.127414796
        + t * (-0.142248368 + t * (0.7107068705 + t * (-0.7265760135 + t * 0.5307027145)))
    )
    tail = series * bell
    cdf = jnp.where(u >= 0, 1.0 - tail, tail)
    return u * cdf, cdf + u * (bell * 0.3989422804014327)


def normed(value):
    centre = value - jnp.mean(value, axis=-1, keepdims=True)
    inv = lax.rsqrt(jnp.mean(centre * centre, axis=-1, keepdims=True) + 1e-6)
    return centre * inv, inv


def normed_back(e, z, inv):
    mean_e = jnp.mean(e, axis=-1, keepdims=True)
    mean_ez = jnp.mean(e * z, axis=-1, keepdims=True)
    return (e - mean_e - z * mean_ez) * inv


def forward_kernel(
    x_ref, o_ref, dy_ref, wo_ref, wi_ref, wb_ref, vec_ref, bi_ref,
    mixed_ref, h_ref, z_ref, inv_ref, g_ref, slope_ref, dr_ref, df_ref, sums_ref,
):
    b_out, gain1, shift1, b_back, gain2, shift2 = [vec_ref[i : i + 1, :] for i in range(2, 8)]
    r1 = x_ref[...].astype(f32) + dot(o_ref[...], wo_ref[...]) + b_out
    z1, inv1 = normed(r1)
    z_ref[...] = z1
    inv_ref[...] = inv1
    h1 = z1 * gain1 + shift1
    low = h1.astype(bf16)
    h_ref[...] = low
    r2 = h1 + b_back
    for j in range(wi_ref.shape[0]):
        cols = slice(j * wi_ref.shape[2], (j + 1) * wi_ref.shape[2])
        g, slope = gelu_and_slope(dot(low, wi_ref[j]) + bi_ref[j : j + 1, :])
        g_low = g.astype(bf16)
        g_ref[:, cols] = g_low
        slope_ref[:, cols] = slope.astype(bf16)
        r2 = r2 + dot(g_low, wb_ref[cols, :])
    z2, inv2 = normed(r2)
    mixed_ref[...] = (z2 * gain2 + shift2).astype(bf16)
    dy = dy_ref[...].astype(f32)
    dr = normed_back(dy * gain2, z2, inv2)
    dr_ref[...] = dr
    df = dr.astype(bf16)
    df_ref[...] = df

    @pl.when(pl.program_id(0) == 0)
    def _():
        sums_ref[...] = jnp.zeros_like(sums_ref)

    for i, term in enumerate((df.astype(f32), dy * z2, dy)):
        sums_ref[i : i + 1, :] += jnp.sum(term, axis=0, keepdims=True)


def forward(x, o, dy, wo, wi, wb, vec, bi, rows=256):
    n, d = x.shape
    ff = wb.shape[0]
    tok = lambda w: pl.BlockSpec((rows, w), lambda i: (i, 0))
    return pl.pallas_call(
        forward_kernel,
        grid=(n // rows,),
        in_specs=[tok(d), tok(d), tok(d)] + [whole(a) for a in (wo, wi, wb, vec, bi)],
        out_specs=[
            tok(d), tok(d), tok(d), tok(1), tok(ff), tok(ff), tok(d), tok(d),
            pl.BlockSpec((8, d), lambda i: (0, 0)),
        ],
        out_shape=[
            shape_of((n, d), bf16), shape_of((n, d), bf16), shape_of((n, d)), shape_of((n, 1)),
            shape_of((n, ff), bf16), shape_of((n, ff), bf16), shape_of((n, d)),
            shape_of((n, d), bf16), shape_of((8, d)),
        ],
        compiler_params=PARAMS,
        name="forward",
    )(x, o, dy, wo, wi, wb, vec, bi)


def backward_kernel(
    df_ref, slope_ref, dr_ref, z_ref, inv_ref, wo_ref, wi_ref, wb_ref, vec_ref,
    du_ref, dr1_ref, da_ref, do_ref, sums_ref, bsum_ref,
):
    @pl.when(pl.program_id(0) == 0)
    def _():
        sums_ref[...] = jnp.zeros_like(sums_ref)
        bsum_ref[...] = jnp.zeros_like(bsum_ref)

    df = df_ref[...]
    dh = dr_ref[...]
    for j in range(wi_ref.shape[0]):
        cols = slice(j * wi_ref.shape[2], (j + 1) * wi_ref.shape[2])
        du = (dot(df, wb_ref[cols, :], NT) * slope_ref[:, cols].astype(f32)).astype(bf16)
        du_ref[:, cols] = du
        bsum_ref[j : j + 1, :] += jnp.sum(du.astype(f32), axis=0, keepdims=True)
        dh = dh + dot(du, wi_ref[j], NT)
    z1 = z_ref[...]
    dr1 = normed_back(dh * vec_ref[3:4, :], z1, inv_ref[...])
    dr1_ref[...] = dr1
    da = dr1.astype(bf16)
    da_ref[...] = da
    do_ref[...] = dot(da, wo_ref[...], NT).astype(bf16)
    for i, term in enumerate((da.astype(f32), dh * z1, dh)):
        sums_ref[i : i + 1, :] += jnp.sum(term, axis=0, keepdims=True)


def backward(df, slope, dr, z, inv, wo, wi, wb, vec, rows=256):
    n, d = df.shape
    ff = wb.shape[0]
    tok = lambda w: pl.BlockSpec((rows, w), lambda i: (i, 0))
    return pl.pallas_call(
        backward_kernel,
        grid=(n // rows,),
        in_specs=[tok(d), tok(ff), tok(d), tok(d), tok(1)] + [whole(a) for a in (wo, wi, wb, vec)],
        out_specs=[
            tok(ff), tok(d), tok(d), tok(d),
            pl.BlockSpec((8, d), lambda i: (0, 0)),
            pl.BlockSpec((wi.shape[0], wi.shape[2]), lambda i: (0, 0)),
        ],
        out_shape=[
            shape_of((n, ff), bf16), shape_of((n, d)), shape_of((n, d), bf16),
            shape_of((n, d), bf16), shape_of((8, d)), shape_of((wi.shape[0], wi.shape[2])),
        ],
        compiler_params=PARAMS,
        name="backward",
    )(df, slope, dr, z, inv, wo, wi, wb, vec)


def outer_kernel(left_ref, right_ref, out_ref):
    out_ref[...] = dot(left_ref[...], right_ref[...], TN).astype(bf16)


def outer_rows(left, right, block=768):
    n, m = left.shape
    p = right.shape[1]
    return pl.pallas_call(
        outer_kernel,
        grid=(m // block,),
        in_specs=[pl.BlockSpec((n, block), lambda i: (0, i)), whole(right)],
        out_specs=pl.BlockSpec((block, p), lambda i: (i, 0)),
        out_shape=shape_of((m, p), bf16),
        compiler_params=PARAMS,
        name="outer_rows",
    )(left, right)


def outer_cols(left, right, block=768):
    n, m = left.shape
    p = right.shape[1]
    return pl.pallas_call(
        outer_kernel,
        grid=(p // block,),
        in_specs=[whole(left), pl.BlockSpec((n, block), lambda i: (0, i))],
        out_specs=pl.BlockSpec((m, block), lambda i: (0, i)),
        out_shape=shape_of((m, p), bf16),
        compiler_params=PARAMS,
        name="outer_cols",
    )(left, right)


def qkv_outer_kernel(x_ref, grads_ref, out_ref, sums_ref):
    grads = grads_ref[0]
    out_ref[...] = dot(x_ref[...], grads, TN).astype(bf16)
    sums_ref[0] = jnp.sum(grads.astype(f32), axis=0, keepdims=True)


def qkv_outer(x, grads):
    n, d = x.shape
    return pl.pallas_call(
        qkv_outer_kernel,
        grid=(3,),
        in_specs=[whole(x), pl.BlockSpec((1, n, d), lambda i: (i, 0, 0))],
        out_specs=[pl.BlockSpec((d, d), lambda i: (0, i)), pl.BlockSpec((1, 1, d), lambda i: (i, 0, 0))],
        out_shape=[shape_of((d, 3 * d), bf16), shape_of((3, 1, d))],
        compiler_params=PARAMS,
        name="qkv_outer",
    )(x, grads)


def input_grad_kernel(dr_ref, grads_ref, wq_ref, wk_ref, wv_ref, out_ref):
    total = dr_ref[...]
    for i, w_ref in enumerate((wq_ref, wk_ref, wv_ref)):
        total = total + dot(grads_ref[i], w_ref[...], NT)
    out_ref[...] = total


def input_grad(dr, grads, wq, wk, wv, rows=256):
    n, d = dr.shape
    tok = pl.BlockSpec((rows, d), lambda i: (i, 0))
    return pl.pallas_call(
        input_grad_kernel,
        grid=(n // rows,),
        in_specs=[tok, pl.BlockSpec((3, rows, d), lambda i: (0, i, 0))]
        + [whole(a) for a in (wq, wk, wv)],
        out_specs=tok,
        out_shape=shape_of((n, d)),
        compiler_params=PARAMS,
        name="input_grad",
    )(dr, grads, wq, wk, wv)


def bit_of(axis, bit):
    return (lax.axis_index(axis) // bit) % 2


def swap(x, axis, bits):
    size = lax.axis_size(axis)
    return lax.ppermute(x, axis, [(i, i ^ bits) for i in range(size)])


def ordered(mine, own, other):
    return jnp.where(mine == 0, own, other), jnp.where(mine == 0, other, own)


def gather_bit(x, axis, bit):
    first, second = ordered(bit_of(axis, bit), x, swap(x, axis, bit))
    return jnp.stack([first, second], 1).reshape((2 * x.shape[0],) + x.shape[1:])


def gather_two_bits(x, axis, high, low):
    a, b, c, d = x, swap(x, axis, low), swap(x, axis, high), swap(x, axis, high | low)
    a, b = ordered(bit_of(axis, low), a, b)
    c, d = ordered(bit_of(axis, low), c, d)
    a, c = ordered(bit_of(axis, high), a, c)
    b, d = ordered(bit_of(axis, high), b, d)
    return jnp.stack([a, b, c, d], 1).reshape((4 * x.shape[0],) + x.shape[1:])


def upper_bits():
    count = lax.axis_size("dp").bit_length() - 1
    return [1 << i for i in range(count - 1, 0, -1)]


def gather(x):
    rows, cols = x.shape
    x = x[None]
    bits = upper_bits()
    if len(bits) == 2:
        x = gather_two_bits(x, "dp", *bits)
    else:
        for bit in bits:
            x = gather_bit(x, "dp", bit)
    k = x.shape[0]
    one = gather_bit(gather_bit(x[:, :, : cols // 2], "dp", 1), "fsdp", 2)
    two = gather_bit(gather_bit(x[:, :, cols // 2 :], "fsdp", 2), "dp", 1)
    two = jnp.swapaxes(two.reshape(k, 2, 2, rows, cols // 2), 1, 2).reshape(one.shape)
    x = jnp.concatenate([one, two], -1)
    return gather_bit(x, "fsdp", 1)


def scatter_bit(x, axis, bit, dim):
    mine = bit_of(axis, bit)
    keep = lax.dynamic_index_in_dim(x, mine, dim, keepdims=False)
    send = lax.dynamic_index_in_dim(x, 1 - mine, dim, keepdims=False)
    return (keep.astype(f32) + swap(send, axis, bit).astype(f32)).astype(x.dtype)


def scatter_two_bits(x, axis, high, low):
    mine = bit_of(axis, high) * 2 + bit_of(axis, low)
    part = lambda i: lax.dynamic_index_in_dim(x, mine ^ i, 0, keepdims=False)
    total = part(0).astype(f32)
    for i, bits in ((1, low), (2, high), (3, high | low)):
        total = total + swap(part(i), axis, bits).astype(f32)
    return total


def scatter_sum(x):
    devices, rows, cols = x.shape
    bits = upper_bits()
    x = scatter_bit(x.reshape(devices // 8, 2, 2, 2, rows, cols), "fsdp", 1, 3)
    one = scatter_bit(scatter_bit(x[..., : cols // 2], "fsdp", 2, 2), "dp", 1, 1)
    two = scatter_bit(scatter_bit(x[..., cols // 2 :], "dp", 1, 1), "fsdp", 2, 1)
    x = jnp.concatenate([one, two], -1)
    if len(bits) == 2:
        return scatter_two_bits(x, "dp", *bits)
    x = x.reshape((2,) * len(bits) + (rows, cols))
    for bit in bits:
        x = scatter_bit(x, "dp", bit, 0)
    return x.astype(f32)


def places(lengths, n):
    ends = jnp.cumsum(lengths)
    start = jnp.sum(jnp.where(lengths == n // 2, ends - n // 2, 0))
    position = (start + n // 2 + jnp.arange(n // 2, dtype=jnp.int32)) % n
    segment = jnp.sum((position[:, None] >= ends[None, :]).astype(jnp.int32), axis=1)
    return start, segment.astype(f32)


def body(
    tokens, lengths, cotangent, w_query, w_key, w_value, w_out, b_query, b_value, b_out,
    norm1_gain, norm1_shift, w_in, w_back, b_in, b_back, norm2_gain, norm2_shift,
):
    _, n, d = tokens.shape
    devices = lax.axis_size("dp") * lax.axis_size("fsdp")
    r = w_query.shape[0]
    small = jnp.concatenate(
        [b_query, b_value, b_out, norm1_gain, norm1_shift, b_back, norm2_gain, norm2_shift, b_in]
    )
    small = jnp.pad(small, (0, 8 * d - small.shape[0])).reshape(8, d)
    first = gather(jnp.concatenate([w_query, w_key, w_value, small]))
    second = gather(
        jnp.concatenate([w_out] + [w_in[:, j * d : (j + 1) * d] for j in range(4)] + [w_back])
    )
    wq, wk, wv = [first[:, i * r : (i + 1) * r].reshape(d, d) for i in range(3)]
    small = first[:, 3 * r].astype(f32)
    vec = jnp.transpose(small[:, : 8 * r].reshape(devices, 8, r), (1, 0, 2)).reshape(8, d)
    bi = small[:, 8 * r : 12 * r].reshape(4, d)
    wo = second[:, :r].reshape(d, d)
    wi = jnp.swapaxes(second[:, r : 5 * r].reshape(devices, 4, r, d), 0, 1).reshape(4, d, d)
    wb = second[:, 5 * r :].reshape(4 * d, d)

    start, segment = places(lengths[0], n)
    seg_row, seg_col = segment[None, :], segment[:, None]
    x = jnp.roll(tokens[0], -start, axis=0)
    dy = jnp.roll(cotangent[0], -start, axis=0)

    q, k, v, o, lse = attend(x, wq, wk, wv, vec[0:1], vec[1:2], seg_row, seg_col)
    mixed, h, z, inv, g, slope, dr, df, sums2 = forward(x, o, dy, wo, wi, wb, vec, bi)
    back_grad = scatter_sum(outer_rows(g, df).reshape(devices, 4 * r, d))
    du, dr1, da, do, sums1, bi_sum = backward(df, slope, dr, z, inv, wo, wi, wb, vec)
    in_grad = scatter_sum(outer_cols(h, du).reshape(devices, r, 4 * d))
    out_outer = outer_rows(o, da)
    grads = attend_back(q, k, v, do, lse, seg_row, seg_col)
    qkv_outers, qkv_sums = qkv_outer(x, grads)
    shards = lambda a: a.reshape(-1, devices, r)
    sums = jnp.concatenate([shards(a) for a in (qkv_sums[0], qkv_sums[2], sums1[0:3], sums2[0:3])])
    sums = jnp.concatenate([jnp.transpose(sums, (1, 2, 0)), bi_sum.reshape(devices, r, 4)], -1)
    sums = jnp.pad(sums, ((0, 0), (0, 0), (0, 128 - 12))).astype(bf16)
    rest = scatter_sum(
        jnp.concatenate(
            [qkv_outers.reshape(devices, r, 3 * d), out_outer.reshape(devices, r, d), sums], -1
        )
    )
    grad_tokens = input_grad(dr1, grads, wq, wk, wv)
    gq, gk, gv, go = [rest[:, i * d : (i + 1) * d] for i in range(4)]
    vecs = rest[:, 4 * d : 4 * d + 8].T
    gbi = rest[:, 4 * d + 8 : 4 * d + 12].reshape(4 * r)
    back = lambda a: jnp.roll(a, start, axis=0)[None]
    return (
        back(mixed), back(grad_tokens), gq, gk, gv, go,
        vecs[0], vecs[1], vecs[2], vecs[3], vecs[4],
        in_grad, back_grad, gbi, vecs[5], vecs[6], vecs[7],
    )


def solution(mesh):
    act, mat, vec = P(AXES, None, None), P(AXES, None), P(AXES)
    return jax.shard_map(
        body,
        mesh=mesh,
        in_specs=(act, mat, act, mat, mat, mat, mat, vec, vec, vec, vec, vec, mat, mat, vec, vec, vec, vec),
        out_specs=(act, act, mat, mat, mat, mat, vec, vec, vec, vec, vec, mat, mat, vec, vec, vec, vec),
        check_vma=False,
    )
```

```python
import functools

import jax
import jax.numpy as jnp
from jax import lax
from jax.experimental import pallas as pl
from jax.experimental.pallas import tpu as pltpu
from jax.sharding import PartitionSpec as P

HEAD_DIM = 64
MASKED = -1e30
AXES = ("dp", "fsdp")
CHUNKS = 16
f32 = jnp.float32
bf16 = jnp.bfloat16
NN = (((1,), (0,)), ((), ()))
NT = (((1,), (1,)), ((), ()))
TN = (((0,), (0,)), ((), ()))
PARAMS = pltpu.CompilerParams(vmem_limit_bytes=56 << 20)


def dot(left, right, dims=NN):
    return lax.dot_general(left, right, dims, preferred_element_type=f32)


def shape_of(shape, dtype=f32):
    return jax.ShapeDtypeStruct(shape, dtype)


def lasts(us):
    return pl.CostEstimate(flops=int(us * 1.1e9), bytes_accessed=0, transcendentals=0)


def whole(array):
    return pl.BlockSpec(array.shape, lambda i: (0,) * array.ndim)


def flat(weight):
    return weight.reshape(-1, weight.shape[-1])


def put_pieces(where_ref, pieces, pack_ref):
    width = pieces[0].shape[-1]
    for i, piece in enumerate(pieces):
        half = where_ref[0] if i < 4 else 1 - where_ref[0]
        cols = pl.ds(pl.multiple_of(half * width, 128), width)
        for j in range(4):
            pack_ref[where_ref[1 + 4 * i + j], :, :, cols] = piece[j]


def once(array):
    rank = array.ndim
    return pl.BlockSpec(array.shape, lambda i, s: (0,) * rank, pipeline_mode=pl.Buffered(1))


def spread(small_ref, vec_ref, bias_ref):
    d = vec_ref.shape[1]
    r = d // 32
    vec = jnp.zeros((16, d), f32)
    bias = [jnp.zeros((1, d), f32) for _ in range(4)]
    for i in range(32):
        half = slice(i % 2 * (d // 2), (i % 2 + 1) * (d // 2))
        mine = small_ref[i // 2, small_ref.shape[1] - 1, :, half].astype(f32)
        mine = jnp.concatenate([mine, jnp.zeros_like(mine)], 1)
        vec = vec + (pltpu.roll(mine, i * r, 1) if i else mine)
        shift = i % 8 * 4 * r
        row = mine[8:9]
        bias[i // 8] = bias[i // 8] + (pltpu.roll(row, shift, 1) if shift else row)
    vec_ref[...] = vec[:8]
    bias_ref[...] = jnp.concatenate(bias, 0)


def second_specs(d):
    at = lambda tiles, j: pl.BlockSpec((CHUNKS, tiles, 16, d), lambda i: (0, j, 0, 0))
    return [at(3, 8), at(12, 0), at(12, 1)]


def attend_kernel(
    where_ref, x_ref, seg_row_ref, seg_col_ref, *refs
):
    pieces = refs[:8]
    q_ref, k_ref, v_ref, o_ref, lse_ref, vec_ref, bi_ref, out_ref, pack_ref, bias_ref, sem = refs[8:]
    half = x_ref.shape[0] // 2
    width = q_ref.shape[1]
    step = pl.program_id(0)
    keep_pack = pltpu.make_async_copy(pack_ref, out_ref, sem)

    @pl.when(step == 0)
    def _():
        bias_ref[...] = jnp.where(seg_col_ref[...] == seg_row_ref[...], 0.0, MASKED)
        put_pieces(where_ref, pieces, pack_ref)
        keep_pack.start()
        spread(pack_ref, vec_ref, bi_ref)

    x = x_ref[...]
    group = pl.ds(pl.multiple_of(step * width, 128), width)
    weight = lambda j: flat(pack_ref[:, 3 * j : 3 * j + 3, :, group])
    query = (dot(x, weight(0)) + vec_ref[0:1, group]).astype(bf16)
    q_ref[...] = query * jnp.asarray(HEAD_DIM**-0.5, bf16)
    k_ref[...] = dot(x, weight(1)).astype(bf16)
    v_ref[...] = (dot(x, weight(2)) + vec_ref[1:2, group]).astype(bf16)
    for part in range(2):
        rows = slice(part * half, (part + 1) * half)
        for pair in range(width // 128):
            cols = slice(pair * 128, (pair + 1) * 128)
            keys = k_ref[rows, cols]
            values_t = v_ref[rows, cols].T
            queries = q_ref[rows, cols]
            lane = lax.broadcasted_iota(jnp.int32, queries.shape, 1)
            outs = []
            for h in range(2):
                mine = (lane < HEAD_DIM) if h == 0 else (lane >= HEAD_DIM)
                scores = dot(keys, jnp.where(mine, queries, jnp.zeros_like(queries)), NT)
                if part == 1:
                    scores = scores + bias_ref[...]
                top = jnp.max(scores, axis=0, keepdims=True)
                terms = jnp.exp(scores - top)
                total = jnp.sum(terms, axis=0, keepdims=True)
                mixed = dot(values_t[h * HEAD_DIM : (h + 1) * HEAD_DIM, :], terms.astype(bf16))
                outs.append(mixed / total)
                lse_ref[0, pair * 2 + h : pair * 2 + h + 1, rows] = top + jnp.log(total)
            o_ref[rows, cols] = jnp.concatenate(outs, 0).T.astype(bf16)

    @pl.when(step == pl.num_programs(0) - 1)
    def _():
        keep_pack.wait()


def attend(where, x, seg_row, seg_col, pieces, width=256):
    n, d = x.shape
    groups = d // width
    tiles = pieces[0].shape[1]
    act = pl.BlockSpec((n, width), lambda i, s: (0, i))
    heads = width // HEAD_DIM
    still = lambda rows: pl.BlockSpec((rows, d), lambda i, s: (0, 0))
    return pl.pallas_call(
        attend_kernel,
        grid_spec=pltpu.PrefetchScalarGridSpec(
            num_scalar_prefetch=1,
            grid=(groups,),
            in_specs=[once(a) for a in (x, seg_row, seg_col, *pieces)],
            out_specs=[
                act, act, act, act, pl.BlockSpec((1, heads, n), lambda i, s: (i, 0, 0)),
                still(8), still(4), pl.BlockSpec(memory_space=pl.ANY),
            ],
            scratch_shapes=[
                pltpu.VMEM((CHUNKS, tiles, 16, d), bf16),
                pltpu.VMEM((n // 2, n // 2), f32),
                pltpu.SemaphoreType.DMA,
            ],
        ),
        out_shape=[shape_of((n, d), bf16)] * 4
        + [shape_of((groups, heads, n)), shape_of((8, d)), shape_of((4, d))]
        + [shape_of((CHUNKS, tiles, 16, d), bf16)],
        compiler_params=PARAMS,
        name="attend",
        cost_estimate=lasts(20),
    )(where, x, seg_row, seg_col, *pieces)


def attend_back_kernel(
    q_ref, k_ref, v_ref, do_ref, lse_ref, seg_row_ref, seg_col_ref, grads_ref, bias_ref
):
    n, width = q_ref.shape
    half = n // 2

    @pl.when(pl.program_id(0) == 0)
    def _():
        bias_ref[...] = jnp.where(seg_col_ref[...] == seg_row_ref[...], 0.0, MASKED)

    for part in range(2):
        rows = slice(part * half, (part + 1) * half)
        for pair in range(width // 128):
            cols = slice(pair * 128, (pair + 1) * 128)
            keys, values = k_ref[rows, cols], v_ref[rows, cols]
            queries, grads = q_ref[rows, cols], do_ref[rows, cols]
            keys_t = keys.T
            lane = lax.broadcasted_iota(jnp.int32, queries.shape, 1)
            dqs = []
            dk = dv = None
            for h in range(2):
                mine = (lane < HEAD_DIM) if h == 0 else (lane >= HEAD_DIM)
                query = jnp.where(mine, queries, jnp.zeros_like(queries))
                grad = jnp.where(mine, grads, jnp.zeros_like(grads))
                scores = dot(keys, query, NT)
                if part == 1:
                    scores = scores + bias_ref[...]
                prob = jnp.exp(scores - lse_ref[0, pair * 2 + h : pair * 2 + h + 1, rows])
                prob_grad = dot(values, grad, NT)
                delta = jnp.sum(prob * prob_grad, axis=0, keepdims=True)
                score_grad = (prob * (prob_grad - delta)).astype(bf16)
                dv_h = dot(prob.astype(bf16), grad)
                dk_h = dot(score_grad, query)
                dv = dv_h if h == 0 else dv + dv_h
                dk = dk_h if h == 0 else dk + dk_h
                dqs.append(dot(keys_t[h * HEAD_DIM : (h + 1) * HEAD_DIM, :], score_grad))
            dq = jnp.concatenate(dqs, 0).T * HEAD_DIM**-0.5
            grads_ref[0, rows, cols] = dq.astype(bf16)
            grads_ref[1, rows, cols] = dk.astype(bf16)
            grads_ref[2, rows, cols] = dv.astype(bf16)


def attend_back(q, k, v, do, lse, seg_row, seg_col, group, width=256):
    n, d = q.shape
    act = pl.BlockSpec((n, width), lambda i: (0, group))
    heads = width // HEAD_DIM
    return pl.pallas_call(
        attend_back_kernel,
        grid=(1,),
        in_specs=[
            act, act, act, act, pl.BlockSpec((1, heads, n), lambda i: (group, 0, 0)),
            whole(seg_row), whole(seg_col),
        ],
        out_specs=pl.BlockSpec((3, n, width), lambda i: (0, 0, 0)),
        out_shape=shape_of((3, n, width), bf16),
        scratch_shapes=[pltpu.VMEM((n // 2, n // 2), f32)],
        compiler_params=PARAMS,
        name="attend_back",
        cost_estimate=lasts(9),
    )(q, k, v, do, lse, seg_row, seg_col)


def gelu_and_slope(u):
    size = jnp.abs(u)
    t = 1.0 / (1.0 + (0.3275911 * 0.7071067811865476) * size)
    bell = jnp.exp(-0.5 * u * u)
    series = t * (
        0.127414796
        + t * (-0.142248368 + t * (0.7107068705 + t * (-0.7265760135 + t * 0.5307027145)))
    )
    tail = series * bell
    cdf = jnp.where(u >= 0, 1.0 - tail, tail)
    return u * cdf, cdf + u * (bell * 0.3989422804014327)


def normed(value):
    centre = value - jnp.mean(value, axis=-1, keepdims=True)
    inv = lax.rsqrt(jnp.mean(centre * centre, axis=-1, keepdims=True) + 1e-6)
    return centre * inv, inv


def normed_back(e, z, inv):
    mean_e = jnp.mean(e, axis=-1, keepdims=True)
    mean_ez = jnp.mean(e * z, axis=-1, keepdims=True)
    return (e - mean_e - z * mean_ez) * inv


def forward_kernel(where_ref, x_ref, o_ref, dy_ref, vec_ref, bi_ref, *refs):
    pieces = refs[:8]
    mixed_ref, h_ref, z_ref, inv_ref, g_ref, slope_ref, dr_ref, df_ref, sums_ref = refs[8:17]
    out_ref, pack_ref, sem = refs[17:]
    step = pl.program_id(0)
    keep_pack = pltpu.make_async_copy(pack_ref, out_ref, sem)

    @pl.when(step == 0)
    def _():
        put_pieces(where_ref, pieces, pack_ref)
        keep_pack.start()
        sums_ref[...] = jnp.zeros_like(sums_ref)

    b_out, gain1, shift1, b_back, gain2, shift2 = [vec_ref[i : i + 1, :] for i in range(2, 8)]
    r1 = x_ref[...].astype(f32) + dot(o_ref[...], flat(pack_ref[:, 24:27])) + b_out
    z1, inv1 = normed(r1)
    z_ref[...] = z1
    inv_ref[...] = inv1
    h1 = z1 * gain1 + shift1
    low = h1.astype(bf16)
    h_ref[...] = low
    r2 = h1 + b_back
    d = low.shape[1]
    for j in range(4):
        cols = slice(j * d, (j + 1) * d)
        wi = flat(pack_ref[:, 3 * j : 3 * j + 3])
        g, slope = gelu_and_slope(dot(low, wi) + bi_ref[j : j + 1, :])
        g_low = g.astype(bf16)
        g_ref[:, cols] = g_low
        slope_ref[:, cols] = slope.astype(bf16)
        r2 = r2 + dot(g_low, flat(pack_ref[4 * j : 4 * j + 4, 12:24]))
    z2, inv2 = normed(r2)
    mixed_ref[...] = (z2 * gain2 + shift2).astype(bf16)
    dy = dy_ref[...].astype(f32)
    dr = normed_back(dy * gain2, z2, inv2)
    dr_ref[...] = dr
    df = dr.astype(bf16)
    df_ref[...] = df

    for i, term in enumerate((df.astype(f32), dy * z2, dy)):
        sums_ref[i : i + 1, :] += jnp.sum(term, axis=0, keepdims=True)

    @pl.when(step == pl.num_programs(0) - 1)
    def _():
        keep_pack.wait()


def forward(where, x, o, dy, vec, bi, pieces, rows=256):
    n, d = x.shape
    ff = 4 * d
    tiles = pieces[0].shape[1]
    tok = lambda w: pl.BlockSpec((rows, w), lambda i, s: (i, 0))
    return pl.pallas_call(
        forward_kernel,
        grid_spec=pltpu.PrefetchScalarGridSpec(
            num_scalar_prefetch=1,
            grid=(n // rows,),
            in_specs=[tok(d), tok(d), tok(d)] + [once(a) for a in (vec, bi, *pieces)],
            out_specs=[
                tok(d), tok(d), tok(d), tok(1), tok(ff), tok(ff), tok(d), tok(d),
                pl.BlockSpec((8, d), lambda i, s: (0, 0)), pl.BlockSpec(memory_space=pl.ANY),
            ],
            scratch_shapes=[
                pltpu.VMEM((CHUNKS, tiles, 16, d), bf16), pltpu.SemaphoreType.DMA,
            ],
        ),
        out_shape=[
            shape_of((n, d), bf16), shape_of((n, d), bf16), shape_of((n, d)), shape_of((n, 1)),
            shape_of((n, ff), bf16), shape_of((n, ff), bf16), shape_of((n, d)),
            shape_of((n, d), bf16), shape_of((8, d)), shape_of((CHUNKS, tiles, 16, d), bf16),
        ],
        compiler_params=PARAMS,
        name="forward",
        cost_estimate=lasts(30),
    )(where, x, o, dy, vec, bi, *pieces)


def backward_kernel(
    df_ref, slope_ref, dr_ref, z_ref, inv_ref, wo_ref, wi_ref, wb_ref, vec_ref,
    du_ref, dr1_ref, da_ref, do_ref, sums_ref, bsum_ref,
):
    @pl.when(pl.program_id(0) == 0)
    def _():
        sums_ref[...] = jnp.zeros_like(sums_ref)
        bsum_ref[...] = jnp.zeros_like(bsum_ref)

    df = df_ref[...]
    dh = dr_ref[...]
    d = df.shape[1]
    for j in range(4):
        cols = slice(j * d, (j + 1) * d)
        wi, wb = flat(wi_ref[:, 3 * j : 3 * j + 3]), flat(wb_ref[4 * j : 4 * j + 4])
        du = (dot(df, wb, NT) * slope_ref[:, cols].astype(f32)).astype(bf16)
        du_ref[:, cols] = du
        bsum_ref[j : j + 1, :] += jnp.sum(du.astype(f32), axis=0, keepdims=True)
        dh = dh + dot(du, wi, NT)
    z1 = z_ref[...]
    dr1 = normed_back(dh * vec_ref[3:4, :], z1, inv_ref[...])
    dr1_ref[...] = dr1
    da = dr1.astype(bf16)
    da_ref[...] = da
    do_ref[...] = dot(da, flat(wo_ref[...]), NT).astype(bf16)
    for i, term in enumerate((da.astype(f32), dh * z1, dh)):
        sums_ref[i : i + 1, :] += jnp.sum(term, axis=0, keepdims=True)


def backward(df, slope, dr, z, inv, pack, vec, rows=256):
    n, d = df.shape
    ff = 4 * d
    tok = lambda w: pl.BlockSpec((rows, w), lambda i: (i, 0))
    return pl.pallas_call(
        backward_kernel,
        grid=(n // rows,),
        in_specs=[tok(d), tok(ff), tok(d), tok(d), tok(1)] + second_specs(d) + [whole(vec)],
        out_specs=[
            tok(ff), tok(d), tok(d), tok(d),
            pl.BlockSpec((8, d), lambda i: (0, 0)), pl.BlockSpec((4, d), lambda i: (0, 0)),
        ],
        out_shape=[
            shape_of((n, ff), bf16), shape_of((n, d)), shape_of((n, d), bf16),
            shape_of((n, d), bf16), shape_of((8, d)), shape_of((4, d)),
        ],
        compiler_params=PARAMS,
        name="backward",
        cost_estimate=lasts(20),
    )(df, slope, dr, z, inv, pack, pack, pack, vec)


def put_slabs(where_ref, val_ref, keep_ref, send_ref, first, count, cols):
    r = keep_ref.shape[1]
    core = where_ref[0]
    for i in range(count):
        low = pl.multiple_of(2 * i * r + core * r, 8)
        high = pl.multiple_of(2 * i * r + (1 - core) * r, 8)
        keep_ref[where_ref[1 + first + i], :, cols] = val_ref[pl.ds(low, r), :].astype(bf16)
        send_ref[where_ref[1 + CHUNKS + first + i], :, cols] = val_ref[pl.ds(high, r), :].astype(bf16)


def slab_call(kernel, name, where, grid, in_specs, args, r, width, scratch, us):
    slabs = pl.BlockSpec((CHUNKS, r, width), lambda i, s: (0, 0, 0))
    return pl.pallas_call(
        kernel,
        grid_spec=pltpu.PrefetchScalarGridSpec(
            num_scalar_prefetch=1,
            grid=grid,
            in_specs=in_specs,
            out_specs=[slabs, slabs],
            scratch_shapes=scratch,
        ),
        out_shape=[shape_of((CHUNKS, r, width), bf16)] * 2,
        compiler_params=PARAMS,
        name=name,
        cost_estimate=lasts(us),
    )(where, *args)


def back_outer_kernel(where_ref, g_ref, df_ref, keep_ref, send_ref, val_ref):
    val_ref[...] = dot(g_ref[...], df_ref[...], TN)
    step = pl.program_id(0)
    put_slabs(where_ref, val_ref, keep_ref, send_ref, step * 4, 4, slice(None))


def back_outer(where, g, df):
    n, ff = g.shape
    d = df.shape[1]
    specs = [pl.BlockSpec((n, d), lambda i, s: (0, i)), pl.BlockSpec((n, d), lambda i, s: (0, 0))]
    return slab_call(
        back_outer_kernel, "back_outer", where, (4,), specs, (g, df), ff // 32, d,
        [pltpu.VMEM((d, d), f32)], 11,
    )


def mid_outer_kernel(
    where_ref, h_ref, du_ref, o_ref, da_ref, sums_ref,
    keep_ref, send_ref, val_ref,
):
    step = pl.program_id(0)
    d = h_ref.shape[1]

    @pl.when(step < 4)
    def _():
        val_ref[...] = dot(h_ref[...], du_ref[...], TN)

    @pl.when(step == 4)
    def _():
        val_ref[...] = dot(o_ref[...], da_ref[...], TN)
        put_slabs(where_ref, sums_ref, keep_ref, send_ref, 0, CHUNKS, slice(5 * d, 5 * d + 128))

    cols = pl.ds(pl.multiple_of(step * d, 128), d)
    put_slabs(where_ref, val_ref, keep_ref, send_ref, 0, CHUNKS, cols)


def mid_outer(where, h, du, o, da, sums):
    n, d = h.shape
    keep = lambda a: pl.BlockSpec(a.shape, lambda i, s: (0, 0))
    block = pl.BlockSpec((n, d), lambda i, s: (0, jnp.minimum(i, 3)))
    specs = [keep(h), block, keep(o), keep(da), keep(sums)]
    return slab_call(
        mid_outer_kernel, "mid_outer", where, (5,), specs, (h, du, o, da, sums), d // 32,
        5 * d + 128, [pltpu.VMEM((d, d), f32)], 14,
    )


def qkv_outer_kernel(where_ref, x_ref, *refs):
    grad_refs, (keep_ref, send_ref, val_ref, sums_ref) = refs[:-4], refs[-4:]
    d = x_ref.shape[1]
    step = pl.program_id(0)
    width = grad_refs[0].shape[2]

    @pl.when(step == 0)
    def _():
        sums_ref[...] = jnp.zeros_like(sums_ref)

    for i, ref in enumerate(grad_refs):
        grads = ref[0]
        cols = slice(i * width, (i + 1) * width)
        val_ref[:, cols] = dot(x_ref[...], grads, TN)
        total = jnp.sum(grads.astype(f32), axis=0, keepdims=True)
        sums_ref[pl.ds(step, 1), cols] = total
    put_slabs(
        where_ref, val_ref, keep_ref, send_ref, 0, CHUNKS, pl.ds(pl.multiple_of(step * d, 128), d)
    )

    @pl.when(step == 2)
    def _():
        val_ref[:, :128] = sums_ref[...].T
        put_slabs(
            where_ref, val_ref.at[:, :128], keep_ref, send_ref, 0, CHUNKS, slice(3 * d, 3 * d + 128)
        )


def qkv_outer(where, x, grads):
    n, d = x.shape
    block = pl.BlockSpec((1, n, grads[0].shape[2]), lambda i, s: (i, 0, 0))
    specs = [pl.BlockSpec((n, d), lambda i, s: (0, 0))] + [block] * len(grads)
    return slab_call(
        qkv_outer_kernel, "qkv_outer", where, (3,), specs, (x, *grads), d // 32, 3 * d + 128,
        [pltpu.VMEM((d, d), f32), pltpu.VMEM((128, d), f32)], 10,
    )


def input_grad_kernel(dr_ref, *refs):
    grad_refs, (wq_ref, wk_ref, wv_ref, out_ref) = refs[:-4], refs[-4:]
    width = grad_refs[0].shape[2]
    total = dr_ref[...]
    for i, w_ref in enumerate((wq_ref, wk_ref, wv_ref)):
        for j, ref in enumerate(grad_refs):
            w = flat(w_ref[:, :, :, j * width : (j + 1) * width])
            total = total + dot(ref[i], w, NT)
    out_ref[...] = total


def input_grad(dr, grads, pack, rows=256):
    n, d = dr.shape
    width = grads[0].shape[2]
    weight = lambda j: pl.BlockSpec((CHUNKS, 3, 16, d), lambda i: (0, j, 0, 0))
    return pl.pallas_call(
        input_grad_kernel,
        grid=(n // rows,),
        in_specs=[pl.BlockSpec((rows, d), lambda i: (i, 0))]
        + [pl.BlockSpec((3, rows, width), lambda i: (0, i, 0))] * len(grads)
        + [weight(0), weight(1), weight(2)],
        out_specs=pl.BlockSpec((rows, d), lambda i: (i, 0)),
        out_shape=shape_of((n, d)),
        compiler_params=PARAMS,
        name="input_grad",
        cost_estimate=lasts(9),
    )(dr, *grads, pack, pack, pack)


def bit_of(axis, bit):
    return (lax.axis_index(axis) // bit) % 2


def swap(x, axis, bits):
    size = lax.axis_size(axis)
    return lax.ppermute(x, axis, [(i, i ^ bits) for i in range(size)])


def ordered(mine, own, other):
    return jnp.where(mine == 0, own, other), jnp.where(mine == 0, other, own)


def gather_bit(x, axis, bit):
    first, second = ordered(bit_of(axis, bit), x, swap(x, axis, bit))
    return jnp.stack([first, second], 1).reshape((2 * x.shape[0],) + x.shape[1:])


def gather_two_bits(x, axis, high, low):
    a, b, c, d = x, swap(x, axis, low), swap(x, axis, high), swap(x, axis, high | low)
    a, b = ordered(bit_of(axis, low), a, b)
    c, d = ordered(bit_of(axis, low), c, d)
    a, c = ordered(bit_of(axis, high), a, c)
    b, d = ordered(bit_of(axis, high), b, d)
    return jnp.stack([a, b, c, d], 1).reshape((4 * x.shape[0],) + x.shape[1:])


def upper_bits():
    count = lax.axis_size("dp").bit_length() - 1
    return [1 << i for i in range(count - 1, 0, -1)]


def gather(x):
    rows, cols = x.shape
    x = x[None]
    bits = upper_bits()
    if len(bits) == 2:
        x = gather_two_bits(x, "dp", *bits)
    else:
        for bit in bits:
            x = gather_bit(x, "dp", bit)
    k = x.shape[0]
    one = gather_bit(gather_bit(x[:, :, : cols // 2], "dp", 1), "fsdp", 2)
    two = gather_bit(gather_bit(x[:, :, cols // 2 :], "fsdp", 2), "dp", 1)
    two = jnp.swapaxes(two.reshape(k, 2, 2, rows, cols // 2), 1, 2).reshape(one.shape)
    x = jnp.concatenate([one, two], -1)
    return gather_bit(x, "fsdp", 1)


def scatter_bit(x, axis, bit, dim):
    mine = bit_of(axis, bit)
    keep = lax.dynamic_index_in_dim(x, mine, dim, keepdims=False)
    send = lax.dynamic_index_in_dim(x, 1 - mine, dim, keepdims=False)
    return (keep.astype(f32) + swap(send, axis, bit).astype(f32)).astype(x.dtype)


def scatter_two_bits(x, axis, high, low):
    mine = bit_of(axis, high) * 2 + bit_of(axis, low)
    part = lambda i: lax.dynamic_index_in_dim(x, mine ^ i, 0, keepdims=False)
    total = part(0).astype(f32)
    for i, bits in ((1, low), (2, high), (3, high | low)):
        total = total + swap(part(i), axis, bits).astype(f32)
    return total


def scatter_sum(x):
    devices, rows, cols = x.shape
    bits = upper_bits()
    x = scatter_bit(x.reshape(devices // 8, 2, 2, 2, rows, cols), "fsdp", 1, 3)
    one = scatter_bit(scatter_bit(x[..., : cols // 2], "fsdp", 2, 2), "dp", 1, 1)
    two = scatter_bit(scatter_bit(x[..., cols // 2 :], "dp", 1, 1), "fsdp", 2, 1)
    x = jnp.concatenate([one, two], -1)
    if len(bits) == 2:
        return scatter_two_bits(x, "dp", *bits)
    x = x.reshape((2,) * len(bits) + (rows, cols))
    for bit in bits:
        x = scatter_bit(x, "dp", bit, 0)
    return x.astype(f32)


def seats():
    dp, fsdp = lax.axis_index("dp"), lax.axis_index("fsdp")
    return dp // 2, dp % 2, fsdp // 2, fsdp % 2


def swap_all(x, dz=0, first=0, second=0, core=0):
    pairs = []
    for i in range(32):
        z, y, xx, c = i // 8, i // 4 % 2, i // 2 % 2, i % 2
        dy, dx = (first, second) if c == 0 else (second, first)
        pairs.append((i, (((z ^ dz) * 2 + (y ^ dy)) * 2 + (xx ^ dx)) * 2 + (c ^ core)))
    return lax.ppermute(x, AXES, pairs)


def after(x, *others):
    return lax.optimization_barrier((x, *others))[0]


def halves_kernel(core_ref, wq_ref, wk_ref, wv_ref, wo_ref, wi_ref, wb_ref, own_ref, send_ref):
    r, d = wq_ref.shape
    for core, out in ((core_ref[0], own_ref), (1 - core_ref[0], send_ref)):
        half = lambda base: pl.ds(pl.multiple_of(base + core * (d // 2), 128), d // 2)
        for j in range(4):
            out[j] = wi_ref[:, half(j * d)]
        back = wb_ref[:, half(0)].astype(f32)
        for j in range(4):
            out[4 + j] = back[j * r : (j + 1) * r].astype(bf16)
        for j, ref in enumerate((wo_ref, wq_ref, wk_ref, wv_ref)):
            out[8 + j] = ref[:, half(0)]


def halves(core, *weights):
    r, d = weights[0].shape
    return pl.pallas_call(
        halves_kernel,
        in_specs=[pl.BlockSpec(memory_space=pltpu.SMEM)]
        + [pl.BlockSpec(memory_space=pltpu.VMEM)] * 6,
        out_specs=[pl.BlockSpec(memory_space=pltpu.VMEM)] * 2,
        out_shape=[shape_of((12, r, d // 2), bf16)] * 2,
        compiler_params=PARAMS,
        name="halves",
        cost_estimate=lasts(2),
    )(core, *weights)


def chip_kernel(core_ref, own_ref, got_ref, *refs, runs):
    extra, out_ref, rows_ref = refs[:-2], refs[-2], refs[-1]
    swapped = core_ref[0] == 1
    tile = 0
    for start, count in runs:
        own = own_ref[start : start + count].astype(f32)
        got = got_ref[start : start + count].astype(f32)
        low = jnp.where(swapped, got, own)
        high = jnp.where(swapped, own, got)
        rows = [a[i] for a in (low, high) for i in range(count)]
        rows = jnp.concatenate(rows, 0).astype(bf16)
        tiles = rows.shape[0] // 16
        out_ref[tile : tile + tiles] = rows.reshape(tiles, 16, rows.shape[1])
        tile += tiles
    if extra:
        rows_ref[...] = jnp.zeros_like(rows_ref)
        for i, ref in enumerate(extra):
            rows_ref[i : i + 1, : ref.shape[1]] = ref[...].astype(f32)
        out_ref[tile] = rows_ref[...].astype(bf16)


def chip_shard(core, own, got, runs, *extra):
    tiles = 2 * own.shape[0] * own.shape[1] // 16 + bool(extra)
    return pl.pallas_call(
        functools.partial(chip_kernel, runs=runs),
        in_specs=[pl.BlockSpec(memory_space=pltpu.SMEM)]
        + [pl.BlockSpec(memory_space=pltpu.VMEM)] * (2 + len(extra)),
        out_specs=pl.BlockSpec(memory_space=pltpu.VMEM),
        out_shape=shape_of((tiles, 16, own.shape[2]), bf16),
        scratch_shapes=[pltpu.VMEM((16, own.shape[2]), f32)],
        compiler_params=PARAMS,
        name="chip_shard",
        cost_estimate=lasts(2),
    )(core, own, got, *extra)


def along_z(shard):
    return [shard] + [swap_all(shard, dz=i) for i in (1, 2, 3)]


def near_pieces(stack):
    return [stack, swap_all(stack, first=1), swap_all(stack, second=1)]


def all_pieces(near):
    own = near + [swap_all(near[1], second=1)]
    return own + [swap_all(piece, core=1) for piece in own]


class Scatter:
    def __init__(self, small_slice, keep, send):
        self.state = (keep, send)
        self.small_slice = small_slice
        self.steps = 0
        self.total = None

    def hold(self, *late):
        self.state = tuple(after(part, *late) for part in self.state)

    def step(self, *late):
        if not self.small_slice:
            return ()
        self.steps += 1
        if self.steps <= 3:
            keep, send = self.state
            how = ({"core": 1}, {"second": 1}, {"first": 1})[self.steps - 1]
            got = after(swap_all(send, **how), *late)
            total = (keep.astype(f32) + got.astype(f32)).astype(bf16)
            half = total.shape[0] // 2
            self.state = (total[:half], total[half:]) if self.steps < 3 else (total,)
            return self.state
        (parts,) = self.state
        total = parts[0].astype(f32)
        for i in (1, 2, 3):
            total = total + after(swap_all(parts[i], dz=i), *late).astype(f32)
        self.total = total
        return (total,)

    def result(self, devices):
        if self.small_slice:
            while self.total is None:
                self.step()
            return self.total
        keep, send = self.state
        stacked = jnp.stack([keep, send], 1)
        return scatter_sum(stacked.reshape(devices, -1, keep.shape[-1]))


def places(lengths, n):
    ends = jnp.cumsum(lengths)
    start = jnp.sum(jnp.where(lengths == n // 2, ends - n // 2, 0))
    position = (start + n // 2 + jnp.arange(n // 2, dtype=jnp.int32)) % n
    segment = jnp.sum((position[:, None] >= ends[None, :]).astype(jnp.int32), axis=1)
    return start, segment.astype(f32)


def vectors(small, r, d):
    vec = jnp.transpose(small[:, : 8 * r].reshape(-1, 8, r), (1, 0, 2)).reshape(8, d)
    return vec, small[:, 8 * r : 12 * r].reshape(4, d)


def body(
    tokens, lengths, cotangent, w_query, w_key, w_value, w_out, b_query, b_value, b_out,
    norm1_gain, norm1_shift, w_in, w_back, b_in, b_back, norm2_gain, norm2_shift,
):
    _, n, d = tokens.shape
    devices = lax.axis_size("dp") * lax.axis_size("fsdp")
    r = w_query.shape[0]
    small_slice = lax.axis_size("dp") == 8 and lax.axis_size("fsdp") == 4
    start, segment = places(lengths[0], n)
    seg_row, seg_col = segment[None, :], segment[:, None]
    x = jnp.roll(tokens[0], -start, axis=0)
    dy = jnp.roll(cotangent[0], -start, axis=0)
    small = [b_query, b_value, b_out, norm1_gain, norm1_shift, b_back, norm2_gain, norm2_shift, b_in]
    if small_slice:
        z, y, across, core = seats()
        i = jnp.arange(32, dtype=jnp.int32)
        first, second = i // 4 % 2, i // 8 % 2
        other = (core + i // 16) % 2
        chip = ((z ^ i % 4) * 2 + (y ^ jnp.where(other == 0, first, second))) * 2
        chip = chip + (across ^ jnp.where(other == 0, second, first))
        gather_at = jnp.concatenate([core[None], chip])
        i = jnp.arange(16, dtype=jnp.int32)
        dz, dy_, dx = z ^ i // 4, y ^ i // 2 % 2, across ^ i % 2
        slot = lambda c: jnp.where(c == 0, dx, dy_) * 8 + jnp.where(c == 0, dy_, dx) * 4 + dz
        where = jnp.concatenate([core[None], slot(core), slot(1 - core)])
        own, send = halves(core[None], w_query, w_key, w_value, w_out, w_in, w_back)
        runs = [(0, 1), (1, 1), (2, 1), (3, 1), (4, 4), (8, 1), (9, 1), (10, 1), (11, 1)]
        shard = chip_shard(core[None], own, swap_all(send, core=1), runs, *[a[None] for a in small])
        shards = [after(a, x, dy, gather_at, where) for a in along_z(shard)]
        near1 = near_pieces(jnp.stack([a[27:] for a in shards]))
        near2 = near_pieces(jnp.stack([a[:27] for a in shards]))
        pieces1 = all_pieces(near1)
    else:
        step = jnp.arange(16, dtype=jnp.int32)
        gather_at = where = jnp.concatenate([jnp.zeros((1,), jnp.int32), step, step])
        small = jnp.concatenate(small)
        small = jnp.pad(small, (0, 8 * d - small.shape[0])).reshape(8, d)
        pack1 = gather(jnp.concatenate([w_query, w_key, w_value, small]))
        vec, bi = vectors(pack1[:, 3 * r], r, d)
        rows = jnp.pad(vec.reshape(8, 16, 2, -1), ((0, 0), (0, 0), (0, 0), (0, d // 2 - d // 32)))
        row = jnp.pad(bi.reshape(1, 16, 2, -1), ((0, 7), (0, 0), (0, 0), (0, d // 2 - d // 8)))
        small = jnp.transpose(jnp.concatenate([rows, row]), (1, 0, 2, 3)).reshape(16, 1, 16, d)
        tiles = lambda w: w.reshape(CHUNKS, -1, 16, d)
        pack1 = [tiles(pack1[:, i * r : (i + 1) * r]) for i in range(3)] + [small]
        pack2 = gather(jnp.concatenate([w_in[:, j * d : (j + 1) * d] for j in range(4)] + [w_back, w_out]))
        cuts = [i * r for i in (0, 1, 2, 3, 4, 8, 9)]
        pack2 = [tiles(pack2[:, a:b]) for a, b in zip(cuts, cuts[1:])]
        cut = lambda p: [
            jnp.concatenate(p, 1)[4 * i : 4 * i + 4, :, :, j * (d // 2) : (j + 1) * (d // 2)]
            for j in range(2)
            for i in range(4)
        ]
        pieces1, pieces2 = cut(pack1), cut(pack2)

    q, k, v, o, lse, vec, bi, pack1 = attend(gather_at, x, seg_row, seg_col, pieces1)
    if small_slice:
        pieces2 = all_pieces([after(a, o) for a in near2])
    mixed, h, zhat, inv, g, slope, dr, df, sums2, pack2 = forward(
        gather_at, x, o, dy, vec, bi, pieces2
    )
    scatter1 = Scatter(small_slice, *back_outer(where, g, df))
    du, dr1, da, do, sums1, bsum = backward(
        after(df, *scatter1.state), slope, dr, zhat, inv, pack2, vec
    )
    sums = jnp.concatenate([sums1[0:3], sums2[0:3]]).T
    sums = jnp.pad(jnp.concatenate([sums, bsum.reshape(d, 4)], 1), ((0, 0), (0, 118)))
    h_late = after(h, du, *scatter1.step(du))
    scatter2 = Scatter(small_slice, *mid_outer(where, h_late, du, o, da, sums))
    late = after(q, *scatter1.step(*scatter2.state))
    scatter2.hold(late)
    grads = [attend_back(late, k, v, do, lse, seg_row, seg_col, 0)]
    late = after(q, *scatter1.step(grads[0]), *scatter2.step(grads[0]))
    grads.append(attend_back(late, k, v, do, lse, seg_row, seg_col, 1))
    late = after(q, grads[1], *scatter1.step(grads[1]))
    grads.append(attend_back(late, k, v, do, lse, seg_row, seg_col, 2))
    late = after(x, *scatter2.step(grads[2]))
    scatter3 = Scatter(small_slice, *qkv_outer(where, late, grads))
    late = scatter2.step(*scatter3.state)
    grad_tokens = input_grad(after(dr1, *scatter3.state, *late), grads, pack1)
    unroll = lambda a: jnp.roll(a, start, axis=0)[None]
    late = scatter3.step(grad_tokens)
    late = scatter2.step(grad_tokens, *late)
    mixed, grad_tokens = unroll(after(mixed, grad_tokens)), unroll(grad_tokens)
    scatter3.step(mixed, grad_tokens, *late)
    mid_grad = scatter2.result(devices)
    back_grad = scatter1.result(devices)
    rest = scatter3.result(devices)
    gq, gk, gv = [rest[:, i * d : (i + 1) * d] for i in range(3)]
    gbq, _, gbv = rest[:, 3 * d : 3 * d + 3].T
    in_grad, out_grad = mid_grad[:, : 4 * d], mid_grad[:, 4 * d : 5 * d]
    vecs = mid_grad[:, 5 * d : 5 * d + 6].T
    gbi = mid_grad[:, 5 * d + 6 : 5 * d + 10].reshape(4 * r)
    return (
        mixed, grad_tokens, gq, gk, gv, out_grad,
        gbq, gbv, vecs[0], vecs[1], vecs[2],
        in_grad, back_grad, gbi, vecs[3], vecs[4], vecs[5],
    )


def solution(mesh):
    act, mat, vec = P(AXES, None, None), P(AXES, None), P(AXES)
    return jax.shard_map(
        body,
        mesh=mesh,
        in_specs=(act, mat, act, mat, mat, mat, mat, vec, vec, vec, vec, vec, mat, mat, vec, vec, vec, vec),
        out_specs=(act, act, mat, mat, mat, mat, vec, vec, vec, vec, vec, mat, mat, vec, vec, vec, vec),
        check_vma=False,
    )
```

```python
import functools

import jax
import jax.numpy as jnp
from jax import lax
from jax.experimental import pallas as pl
from jax.experimental.pallas import tpu as pltpu
from jax.sharding import PartitionSpec as P

HEAD_DIM = 64
MASKED = -1e30
AXES = ("dp", "fsdp")
CHUNKS = 16
f32 = jnp.float32
bf16 = jnp.bfloat16
NN = (((1,), (0,)), ((), ()))
NT = (((1,), (1,)), ((), ()))
TN = (((0,), (0,)), ((), ()))
PARAMS = pltpu.CompilerParams(vmem_limit_bytes=56 << 20)


def dot(left, right, dims=NN):
    return lax.dot_general(left, right, dims, preferred_element_type=f32)


def shape_of(shape, dtype=f32):
    return jax.ShapeDtypeStruct(shape, dtype)


def lasts(us):
    return pl.CostEstimate(flops=int(us * 1.1e9), bytes_accessed=0, transcendentals=0)


def whole(array):
    return pl.BlockSpec(array.shape, lambda i: (0,) * array.ndim)


def flat(weight):
    return weight.reshape(-1, weight.shape[-1])


def put_pieces(where_ref, pieces, pack_ref):
    width = pieces[0].shape[-1]
    at = 1
    for i, piece in enumerate(pieces):
        half = where_ref[0] if i < len(pieces) // 2 else 1 - where_ref[0]
        cols = pl.ds(pl.multiple_of(half * width, 128), width)
        for j in range(piece.shape[0]):
            pack_ref[where_ref[at], :, :, cols] = piece[j]
            at += 1


def once(array):
    rank = array.ndim
    return pl.BlockSpec(array.shape, lambda i, s: (0,) * rank, pipeline_mode=pl.Buffered(1))


def spread(small_ref, vec_ref, bias_ref):
    d = vec_ref.shape[1]
    r = d // 32
    vec = jnp.zeros((16, d), f32)
    bias = [jnp.zeros((1, d), f32) for _ in range(4)]
    for i in range(32):
        half = slice(i % 2 * (d // 2), (i % 2 + 1) * (d // 2))
        mine = small_ref[i // 2, small_ref.shape[1] - 1, :, half].astype(f32)
        mine = jnp.concatenate([mine, jnp.zeros_like(mine)], 1)
        vec = vec + (pltpu.roll(mine, i * r, 1) if i else mine)
        shift = i % 8 * 4 * r
        row = mine[8:9]
        bias[i // 8] = bias[i // 8] + (pltpu.roll(row, shift, 1) if shift else row)
    vec_ref[...] = vec[:8]
    bias_ref[...] = jnp.concatenate(bias, 0)


def second_specs(d):
    at = lambda tiles, j: pl.BlockSpec((CHUNKS, tiles, 16, d), lambda i: (0, j, 0, 0))
    return [at(3, 8), at(12, 1), at(12, 0)]


def attend_kernel(
    where_ref, x_ref, seg_row_ref, seg_col_ref, *refs
):
    pieces = refs[:-11]
    q_ref, k_ref, v_ref, o_ref, lse_ref, vec_ref, bi_ref, out_ref, pack_ref, bias_ref, sem = refs[-11:]
    half = x_ref.shape[0] // 2
    width = q_ref.shape[1]
    step = pl.program_id(0)
    keep_pack = pltpu.make_async_copy(pack_ref, out_ref, sem)

    @pl.when(step == 0)
    def _():
        bias_ref[...] = jnp.where(seg_col_ref[...] == seg_row_ref[...], 0.0, MASKED)
        put_pieces(where_ref, pieces, pack_ref)
        keep_pack.start()
        spread(pack_ref, vec_ref, bi_ref)

    x = x_ref[...]
    group = pl.ds(pl.multiple_of(step * width, 128), width)
    weight = lambda j: flat(pack_ref[:, 3 * j : 3 * j + 3, :, group])
    query = (dot(x, weight(0)) + vec_ref[0:1, group]).astype(bf16)
    q_ref[...] = query * jnp.asarray(HEAD_DIM**-0.5, bf16)
    k_ref[...] = dot(x, weight(1)).astype(bf16)
    v_ref[...] = (dot(x, weight(2)) + vec_ref[1:2, group]).astype(bf16)
    for part in range(2):
        rows = slice(part * half, (part + 1) * half)
        for pair in range(width // 128):
            cols = slice(pair * 128, (pair + 1) * 128)
            keys = k_ref[rows, cols]
            values_t = v_ref[rows, cols].T
            queries = q_ref[rows, cols]
            lane = lax.broadcasted_iota(jnp.int32, queries.shape, 1)
            outs = []
            for h in range(2):
                mine = (lane < HEAD_DIM) if h == 0 else (lane >= HEAD_DIM)
                scores = dot(keys, jnp.where(mine, queries, jnp.zeros_like(queries)), NT)
                if part == 1:
                    scores = scores + bias_ref[...]
                top = jnp.max(scores, axis=0, keepdims=True)
                terms = jnp.exp(scores - top)
                total = jnp.sum(terms, axis=0, keepdims=True)
                mixed = dot(values_t[h * HEAD_DIM : (h + 1) * HEAD_DIM, :], terms.astype(bf16))
                outs.append(mixed / total)
                lse_ref[0, pair * 2 + h : pair * 2 + h + 1, rows] = top + jnp.log(total)
            o_ref[rows, cols] = jnp.concatenate(outs, 0).T.astype(bf16)

    @pl.when(step == pl.num_programs(0) - 1)
    def _():
        keep_pack.wait()


def attend(where, x, seg_row, seg_col, pieces, width=256):
    n, d = x.shape
    groups = d // width
    tiles = pieces[0].shape[1]
    act = pl.BlockSpec((n, width), lambda i, s: (0, i))
    heads = width // HEAD_DIM
    still = lambda rows: pl.BlockSpec((rows, d), lambda i, s: (0, 0))
    return pl.pallas_call(
        attend_kernel,
        grid_spec=pltpu.PrefetchScalarGridSpec(
            num_scalar_prefetch=1,
            grid=(groups,),
            in_specs=[once(a) for a in (x, seg_row, seg_col, *pieces)],
            out_specs=[
                act, act, act, act, pl.BlockSpec((1, heads, n), lambda i, s: (i, 0, 0)),
                still(8), still(4), pl.BlockSpec(memory_space=pl.ANY),
            ],
            scratch_shapes=[
                pltpu.VMEM((CHUNKS, tiles, 16, d), bf16),
                pltpu.VMEM((n // 2, n // 2), f32),
                pltpu.SemaphoreType.DMA,
            ],
        ),
        out_shape=[shape_of((n, d), bf16)] * 4
        + [shape_of((groups, heads, n)), shape_of((8, d)), shape_of((4, d))]
        + [shape_of((CHUNKS, tiles, 16, d), bf16)],
        compiler_params=PARAMS,
        name="attend",
        cost_estimate=lasts(0),
    )(where, x, seg_row, seg_col, *pieces)


def attend_back_kernel(
    q_ref, k_ref, v_ref, do_ref, lse_ref, seg_row_ref, seg_col_ref, grads_ref, bias_ref
):
    n, width = q_ref.shape
    half = n // 2

    @pl.when(pl.program_id(0) == 0)
    def _():
        bias_ref[...] = jnp.where(seg_col_ref[...] == seg_row_ref[...], 0.0, MASKED)

    for part in range(2):
        rows = slice(part * half, (part + 1) * half)
        for pair in range(width // 128):
            cols = slice(pair * 128, (pair + 1) * 128)
            keys, values = k_ref[rows, cols], v_ref[rows, cols]
            queries, grads = q_ref[rows, cols], do_ref[rows, cols]
            keys_t = keys.T
            lane = lax.broadcasted_iota(jnp.int32, queries.shape, 1)
            dqs = []
            dk = dv = None
            for h in range(2):
                mine = (lane < HEAD_DIM) if h == 0 else (lane >= HEAD_DIM)
                query = jnp.where(mine, queries, jnp.zeros_like(queries))
                grad = jnp.where(mine, grads, jnp.zeros_like(grads))
                scores = dot(keys, query, NT)
                if part == 1:
                    scores = scores + bias_ref[...]
                prob = jnp.exp(scores - lse_ref[0, pair * 2 + h : pair * 2 + h + 1, rows])
                prob_grad = dot(values, grad, NT)
                delta = jnp.sum(prob * prob_grad, axis=0, keepdims=True)
                score_grad = (prob * (prob_grad - delta)).astype(bf16)
                dv_h = dot(prob.astype(bf16), grad)
                dk_h = dot(score_grad, query)
                dv = dv_h if h == 0 else dv + dv_h
                dk = dk_h if h == 0 else dk + dk_h
                dqs.append(dot(keys_t[h * HEAD_DIM : (h + 1) * HEAD_DIM, :], score_grad))
            dq = jnp.concatenate(dqs, 0).T * HEAD_DIM**-0.5
            grads_ref[0, rows, cols] = dq.astype(bf16)
            grads_ref[1, rows, cols] = dk.astype(bf16)
            grads_ref[2, rows, cols] = dv.astype(bf16)


def attend_back(q, k, v, do, lse, seg_row, seg_col, group, width=256):
    n, d = q.shape
    act = pl.BlockSpec((n, width), lambda i: (0, group))
    heads = width // HEAD_DIM
    return pl.pallas_call(
        attend_back_kernel,
        grid=(1,),
        in_specs=[
            act, act, act, act, pl.BlockSpec((1, heads, n), lambda i: (group, 0, 0)),
            whole(seg_row), whole(seg_col),
        ],
        out_specs=pl.BlockSpec((3, n, width), lambda i: (0, 0, 0)),
        out_shape=shape_of((3, n, width), bf16),
        scratch_shapes=[pltpu.VMEM((n // 2, n // 2), f32)],
        compiler_params=PARAMS,
        name="attend_back",
        cost_estimate=lasts(9),
    )(q, k, v, do, lse, seg_row, seg_col)


def gelu_and_slope(u):
    size = jnp.abs(u)
    t = 1.0 / (1.0 + (0.3275911 * 0.7071067811865476) * size)
    bell = jnp.exp(-0.5 * u * u)
    series = t * (
        0.127414796
        + t * (-0.142248368 + t * (0.7107068705 + t * (-0.7265760135 + t * 0.5307027145)))
    )
    tail = series * bell
    cdf = jnp.where(u >= 0, 1.0 - tail, tail)
    return u * cdf, cdf + u * (bell * 0.3989422804014327)


def normed(value):
    centre = value - jnp.mean(value, axis=-1, keepdims=True)
    inv = lax.rsqrt(jnp.mean(centre * centre, axis=-1, keepdims=True) + 1e-6)
    return centre * inv, inv


def normed_back(e, z, inv):
    mean_e = jnp.mean(e, axis=-1, keepdims=True)
    mean_ez = jnp.mean(e * z, axis=-1, keepdims=True)
    return (e - mean_e - z * mean_ez) * inv


def forward_kernel(where_ref, x_ref, o_ref, dy_ref, vec_ref, bi_ref, *refs):
    pieces = refs[:-12]
    mixed_ref, h_ref, z_ref, inv_ref, g_ref, slope_ref, dr_ref, df_ref, sums_ref = refs[-12:-3]
    out_ref, pack_ref, sem = refs[-3:]
    step = pl.program_id(0)
    keep_pack = pltpu.make_async_copy(pack_ref, out_ref, sem)

    @pl.when(step == 0)
    def _():
        put_pieces(where_ref, pieces, pack_ref)
        keep_pack.start()
        sums_ref[...] = jnp.zeros_like(sums_ref)

    b_out, gain1, shift1, b_back, gain2, shift2 = [vec_ref[i : i + 1, :] for i in range(2, 8)]
    r1 = x_ref[...].astype(f32) + dot(o_ref[...], flat(pack_ref[:, 24:27])) + b_out
    z1, inv1 = normed(r1)
    z_ref[...] = z1
    inv_ref[...] = inv1
    h1 = z1 * gain1 + shift1
    low = h1.astype(bf16)
    h_ref[...] = low
    r2 = h1 + b_back
    d = low.shape[1]
    for j in range(4):
        cols = slice(j * d, (j + 1) * d)
        wi = flat(pack_ref[:, 12 + 3 * j : 15 + 3 * j])
        g, slope = gelu_and_slope(dot(low, wi) + bi_ref[j : j + 1, :])
        g_low = g.astype(bf16)
        g_ref[:, cols] = g_low
        slope_ref[:, cols] = slope.astype(bf16)
        r2 = r2 + dot(g_low, flat(pack_ref[4 * j : 4 * j + 4, :12]))
    z2, inv2 = normed(r2)
    mixed_ref[...] = (z2 * gain2 + shift2).astype(bf16)
    dy = dy_ref[...].astype(f32)
    dr = normed_back(dy * gain2, z2, inv2)
    dr_ref[...] = dr
    df = dr.astype(bf16)
    df_ref[...] = df

    for i, term in enumerate((df.astype(f32), dy * z2, dy)):
        sums_ref[i : i + 1, :] += jnp.sum(term, axis=0, keepdims=True)

    @pl.when(step == pl.num_programs(0) - 1)
    def _():
        keep_pack.wait()


def forward(where, x, o, dy, vec, bi, pieces, rows=256):
    n, d = x.shape
    ff = 4 * d
    tiles = pieces[0].shape[1]
    tok = lambda w: pl.BlockSpec((rows, w), lambda i, s: (i, 0))
    return pl.pallas_call(
        forward_kernel,
        grid_spec=pltpu.PrefetchScalarGridSpec(
            num_scalar_prefetch=1,
            grid=(n // rows,),
            in_specs=[tok(d), tok(d), tok(d)] + [once(a) for a in (vec, bi, *pieces)],
            out_specs=[
                tok(d), tok(d), tok(d), tok(1), tok(ff), tok(ff), tok(d), tok(d),
                pl.BlockSpec((8, d), lambda i, s: (0, 0)), pl.BlockSpec(memory_space=pl.ANY),
            ],
            scratch_shapes=[
                pltpu.VMEM((CHUNKS, tiles, 16, d), bf16), pltpu.SemaphoreType.DMA,
            ],
        ),
        out_shape=[
            shape_of((n, d), bf16), shape_of((n, d), bf16), shape_of((n, d)), shape_of((n, 1)),
            shape_of((n, ff), bf16), shape_of((n, ff), bf16), shape_of((n, d)),
            shape_of((n, d), bf16), shape_of((8, d)), shape_of((CHUNKS, tiles, 16, d), bf16),
        ],
        compiler_params=PARAMS,
        name="forward",
        cost_estimate=lasts(30),
    )(where, x, o, dy, vec, bi, *pieces)


def backward_kernel(
    df_ref, slope_ref, dr_ref, z_ref, inv_ref, wo_ref, wi_ref, wb_ref, vec_ref,
    du_ref, dr1_ref, da_ref, do_ref, sums_ref, bsum_ref,
):
    @pl.when(pl.program_id(0) == 0)
    def _():
        sums_ref[...] = jnp.zeros_like(sums_ref)
        bsum_ref[...] = jnp.zeros_like(bsum_ref)

    df = df_ref[...]
    dh = dr_ref[...]
    d = df.shape[1]
    for j in range(4):
        cols = slice(j * d, (j + 1) * d)
        wi, wb = flat(wi_ref[:, 3 * j : 3 * j + 3]), flat(wb_ref[4 * j : 4 * j + 4])
        du = (dot(df, wb, NT) * slope_ref[:, cols].astype(f32)).astype(bf16)
        du_ref[:, cols] = du
        bsum_ref[j : j + 1, :] += jnp.sum(du.astype(f32), axis=0, keepdims=True)
        dh = dh + dot(du, wi, NT)
    z1 = z_ref[...]
    dr1 = normed_back(dh * vec_ref[3:4, :], z1, inv_ref[...])
    dr1_ref[...] = dr1
    da = dr1.astype(bf16)
    da_ref[...] = da
    do_ref[...] = dot(da, flat(wo_ref[...]), NT).astype(bf16)
    for i, term in enumerate((da.astype(f32), dh * z1, dh)):
        sums_ref[i : i + 1, :] += jnp.sum(term, axis=0, keepdims=True)


def backward(df, slope, dr, z, inv, pack, vec, rows=256):
    n, d = df.shape
    ff = 4 * d
    tok = lambda w: pl.BlockSpec((rows, w), lambda i: (i, 0))
    return pl.pallas_call(
        backward_kernel,
        grid=(n // rows,),
        in_specs=[tok(d), tok(ff), tok(d), tok(d), tok(1)] + second_specs(d) + [whole(vec)],
        out_specs=[
            tok(ff), tok(d), tok(d), tok(d),
            pl.BlockSpec((8, d), lambda i: (0, 0)), pl.BlockSpec((4, d), lambda i: (0, 0)),
        ],
        out_shape=[
            shape_of((n, ff), bf16), shape_of((n, d)), shape_of((n, d), bf16),
            shape_of((n, d), bf16), shape_of((8, d)), shape_of((4, d)),
        ],
        compiler_params=PARAMS,
        name="backward",
        cost_estimate=lasts(20),
    )(df, slope, dr, z, inv, pack, pack, pack, vec)


def put_slabs(where_ref, val_ref, keep_ref, send_ref, first, count, cols):
    r = keep_ref.shape[1]
    core = where_ref[0]
    for i in range(count):
        low = pl.multiple_of(2 * i * r + core * r, 8)
        high = pl.multiple_of(2 * i * r + (1 - core) * r, 8)
        keep_ref[where_ref[1 + first + i], :, cols] = val_ref[pl.ds(low, r), :].astype(bf16)
        send_ref[where_ref[1 + CHUNKS + first + i], :, cols] = val_ref[pl.ds(high, r), :].astype(bf16)


def slab_call(kernel, name, where, grid, in_specs, args, r, width, scratch, us, block=None):
    if block is None:
        slabs = pl.BlockSpec((CHUNKS, r, width), lambda i, s: (0, 0, 0))
    else:
        slabs = pl.BlockSpec((CHUNKS, r, block), lambda i, s: (0, 0, i))
    return pl.pallas_call(
        kernel,
        grid_spec=pltpu.PrefetchScalarGridSpec(
            num_scalar_prefetch=1,
            grid=grid,
            in_specs=in_specs,
            out_specs=[slabs, slabs],
            scratch_shapes=scratch,
        ),
        out_shape=[shape_of((CHUNKS, r, width), bf16)] * 2,
        compiler_params=PARAMS,
        name=name,
        cost_estimate=lasts(us),
    )(where, *args)


def back_outer_kernel(where_ref, g_ref, df_ref, keep_ref, send_ref, val_ref):
    val_ref[...] = dot(g_ref[...], df_ref[...], TN)
    step = pl.program_id(0)
    put_slabs(where_ref, val_ref, keep_ref, send_ref, step * 4, 4, slice(None))


def back_outer(where, g, df):
    n, ff = g.shape
    d = df.shape[1]
    specs = [pl.BlockSpec((n, d), lambda i, s: (0, i)), pl.BlockSpec((n, d), lambda i, s: (0, 0))]
    return slab_call(
        back_outer_kernel, "back_outer", where, (4,), specs, (g, df), ff // 32, d,
        [pltpu.VMEM((d, d), f32)], 11,
    )


def put_sums(sums1_ref, sums2_ref, bsum_ref, val_ref):
    d = sums1_ref.shape[1]
    r = d // 32
    rows = [sums1_ref[...], sums2_ref[...], jnp.zeros((112, d), f32)]
    val_ref[:, :128] = jnp.concatenate(rows, 0).T
    lane = lax.broadcasted_iota(jnp.int32, (1, 128), 1)
    mine = (lane >= 16) & (lane < 16 + 4 * r)
    for i in range(32):
        row = bsum_ref[i // 8 : i // 8 + 1, :]
        part = pltpu.roll(row, (16 - i % 8 * 4 * r) % d, 1)[:, :128]
        val_ref[i * r : i * r + 1, :128] += jnp.where(mine, part, 0.0)


def mid_outer_kernel(
    where_ref, h_ref, du_ref, o_ref, da_ref, sums1_ref, sums2_ref, bsum_ref,
    keep_ref, send_ref, val_ref,
):
    step = pl.program_id(0)

    @pl.when(step < 4)
    def _():
        val_ref[...] = dot(h_ref[...], du_ref[...], TN)

    @pl.when(step == 4)
    def _():
        val_ref[...] = dot(o_ref[...], da_ref[...], TN)

    @pl.when(step < 5)
    def _():
        put_slabs(where_ref, val_ref, keep_ref, send_ref, 0, CHUNKS, slice(None))

    @pl.when(step == 5)
    def _():
        put_sums(sums1_ref, sums2_ref, bsum_ref, val_ref)
        put_slabs(where_ref, val_ref.at[:, :128], keep_ref, send_ref, 0, CHUNKS, slice(0, 128))


def mid_outer(where, h, du, o, da, sums1, sums2, bsum):
    n, d = h.shape
    keep = lambda a: pl.BlockSpec(a.shape, lambda i, s: (0, 0))
    block = pl.BlockSpec((n, d), lambda i, s: (0, jnp.minimum(i, 3)))
    specs = [keep(h), block, keep(o), keep(da), keep(sums1), keep(sums2), keep(bsum)]
    return slab_call(
        mid_outer_kernel, "mid_outer", where, (6,), specs, (h, du, o, da, sums1, sums2, bsum), d // 32,
        5 * d + 128, [pltpu.VMEM((d, d), f32)], 14, d,
    )


def qkv_outer_kernel(where_ref, x_ref, *refs):
    grad_refs, (keep_ref, send_ref, val_ref, sums_ref) = refs[:-4], refs[-4:]
    step = pl.program_id(0)
    width = grad_refs[0].shape[2]

    @pl.when(step == 0)
    def _():
        sums_ref[...] = jnp.zeros_like(sums_ref)

    @pl.when(step < 3)
    def _():
        for i, ref in enumerate(grad_refs):
            grads = ref[0]
            cols = slice(i * width, (i + 1) * width)
            val_ref[:, cols] = dot(x_ref[...], grads, TN)
            total = jnp.sum(grads.astype(f32), axis=0, keepdims=True)
            sums_ref[pl.ds(step, 1), cols] = total
        put_slabs(where_ref, val_ref, keep_ref, send_ref, 0, CHUNKS, slice(None))

    @pl.when(step == 3)
    def _():
        val_ref[:, :128] = sums_ref[...].T
        put_slabs(where_ref, val_ref.at[:, :128], keep_ref, send_ref, 0, CHUNKS, slice(0, 128))


def qkv_outer(where, x, grads):
    n, d = x.shape
    block = pl.BlockSpec((1, n, grads[0].shape[2]), lambda i, s: (jnp.minimum(i, 2), 0, 0))
    specs = [pl.BlockSpec((n, d), lambda i, s: (0, 0))] + [block] * len(grads)
    return slab_call(
        qkv_outer_kernel, "qkv_outer", where, (4,), specs, (x, *grads), d // 32, 3 * d + 128,
        [pltpu.VMEM((d, d), f32), pltpu.VMEM((128, d), f32)], 10, d,
    )


def input_grad_kernel(dr_ref, *refs):
    grad_refs, (wq_ref, wk_ref, wv_ref, out_ref) = refs[:-4], refs[-4:]
    width = grad_refs[0].shape[2]
    total = dr_ref[...]
    for i, w_ref in enumerate((wq_ref, wk_ref, wv_ref)):
        for j, ref in enumerate(grad_refs):
            w = flat(w_ref[:, :, :, j * width : (j + 1) * width])
            total = total + dot(ref[i], w, NT)
    out_ref[...] = total


def input_grad(dr, grads, pack, rows=256):
    n, d = dr.shape
    width = grads[0].shape[2]
    weight = lambda j: pl.BlockSpec((CHUNKS, 3, 16, d), lambda i: (0, j, 0, 0))
    return pl.pallas_call(
        input_grad_kernel,
        grid=(n // rows,),
        in_specs=[pl.BlockSpec((rows, d), lambda i: (i, 0))]
        + [pl.BlockSpec((3, rows, width), lambda i: (0, i, 0))] * len(grads)
        + [weight(0), weight(1), weight(2)],
        out_specs=pl.BlockSpec((rows, d), lambda i: (i, 0)),
        out_shape=shape_of((n, d)),
        compiler_params=PARAMS,
        name="input_grad",
        cost_estimate=lasts(9),
    )(dr, *grads, pack, pack, pack)


def bit_of(axis, bit):
    return (lax.axis_index(axis) // bit) % 2


def swap(x, axis, bits):
    size = lax.axis_size(axis)
    return lax.ppermute(x, axis, [(i, i ^ bits) for i in range(size)])


def ordered(mine, own, other):
    return jnp.where(mine == 0, own, other), jnp.where(mine == 0, other, own)


def gather_bit(x, axis, bit):
    first, second = ordered(bit_of(axis, bit), x, swap(x, axis, bit))
    return jnp.stack([first, second], 1).reshape((2 * x.shape[0],) + x.shape[1:])


def gather_two_bits(x, axis, high, low):
    a, b, c, d = x, swap(x, axis, low), swap(x, axis, high), swap(x, axis, high | low)
    a, b = ordered(bit_of(axis, low), a, b)
    c, d = ordered(bit_of(axis, low), c, d)
    a, c = ordered(bit_of(axis, high), a, c)
    b, d = ordered(bit_of(axis, high), b, d)
    return jnp.stack([a, b, c, d], 1).reshape((4 * x.shape[0],) + x.shape[1:])


def upper_bits():
    count = lax.axis_size("dp").bit_length() - 1
    return [1 << i for i in range(count - 1, 0, -1)]


def gather(x):
    rows, cols = x.shape
    x = x[None]
    bits = upper_bits()
    if len(bits) == 2:
        x = gather_two_bits(x, "dp", *bits)
    else:
        for bit in bits:
            x = gather_bit(x, "dp", bit)
    k = x.shape[0]
    one = gather_bit(gather_bit(x[:, :, : cols // 2], "dp", 1), "fsdp", 2)
    two = gather_bit(gather_bit(x[:, :, cols // 2 :], "fsdp", 2), "dp", 1)
    two = jnp.swapaxes(two.reshape(k, 2, 2, rows, cols // 2), 1, 2).reshape(one.shape)
    x = jnp.concatenate([one, two], -1)
    return gather_bit(x, "fsdp", 1)


def scatter_bit(x, axis, bit, dim):
    mine = bit_of(axis, bit)
    keep = lax.dynamic_index_in_dim(x, mine, dim, keepdims=False)
    send = lax.dynamic_index_in_dim(x, 1 - mine, dim, keepdims=False)
    return (keep.astype(f32) + swap(send, axis, bit).astype(f32)).astype(x.dtype)


def scatter_two_bits(x, axis, high, low):
    mine = bit_of(axis, high) * 2 + bit_of(axis, low)
    part = lambda i: lax.dynamic_index_in_dim(x, mine ^ i, 0, keepdims=False)
    total = part(0).astype(f32)
    for i, bits in ((1, low), (2, high), (3, high | low)):
        total = total + swap(part(i), axis, bits).astype(f32)
    return total


def scatter_sum(x):
    devices, rows, cols = x.shape
    bits = upper_bits()
    x = scatter_bit(x.reshape(devices // 8, 2, 2, 2, rows, cols), "fsdp", 1, 3)
    one = scatter_bit(scatter_bit(x[..., : cols // 2], "fsdp", 2, 2), "dp", 1, 1)
    two = scatter_bit(scatter_bit(x[..., cols // 2 :], "dp", 1, 1), "fsdp", 2, 1)
    x = jnp.concatenate([one, two], -1)
    if len(bits) == 2:
        return scatter_two_bits(x, "dp", *bits)
    x = x.reshape((2,) * len(bits) + (rows, cols))
    for bit in bits:
        x = scatter_bit(x, "dp", bit, 0)
    return x.astype(f32)


def seats():
    dp, fsdp = lax.axis_index("dp"), lax.axis_index("fsdp")
    return dp // 2, dp % 2, fsdp // 2, fsdp % 2


def swap_all(x, dz=0, first=0, second=0, core=0):
    pairs = []
    for i in range(32):
        z, y, xx, c = i // 8, i // 4 % 2, i // 2 % 2, i % 2
        dy, dx = (first, second) if c == 0 else (second, first)
        pairs.append((i, (((z ^ dz) * 2 + (y ^ dy)) * 2 + (xx ^ dx)) * 2 + (c ^ core)))
    return lax.ppermute(x, AXES, pairs)


def after(x, *others):
    return lax.optimization_barrier((x, *others))[0]


def halves_kernel(core_ref, wq_ref, wk_ref, wv_ref, wo_ref, wi_ref, wb_ref, own_ref, send_ref):
    r, d = wq_ref.shape
    for core, out in ((core_ref[0], own_ref), (1 - core_ref[0], send_ref)):
        half = lambda base: pl.ds(pl.multiple_of(base + core * (d // 2), 128), d // 2)
        for j in range(4):
            out[j] = wi_ref[:, half(j * d)]
        back = wb_ref[:, half(0)].astype(f32)
        for j in range(4):
            out[4 + j] = back[j * r : (j + 1) * r].astype(bf16)
        for j, ref in enumerate((wo_ref, wq_ref, wk_ref, wv_ref)):
            out[8 + j] = ref[:, half(0)]


def halves(core, *weights):
    r, d = weights[0].shape
    return pl.pallas_call(
        halves_kernel,
        in_specs=[pl.BlockSpec(memory_space=pltpu.SMEM)]
        + [pl.BlockSpec(memory_space=pltpu.VMEM)] * 6,
        out_specs=[pl.BlockSpec(memory_space=pltpu.VMEM)] * 2,
        out_shape=[shape_of((12, r, d // 2), bf16)] * 2,
        compiler_params=PARAMS,
        name="halves",
        cost_estimate=lasts(2),
    )(core, *weights)


def chip_kernel(core_ref, own_ref, got_ref, *refs):
    small, (one_ref, two_ref, rows_ref) = refs[:-3], refs[-3:]
    swapped = core_ref[0] == 1

    def put(out_ref, tile, start, count):
        own = own_ref[start : start + count].astype(f32)
        got = got_ref[start : start + count].astype(f32)
        low, high = jnp.where(swapped, got, own), jnp.where(swapped, own, got)
        rows = jnp.concatenate([a[i] for a in (low, high) for i in range(count)], 0).astype(bf16)
        tiles = rows.shape[0] // 16
        out_ref[tile : tile + tiles] = rows.reshape(tiles, 16, rows.shape[1])

    for j in range(4):
        put(two_ref, 12 + 3 * j, j, 1)
    put(two_ref, 24, 8, 1)
    put(two_ref, 0, 4, 4)
    for j in range(3):
        put(one_ref, 3 * j, 9 + j, 1)
    rows_ref[...] = jnp.zeros_like(rows_ref)
    for i, ref in enumerate(small):
        rows_ref[i : i + 1, : ref.shape[1]] = ref[...].astype(f32)
    one_ref[9] = rows_ref[...].astype(bf16)


def chip_shards(core, own, got, small):
    width = own.shape[2]
    return pl.pallas_call(
        chip_kernel,
        in_specs=[pl.BlockSpec(memory_space=pltpu.SMEM)]
        + [pl.BlockSpec(memory_space=pltpu.VMEM)] * (2 + len(small)),
        out_specs=[pl.BlockSpec(memory_space=pltpu.VMEM)] * 2,
        out_shape=[shape_of((tiles, 16, width), bf16) for tiles in (10, 27)],
        scratch_shapes=[pltpu.VMEM((16, width), f32)],
        compiler_params=PARAMS,
        name="chip_shards",
        cost_estimate=lasts(2),
    )(core, own, got, *[a[None] for a in small])


def pair_up(x, dz, *late):
    return jnp.concatenate([x, after(swap_all(x, dz=dz), *late)])


def near_pieces(stack):
    return [stack, swap_all(stack, first=1), swap_all(stack, second=1)]


def all_pieces(near):
    own = near + [swap_all(near[1], second=1)]
    return own + [swap_all(piece, core=1) for piece in own]


class Scatter:
    def __init__(self, small_slice, keep, send, direct=False):
        self.state = (keep, send)
        self.small_slice = small_slice
        self.steps = 0
        self.total = None
        self.direct = direct

    def hold(self, *late):
        self.state = tuple(after(part, *late) for part in self.state)

    def step(self, *late):
        if not self.small_slice:
            return ()
        self.steps += 1
        hops = [{"core": 1}, {"second": 1}, {"first": 1}]
        if not self.direct:
            hops += [{"dz": 1}, {"dz": 2}]
        if self.steps <= len(hops):
            keep, send = self.state
            got = after(swap_all(send, **hops[self.steps - 1]), *late)
            total = keep.astype(f32) + got.astype(f32)
            if self.steps == 5:
                self.total = total[0]
                return (self.total,)
            total = total.astype(bf16)
            half = total.shape[0] // 2
            self.state = (total,) if self.direct and self.steps == 3 else (total[:half], total[half:])
            return self.state
        (parts,) = self.state
        total = parts[0].astype(f32)
        for i, dz in ((1, 2), (2, 1), (3, 3)):
            total = total + after(swap_all(parts[i], dz=dz), *late).astype(f32)
        self.total = total
        return (total,)

    def result(self, devices):
        if self.small_slice:
            while self.total is None:
                self.step()
            return self.total
        keep, send = self.state
        stacked = jnp.stack([keep, send], 1)
        return scatter_sum(stacked.reshape(devices, -1, keep.shape[-1]))


def places(lengths, n):
    ends = jnp.cumsum(lengths)
    start = jnp.sum(jnp.where(lengths == n // 2, ends - n // 2, 0))
    position = (start + n // 2 + jnp.arange(n // 2, dtype=jnp.int32)) % n
    segment = jnp.sum((position[:, None] >= ends[None, :]).astype(jnp.int32), axis=1)
    return start, segment.astype(f32)


def vectors(small, r, d):
    vec = jnp.transpose(small[:, : 8 * r].reshape(-1, 8, r), (1, 0, 2)).reshape(8, d)
    return vec, small[:, 8 * r : 12 * r].reshape(4, d)


def body(
    tokens, lengths, cotangent, w_query, w_key, w_value, w_out, b_query, b_value, b_out,
    norm1_gain, norm1_shift, w_in, w_back, b_in, b_back, norm2_gain, norm2_shift,
):
    _, n, d = tokens.shape
    devices = lax.axis_size("dp") * lax.axis_size("fsdp")
    r = w_query.shape[0]
    small_slice = lax.axis_size("dp") == 8 and lax.axis_size("fsdp") == 4
    start, segment = places(lengths[0], n)
    seg_row, seg_col = segment[None, :], segment[:, None]
    rolled = lambda a: jnp.roll(a[0], -start, axis=0)
    small = [b_query, b_value, b_out, norm1_gain, norm1_shift, b_back, norm2_gain, norm2_shift, b_in]
    if small_slice:
        z, y, across, core = seats()
        i = jnp.arange(32, dtype=jnp.int32)
        first, second = i // 4 % 2, i // 8 % 2
        other = (core + i // 16) % 2
        chip = ((z ^ (i % 2 * 2 + i // 2 % 2)) * 2 + (y ^ jnp.where(other == 0, first, second))) * 2
        chip = chip + (across ^ jnp.where(other == 0, second, first))
        gather_at = jnp.concatenate([core[None], chip])
        i = jnp.arange(16, dtype=jnp.int32)
        dz, dy_, dx = z ^ i // 4, y ^ i // 2 % 2, across ^ i % 2
        dz = dz % 2 * 2 + dz // 2
        slot = lambda c: jnp.where(c == 0, dx, dy_) * 8 + jnp.where(c == 0, dy_, dx) * 4 + dz
        where = jnp.concatenate([core[None], slot(core), slot(1 - core)])
        own, send = halves(core[None], w_query, w_key, w_value, w_out, w_in, w_back)
        one, two = chip_shards(core[None], own, swap_all(send, core=1), small)
        x = rolled(after(tokens, one))
        pair1 = pair_up(one[None], 2, x, gather_at, where)
        dy = rolled(after(cotangent, pair1))
        pair2 = pair_up(after(two, pair1)[None], 2)
        stack1 = pair_up(pair1, 1, dy)
        first1 = jnp.concatenate([stack1, after(swap_all(stack1, first=1), pair2)])
        stack2 = pair_up(pair2, 1, first1)
        pieces1 = [first1, swap_all(first1, second=1)]
        near2 = near_pieces(after(stack2, first1))
        pieces1 += [swap_all(piece, core=1) for piece in pieces1]
    else:
        x, dy = rolled(tokens), rolled(cotangent)
        step = jnp.arange(16, dtype=jnp.int32)
        where = jnp.concatenate([jnp.zeros((1,), jnp.int32), step, step])
        gather_at = where
        small = jnp.concatenate(small)
        small = jnp.pad(small, (0, 8 * d - small.shape[0])).reshape(8, d)
        pack1 = gather(jnp.concatenate([w_query, w_key, w_value, small]))
        vec, bi = vectors(pack1[:, 3 * r], r, d)
        rows = jnp.pad(vec.reshape(8, 16, 2, -1), ((0, 0), (0, 0), (0, 0), (0, d // 2 - d // 32)))
        row = jnp.pad(bi.reshape(1, 16, 2, -1), ((0, 7), (0, 0), (0, 0), (0, d // 2 - d // 8)))
        small = jnp.transpose(jnp.concatenate([rows, row]), (1, 0, 2, 3)).reshape(16, 1, 16, d)
        tiles = lambda w: w.reshape(CHUNKS, -1, 16, d)
        pack1 = [tiles(pack1[:, i * r : (i + 1) * r]) for i in range(3)] + [small]
        pack2 = gather(jnp.concatenate([w_in[:, j * d : (j + 1) * d] for j in range(4)] + [w_back, w_out]))
        cuts = [(4, 8), (0, 1), (1, 2), (2, 3), (3, 4), (8, 9)]
        pack2 = [tiles(pack2[:, a * r : b * r]) for a, b in cuts]
        cut = lambda p: [
            jnp.concatenate(p, 1)[4 * i : 4 * i + 4, :, :, j * (d // 2) : (j + 1) * (d // 2)]
            for j in range(2)
            for i in range(4)
        ]
        pieces1, pieces2 = cut(pack1), cut(pack2)

    q, k, v, o, lse, vec, bi, pack1 = attend(gather_at, x, seg_row, seg_col, pieces1)
    if small_slice:
        pieces2 = all_pieces([after(a, o) for a in near2])
    mixed, h, zhat, inv, g, slope, dr, df, sums2, pack2 = forward(
        gather_at, x, o, dy, vec, bi, pieces2
    )
    scatter1 = Scatter(small_slice, *back_outer(where, g, df))
    du, dr1, da, do, sums1, bsum = backward(
        after(df, *scatter1.state), slope, dr, zhat, inv, pack2, vec
    )
    h_late = after(h, du, *scatter1.step(du))
    scatter2 = Scatter(small_slice, *mid_outer(where, h_late, du, o, da, sums1, sums2, bsum))
    late = after(q, *scatter1.step(*scatter2.state))
    scatter2.hold(late)
    grads = [attend_back(late, k, v, do, lse, seg_row, seg_col, 0)]
    late = after(q, *scatter1.step(grads[0]), *scatter2.step(grads[0]))
    grads.append(attend_back(late, k, v, do, lse, seg_row, seg_col, 1))
    late = after(q, grads[1], *scatter1.step(grads[1]))
    grads.append(attend_back(late, k, v, do, lse, seg_row, seg_col, 2))
    late = after(x, *scatter2.step(grads[2]), *scatter1.step(grads[2]))
    scatter3 = Scatter(small_slice, *qkv_outer(where, late, grads), True)
    late = scatter2.step(*scatter3.state)
    late = late + scatter3.step(*late)
    grad_tokens = input_grad(after(dr1, *late), grads, pack1)
    late = scatter3.step(grad_tokens) + scatter2.step(grad_tokens)
    unroll = lambda a, *late: jnp.roll(after(a, *late), start, axis=0)[None]
    mixed, grad_tokens = unroll(mixed, *late), unroll(grad_tokens, *late)
    scatter3.step(mixed, grad_tokens)
    scatter2.step(mixed, grad_tokens)
    mid_grad = scatter2.result(devices)
    back_grad = scatter1.result(devices)
    rest = scatter3.result(devices)
    gq, gk, gv = [rest[:, i * d : (i + 1) * d] for i in range(3)]
    gbq, _, gbv = rest[:, 3 * d : 3 * d + 3].T
    in_grad, out_grad = mid_grad[:, : 4 * d], mid_grad[:, 4 * d : 5 * d]
    vecs = mid_grad[:, 5 * d : 5 * d + 11].T
    if small_slice:
        gbi = mid_grad[0, 5 * d + 16 : 5 * d + 16 + 4 * r]
    else:
        gbi = lax.psum_scatter(bsum.reshape(4 * d), AXES, scatter_dimension=0, tiled=True)
    return (
        mixed, grad_tokens, gq, gk, gv, out_grad,
        gbq, gbv, vecs[0], vecs[1], vecs[2],
        in_grad, back_grad, gbi, vecs[8], vecs[9], vecs[10],
    )


def solution(mesh):
    act, mat, vec = P(AXES, None, None), P(AXES, None), P(AXES)
    return jax.shard_map(
        body,
        mesh=mesh,
        in_specs=(act, mat, act, mat, mat, mat, mat, vec, vec, vec, vec, vec, mat, mat, vec, vec, vec, vec),
        out_specs=(act, act, mat, mat, mat, mat, vec, vec, vec, vec, vec, mat, mat, vec, vec, vec, vec),
        check_vma=False,
    )
```

```python
import functools

import jax
import jax.numpy as jnp
from jax import lax
from jax.experimental import pallas as pl
from jax.experimental.pallas import tpu as pltpu
from jax.sharding import PartitionSpec as P

HEAD_DIM = 64
MASKED = -1e30
AXES = ("dp", "fsdp")
CHUNKS = 16
f32 = jnp.float32
bf16 = jnp.bfloat16
NN = (((1,), (0,)), ((), ()))
NT = (((1,), (1,)), ((), ()))
TN = (((0,), (0,)), ((), ()))
PARAMS = pltpu.CompilerParams(vmem_limit_bytes=56 << 20)


def dot(left, right, dims=NN):
    return lax.dot_general(left, right, dims, preferred_element_type=f32)


def shape_of(shape, dtype=f32):
    return jax.ShapeDtypeStruct(shape, dtype)


def lasts(us):
    return pl.CostEstimate(flops=int(us * 1.1e9), bytes_accessed=0, transcendentals=0)


def whole(array):
    return pl.BlockSpec(array.shape, lambda i: (0,) * array.ndim)


def flat(weight):
    return weight.reshape(-1, weight.shape[-1])


def put_pieces(where_ref, pieces, pack_ref):
    width = pieces[0].shape[-1]
    at = 1
    for i, piece in enumerate(pieces):
        half = where_ref[0] if i < len(pieces) // 2 else 1 - where_ref[0]
        cols = pl.ds(pl.multiple_of(half * width, 128), width)
        for j in range(piece.shape[0]):
            pack_ref[where_ref[at], :, :, cols] = piece[j]
            at += 1


def once(array):
    rank = array.ndim
    return pl.BlockSpec(array.shape, lambda i, s: (0,) * rank, pipeline_mode=pl.Buffered(1))


def spread(small_ref, vec_ref, bias_ref):
    d = vec_ref.shape[1]
    r = d // 32
    vec = jnp.zeros((16, d), f32)
    bias = [jnp.zeros((1, d), f32) for _ in range(4)]
    for i in range(32):
        half = slice(i % 2 * (d // 2), (i % 2 + 1) * (d // 2))
        mine = small_ref[i // 2, small_ref.shape[1] - 1, :, half].astype(f32)
        mine = jnp.concatenate([mine, jnp.zeros_like(mine)], 1)
        vec = vec + (pltpu.roll(mine, i * r, 1) if i else mine)
        shift = i % 8 * 4 * r
        row = mine[8:9]
        bias[i // 8] = bias[i // 8] + (pltpu.roll(row, shift, 1) if shift else row)
    vec_ref[...] = vec[:8]
    bias_ref[...] = jnp.concatenate(bias, 0)


def second_specs(d):
    at = lambda tiles, j: pl.BlockSpec((CHUNKS, tiles, 16, d), lambda i: (0, j, 0, 0))
    return [at(3, 8), at(12, 1), at(12, 0)]


def attend_kernel(
    where_ref, x_ref, seg_row_ref, seg_col_ref, *refs
):
    pieces = refs[:-11]
    q_ref, k_ref, v_ref, o_ref, lse_ref, vec_ref, bi_ref, out_ref, pack_ref, bias_ref, sem = refs[-11:]
    half = x_ref.shape[0] // 2
    width = q_ref.shape[1]
    step = pl.program_id(0)
    keep_pack = pltpu.make_async_copy(pack_ref, out_ref, sem)

    @pl.when(step == 0)
    def _():
        bias_ref[...] = jnp.where(seg_col_ref[...] == seg_row_ref[...], 0.0, MASKED)
        put_pieces(where_ref, pieces, pack_ref)
        keep_pack.start()
        spread(pack_ref, vec_ref, bi_ref)

    x = x_ref[...]
    group = pl.ds(pl.multiple_of(step * width, 128), width)
    weight = lambda j: flat(pack_ref[:, 3 * j : 3 * j + 3, :, group])
    query = (dot(x, weight(0)) + vec_ref[0:1, group]).astype(bf16)
    q_ref[...] = query * jnp.asarray(HEAD_DIM**-0.5, bf16)
    k_ref[...] = dot(x, weight(1)).astype(bf16)
    v_ref[...] = (dot(x, weight(2)) + vec_ref[1:2, group]).astype(bf16)
    for part in range(2):
        rows = slice(part * half, (part + 1) * half)
        for pair in range(width // 128):
            cols = slice(pair * 128, (pair + 1) * 128)
            keys = k_ref[rows, cols]
            values_t = v_ref[rows, cols].T
            queries = q_ref[rows, cols]
            lane = lax.broadcasted_iota(jnp.int32, queries.shape, 1)
            outs = []
            for h in range(2):
                mine = (lane < HEAD_DIM) if h == 0 else (lane >= HEAD_DIM)
                scores = dot(keys, jnp.where(mine, queries, jnp.zeros_like(queries)), NT)
                if part == 1:
                    scores = scores + bias_ref[...]
                top = jnp.max(scores, axis=0, keepdims=True)
                terms = jnp.exp(scores - top)
                total = jnp.sum(terms, axis=0, keepdims=True)
                mixed = dot(values_t[h * HEAD_DIM : (h + 1) * HEAD_DIM, :], terms.astype(bf16))
                outs.append(mixed / total)
                lse_ref[0, pair * 2 + h : pair * 2 + h + 1, rows] = top + jnp.log(total)
            o_ref[rows, cols] = jnp.concatenate(outs, 0).T.astype(bf16)

    @pl.when(step == pl.num_programs(0) - 1)
    def _():
        keep_pack.wait()


def attend(where, x, seg_row, seg_col, pieces, width=256):
    n, d = x.shape
    groups = d // width
    tiles = pieces[0].shape[1]
    act = pl.BlockSpec((n, width), lambda i, s: (0, i))
    heads = width // HEAD_DIM
    still = lambda rows: pl.BlockSpec((rows, d), lambda i, s: (0, 0))
    return pl.pallas_call(
        attend_kernel,
        grid_spec=pltpu.PrefetchScalarGridSpec(
            num_scalar_prefetch=1,
            grid=(groups,),
            in_specs=[once(a) for a in (x, seg_row, seg_col, *pieces)],
            out_specs=[
                act, act, act, act, pl.BlockSpec((1, heads, n), lambda i, s: (i, 0, 0)),
                still(8), still(4), pl.BlockSpec(memory_space=pl.ANY),
            ],
            scratch_shapes=[
                pltpu.VMEM((CHUNKS, tiles, 16, d), bf16),
                pltpu.VMEM((n // 2, n // 2), f32),
                pltpu.SemaphoreType.DMA,
            ],
        ),
        out_shape=[shape_of((n, d), bf16)] * 4
        + [shape_of((groups, heads, n)), shape_of((8, d)), shape_of((4, d))]
        + [shape_of((CHUNKS, tiles, 16, d), bf16)],
        compiler_params=PARAMS,
        name="attend",
        cost_estimate=lasts(0),
    )(where, x, seg_row, seg_col, *pieces)


def attend_back_kernel(
    q_ref, k_ref, v_ref, do_ref, lse_ref, seg_row_ref, seg_col_ref, grads_ref, bias_ref
):
    n, width = q_ref.shape
    half = n // 2

    @pl.when(pl.program_id(0) == 0)
    def _():
        bias_ref[...] = jnp.where(seg_col_ref[...] == seg_row_ref[...], 0.0, MASKED)

    for part in range(2):
        rows = slice(part * half, (part + 1) * half)
        for pair in range(width // 128):
            cols = slice(pair * 128, (pair + 1) * 128)
            keys, values = k_ref[rows, cols], v_ref[rows, cols]
            queries, grads = q_ref[rows, cols], do_ref[rows, cols]
            keys_t = keys.T
            lane = lax.broadcasted_iota(jnp.int32, queries.shape, 1)
            dqs = []
            dk = dv = None
            for h in range(2):
                mine = (lane < HEAD_DIM) if h == 0 else (lane >= HEAD_DIM)
                query = jnp.where(mine, queries, jnp.zeros_like(queries))
                grad = jnp.where(mine, grads, jnp.zeros_like(grads))
                scores = dot(keys, query, NT)
                if part == 1:
                    scores = scores + bias_ref[...]
                prob = jnp.exp(scores - lse_ref[0, pair * 2 + h : pair * 2 + h + 1, rows])
                prob_grad = dot(values, grad, NT)
                delta = jnp.sum(prob * prob_grad, axis=0, keepdims=True)
                score_grad = (prob * (prob_grad - delta)).astype(bf16)
                dv_h = dot(prob.astype(bf16), grad)
                dk_h = dot(score_grad, query)
                dv = dv_h if h == 0 else dv + dv_h
                dk = dk_h if h == 0 else dk + dk_h
                dqs.append(dot(keys_t[h * HEAD_DIM : (h + 1) * HEAD_DIM, :], score_grad))
            dq = jnp.concatenate(dqs, 0).T * HEAD_DIM**-0.5
            grads_ref[0, rows, cols] = dq.astype(bf16)
            grads_ref[1, rows, cols] = dk.astype(bf16)
            grads_ref[2, rows, cols] = dv.astype(bf16)


def attend_back(q, k, v, do, lse, seg_row, seg_col, group, count, width=256):
    n, d = q.shape
    act = pl.BlockSpec((n, width), lambda i: (0, group + i))
    heads = width // HEAD_DIM
    return pl.pallas_call(
        attend_back_kernel,
        grid=(count,),
        in_specs=[
            act, act, act, act, pl.BlockSpec((1, heads, n), lambda i: (group + i, 0, 0)),
            whole(seg_row), whole(seg_col),
        ],
        out_specs=pl.BlockSpec((3, n, width), lambda i: (0, 0, i)),
        out_shape=shape_of((3, n, count * width), bf16),
        scratch_shapes=[pltpu.VMEM((n // 2, n // 2), f32)],
        compiler_params=PARAMS,
        name="attend_back",
        cost_estimate=lasts(9 * count),
    )(q, k, v, do, lse, seg_row, seg_col)


def gelu_and_slope(u):
    size = jnp.abs(u)
    t = 1.0 / (1.0 + (0.3275911 * 0.7071067811865476) * size)
    bell = jnp.exp(-0.5 * u * u)
    series = t * (
        0.127414796
        + t * (-0.142248368 + t * (0.7107068705 + t * (-0.7265760135 + t * 0.5307027145)))
    )
    tail = series * bell
    cdf = jnp.where(u >= 0, 1.0 - tail, tail)
    return u * cdf, cdf + u * (bell * 0.3989422804014327)


def normed(value):
    centre = value - jnp.mean(value, axis=-1, keepdims=True)
    inv = lax.rsqrt(jnp.mean(centre * centre, axis=-1, keepdims=True) + 1e-6)
    return centre * inv, inv


def normed_back(e, z, inv):
    mean_e = jnp.mean(e, axis=-1, keepdims=True)
    mean_ez = jnp.mean(e * z, axis=-1, keepdims=True)
    return (e - mean_e - z * mean_ez) * inv


def forward_kernel(where_ref, x_ref, o_ref, dy_ref, vec_ref, bi_ref, *refs):
    pieces = refs[:-12]
    mixed_ref, h_ref, z_ref, inv_ref, g_ref, slope_ref, dr_ref, df_ref, sums_ref = refs[-12:-3]
    out_ref, pack_ref, sem = refs[-3:]
    step = pl.program_id(0)
    keep_pack = pltpu.make_async_copy(pack_ref, out_ref, sem)

    @pl.when(step == 0)
    def _():
        put_pieces(where_ref, pieces, pack_ref)
        keep_pack.start()
        sums_ref[...] = jnp.zeros_like(sums_ref)

    b_out, gain1, shift1, b_back, gain2, shift2 = [vec_ref[i : i + 1, :] for i in range(2, 8)]
    r1 = x_ref[...].astype(f32) + dot(o_ref[...], flat(pack_ref[:, 24:27])) + b_out
    z1, inv1 = normed(r1)
    z_ref[...] = z1
    inv_ref[...] = inv1
    h1 = z1 * gain1 + shift1
    low = h1.astype(bf16)
    h_ref[...] = low
    r2 = h1 + b_back
    d = low.shape[1]
    for j in range(4):
        cols = slice(j * d, (j + 1) * d)
        wi = flat(pack_ref[:, 12 + 3 * j : 15 + 3 * j])
        g, slope = gelu_and_slope(dot(low, wi) + bi_ref[j : j + 1, :])
        g_low = g.astype(bf16)
        g_ref[:, cols] = g_low
        slope_ref[:, cols] = slope.astype(bf16)
        r2 = r2 + dot(g_low, flat(pack_ref[4 * j : 4 * j + 4, :12]))
    z2, inv2 = normed(r2)
    mixed_ref[...] = (z2 * gain2 + shift2).astype(bf16)
    dy = dy_ref[...].astype(f32)
    dr = normed_back(dy * gain2, z2, inv2)
    dr_ref[...] = dr
    df = dr.astype(bf16)
    df_ref[...] = df

    for i, term in enumerate((df.astype(f32), dy * z2, dy)):
        sums_ref[i : i + 1, :] += jnp.sum(term, axis=0, keepdims=True)

    @pl.when(step == pl.num_programs(0) - 1)
    def _():
        keep_pack.wait()


def forward(where, x, o, dy, vec, bi, pieces, rows=256):
    n, d = x.shape
    ff = 4 * d
    tiles = pieces[0].shape[1]
    tok = lambda w: pl.BlockSpec((rows, w), lambda i, s: (i, 0))
    return pl.pallas_call(
        forward_kernel,
        grid_spec=pltpu.PrefetchScalarGridSpec(
            num_scalar_prefetch=1,
            grid=(n // rows,),
            in_specs=[tok(d), tok(d), tok(d)] + [once(a) for a in (vec, bi, *pieces)],
            out_specs=[
                tok(d), tok(d), tok(d), tok(1), tok(ff), tok(ff), tok(d), tok(d),
                pl.BlockSpec((8, d), lambda i, s: (0, 0)), pl.BlockSpec(memory_space=pl.ANY),
            ],
            scratch_shapes=[
                pltpu.VMEM((CHUNKS, tiles, 16, d), bf16), pltpu.SemaphoreType.DMA,
            ],
        ),
        out_shape=[
            shape_of((n, d), bf16), shape_of((n, d), bf16), shape_of((n, d)), shape_of((n, 1)),
            shape_of((n, ff), bf16), shape_of((n, ff), bf16), shape_of((n, d)),
            shape_of((n, d), bf16), shape_of((8, d)), shape_of((CHUNKS, tiles, 16, d), bf16),
        ],
        compiler_params=PARAMS,
        name="forward",
        cost_estimate=lasts(30),
    )(where, x, o, dy, vec, bi, *pieces)


def backward_kernel(
    df_ref, slope_ref, dr_ref, z_ref, inv_ref, wo_ref, wi_ref, wb_ref, vec_ref,
    du_ref, dr1_ref, da_ref, do_ref, sums_ref, bsum_ref,
):
    @pl.when(pl.program_id(0) == 0)
    def _():
        sums_ref[...] = jnp.zeros_like(sums_ref)
        bsum_ref[...] = jnp.zeros_like(bsum_ref)

    df = df_ref[...]
    dh = dr_ref[...]
    d = df.shape[1]
    for j in range(4):
        cols = slice(j * d, (j + 1) * d)
        wi, wb = flat(wi_ref[:, 3 * j : 3 * j + 3]), flat(wb_ref[4 * j : 4 * j + 4])
        du = (dot(df, wb, NT) * slope_ref[:, cols].astype(f32)).astype(bf16)
        du_ref[:, cols] = du
        bsum_ref[j : j + 1, :] += jnp.sum(du.astype(f32), axis=0, keepdims=True)
        dh = dh + dot(du, wi, NT)
    z1 = z_ref[...]
    dr1 = normed_back(dh * vec_ref[3:4, :], z1, inv_ref[...])
    dr1_ref[...] = dr1
    da = dr1.astype(bf16)
    da_ref[...] = da
    do_ref[...] = dot(da, flat(wo_ref[...]), NT).astype(bf16)
    for i, term in enumerate((da.astype(f32), dh * z1, dh)):
        sums_ref[i : i + 1, :] += jnp.sum(term, axis=0, keepdims=True)


def backward(df, slope, dr, z, inv, pack, vec, rows=256):
    n, d = df.shape
    ff = 4 * d
    tok = lambda w: pl.BlockSpec((rows, w), lambda i: (i, 0))
    return pl.pallas_call(
        backward_kernel,
        grid=(n // rows,),
        in_specs=[tok(d), tok(ff), tok(d), tok(d), tok(1)] + second_specs(d) + [whole(vec)],
        out_specs=[
            tok(ff), tok(d), tok(d), tok(d),
            pl.BlockSpec((8, d), lambda i: (0, 0)), pl.BlockSpec((4, d), lambda i: (0, 0)),
        ],
        out_shape=[
            shape_of((n, ff), bf16), shape_of((n, d)), shape_of((n, d), bf16),
            shape_of((n, d), bf16), shape_of((8, d)), shape_of((4, d)),
        ],
        compiler_params=PARAMS,
        name="backward",
        cost_estimate=lasts(20),
    )(df, slope, dr, z, inv, pack, pack, pack, vec)


def put_slabs(where_ref, val_ref, keep_ref, send_ref, first, count, cols):
    r = keep_ref.shape[1]
    core = where_ref[0]
    for i in range(count):
        low = pl.multiple_of(2 * i * r + core * r, 8)
        high = pl.multiple_of(2 * i * r + (1 - core) * r, 8)
        keep_ref[where_ref[1 + first + i], :, cols] = val_ref[pl.ds(low, r), :].astype(bf16)
        send_ref[where_ref[1 + CHUNKS + first + i], :, cols] = val_ref[pl.ds(high, r), :].astype(bf16)


def outer_slabs(where_ref, left, right, val_ref, keep_ref, send_ref, first, count):
    width = right.shape[1]
    for cols in (slice(0, width * 2 // 3), slice(width * 2 // 3, width)):
        part = val_ref.at[:, cols]
        part[...] = dot(left, right[:, cols], TN)
        put_slabs(where_ref, part, keep_ref, send_ref, first, count, cols)


def slab_call(kernel, name, where, grid, in_specs, args, r, width, scratch, us, block):
    slabs = pl.BlockSpec((CHUNKS, r, block), lambda i, s: (0, 0, i))
    return pl.pallas_call(
        kernel,
        grid_spec=pltpu.PrefetchScalarGridSpec(
            num_scalar_prefetch=1,
            grid=grid,
            in_specs=in_specs,
            out_specs=[slabs, slabs],
            scratch_shapes=scratch,
        ),
        out_shape=[shape_of((CHUNKS, r, width), bf16)] * 2,
        compiler_params=PARAMS,
        name=name,
        cost_estimate=lasts(us),
    )(where, *args)


def back_outer_kernel(where_ref, g_ref, df_ref, keep_out, send_out, val_ref, keep_ref, send_ref, sems):
    step = pl.program_id(0)

    def leaving(chunk):
        keep, send = where_ref[1 + chunk], where_ref[1 + CHUNKS + chunk]
        return (
            pltpu.make_async_copy(keep_ref.at[keep], keep_out.at[keep], sems.at[0, chunk]),
            pltpu.make_async_copy(send_ref.at[send], send_out.at[send], sems.at[1, chunk]),
        )

    outer_slabs(where_ref, g_ref[...], df_ref[...], val_ref, keep_ref, send_ref, step * 4, 4)
    for i in range(4):
        for copy in leaving(step * 4 + i):
            copy.start()

    @pl.when(step == 3)
    def _():
        for i in range(CHUNKS):
            for copy in leaving(i):
                copy.wait()


def back_outer(where, g, df):
    n, ff = g.shape
    d = df.shape[1]
    slabs = (CHUNKS, ff // 32, d)
    return pl.pallas_call(
        back_outer_kernel,
        grid_spec=pltpu.PrefetchScalarGridSpec(
            num_scalar_prefetch=1,
            grid=(4,),
            in_specs=[
                pl.BlockSpec((n, d), lambda i, s: (0, i)), pl.BlockSpec((n, d), lambda i, s: (0, 0)),
            ],
            out_specs=[pl.BlockSpec(memory_space=pl.ANY)] * 2,
            scratch_shapes=[
                pltpu.VMEM((d, d), f32), pltpu.VMEM(slabs, bf16), pltpu.VMEM(slabs, bf16),
                pltpu.SemaphoreType.DMA((2, CHUNKS)),
            ],
        ),
        out_shape=[shape_of(slabs, bf16)] * 2,
        compiler_params=PARAMS,
        name="back_outer",
        cost_estimate=lasts(11),
    )(where, g, df)


def put_sums(sums1_ref, sums2_ref, bsum_ref, val_ref):
    d = sums1_ref.shape[1]
    r = d // 32
    rows = [sums1_ref[...], sums2_ref[...], jnp.zeros((112, d), f32)]
    val_ref[:, :128] = jnp.concatenate(rows, 0).T
    lane = lax.broadcasted_iota(jnp.int32, (1, 128), 1)
    mine = (lane >= 16) & (lane < 16 + 4 * r)
    for i in range(32):
        row = bsum_ref[i // 8 : i // 8 + 1, :]
        part = pltpu.roll(row, (16 - i % 8 * 4 * r) % d, 1)[:, :128]
        val_ref[i * r : i * r + 1, :128] += jnp.where(mine, part, 0.0)


def mid_outer_kernel(
    where_ref, h_ref, du_ref, o_ref, da_ref, sums1_ref, sums2_ref, bsum_ref,
    keep_ref, send_ref, val_ref,
):
    step = pl.program_id(0)

    @pl.when(step < 4)
    def _():
        outer_slabs(where_ref, h_ref[...], du_ref[...], val_ref, keep_ref, send_ref, 0, CHUNKS)

    @pl.when(step == 4)
    def _():
        outer_slabs(where_ref, o_ref[...], da_ref[...], val_ref, keep_ref, send_ref, 0, CHUNKS)

    @pl.when(step == 5)
    def _():
        put_sums(sums1_ref, sums2_ref, bsum_ref, val_ref)
        put_slabs(where_ref, val_ref.at[:, :128], keep_ref, send_ref, 0, CHUNKS, slice(0, 128))


def mid_outer(where, h, du, o, da, sums1, sums2, bsum):
    n, d = h.shape
    keep = lambda a: pl.BlockSpec(a.shape, lambda i, s: (0, 0))
    block = pl.BlockSpec((n, d), lambda i, s: (0, jnp.minimum(i, 3)))
    specs = [keep(h), block, keep(o), keep(da), keep(sums1), keep(sums2), keep(bsum)]
    return slab_call(
        mid_outer_kernel, "mid_outer", where, (6,), specs, (h, du, o, da, sums1, sums2, bsum), d // 32,
        5 * d + 128, [pltpu.VMEM((d, d), f32)], 14, d,
    )


def qkv_outer_kernel(where_ref, x_ref, *refs):
    grad_refs, (keep_ref, send_ref, val_ref, sums_ref) = refs[:-4], refs[-4:]
    step = pl.program_id(0)

    @pl.when(step == 0)
    def _():
        sums_ref[...] = jnp.zeros_like(sums_ref)

    @pl.when(step < 3)
    def _():
        at = 0
        for ref in grad_refs:
            grads = ref[0]
            cols = slice(at, at + ref.shape[2])
            at += ref.shape[2]
            part = val_ref.at[:, cols]
            part[...] = dot(x_ref[...], grads, TN)
            put_slabs(where_ref, part, keep_ref, send_ref, 0, CHUNKS, cols)
            total = jnp.sum(grads.astype(f32), axis=0, keepdims=True)
            sums_ref[pl.ds(step, 1), cols] = total

    @pl.when(step == 3)
    def _():
        val_ref[:, :128] = sums_ref[...].T
        put_slabs(where_ref, val_ref.at[:, :128], keep_ref, send_ref, 0, CHUNKS, slice(0, 128))


def qkv_outer(where, x, grads):
    n, d = x.shape
    block = lambda a: pl.BlockSpec((1, n, a.shape[2]), lambda i, s: (jnp.minimum(i, 2), 0, 0))
    specs = [pl.BlockSpec((n, d), lambda i, s: (0, 0))] + [block(a) for a in grads]
    return slab_call(
        qkv_outer_kernel, "qkv_outer", where, (4,), specs, (x, *grads), d // 32, 3 * d + 128,
        [pltpu.VMEM((d, d), f32), pltpu.VMEM((128, d), f32)], 10, d,
    )


def input_grad_kernel(dr_ref, *refs):
    grad_refs, (wq_ref, wk_ref, wv_ref, out_ref) = refs[:-4], refs[-4:]
    total = dr_ref[...]
    for i, w_ref in enumerate((wq_ref, wk_ref, wv_ref)):
        at = 0
        for ref in grad_refs:
            w = flat(w_ref[:, :, :, at : at + ref.shape[2]])
            at += ref.shape[2]
            total = total + dot(ref[i], w, NT)
    out_ref[...] = total


def input_grad(dr, grads, pack, rows=256):
    n, d = dr.shape
    weight = lambda j: pl.BlockSpec((CHUNKS, 3, 16, d), lambda i: (0, j, 0, 0))
    return pl.pallas_call(
        input_grad_kernel,
        grid=(n // rows,),
        in_specs=[pl.BlockSpec((rows, d), lambda i: (i, 0))]
        + [pl.BlockSpec((3, rows, a.shape[2]), lambda i: (0, i, 0)) for a in grads]
        + [weight(0), weight(1), weight(2)],
        out_specs=pl.BlockSpec((rows, d), lambda i: (i, 0)),
        out_shape=shape_of((n, d)),
        compiler_params=PARAMS,
        name="input_grad",
        cost_estimate=lasts(9),
    )(dr, *grads, pack, pack, pack)


def bit_of(axis, bit):
    return (lax.axis_index(axis) // bit) % 2


def swap(x, axis, bits):
    size = lax.axis_size(axis)
    return lax.ppermute(x, axis, [(i, i ^ bits) for i in range(size)])


def ordered(mine, own, other):
    return jnp.where(mine == 0, own, other), jnp.where(mine == 0, other, own)


def gather_bit(x, axis, bit):
    first, second = ordered(bit_of(axis, bit), x, swap(x, axis, bit))
    return jnp.stack([first, second], 1).reshape((2 * x.shape[0],) + x.shape[1:])


def gather_two_bits(x, axis, high, low):
    a, b, c, d = x, swap(x, axis, low), swap(x, axis, high), swap(x, axis, high | low)
    a, b = ordered(bit_of(axis, low), a, b)
    c, d = ordered(bit_of(axis, low), c, d)
    a, c = ordered(bit_of(axis, high), a, c)
    b, d = ordered(bit_of(axis, high), b, d)
    return jnp.stack([a, b, c, d], 1).reshape((4 * x.shape[0],) + x.shape[1:])


def upper_bits():
    count = lax.axis_size("dp").bit_length() - 1
    return [1 << i for i in range(count - 1, 0, -1)]


def gather(x):
    rows, cols = x.shape
    x = x[None]
    bits = upper_bits()
    if len(bits) == 2:
        x = gather_two_bits(x, "dp", *bits)
    else:
        for bit in bits:
            x = gather_bit(x, "dp", bit)
    k = x.shape[0]
    one = gather_bit(gather_bit(x[:, :, : cols // 2], "dp", 1), "fsdp", 2)
    two = gather_bit(gather_bit(x[:, :, cols // 2 :], "fsdp", 2), "dp", 1)
    two = jnp.swapaxes(two.reshape(k, 2, 2, rows, cols // 2), 1, 2).reshape(one.shape)
    x = jnp.concatenate([one, two], -1)
    return gather_bit(x, "fsdp", 1)


def scatter_bit(x, axis, bit, dim):
    mine = bit_of(axis, bit)
    keep = lax.dynamic_index_in_dim(x, mine, dim, keepdims=False)
    send = lax.dynamic_index_in_dim(x, 1 - mine, dim, keepdims=False)
    return (keep.astype(f32) + swap(send, axis, bit).astype(f32)).astype(x.dtype)


def scatter_two_bits(x, axis, high, low):
    mine = bit_of(axis, high) * 2 + bit_of(axis, low)
    part = lambda i: lax.dynamic_index_in_dim(x, mine ^ i, 0, keepdims=False)
    total = part(0).astype(f32)
    for i, bits in ((1, low), (2, high), (3, high | low)):
        total = total + swap(part(i), axis, bits).astype(f32)
    return total


def scatter_sum(x):
    devices, rows, cols = x.shape
    bits = upper_bits()
    x = scatter_bit(x.reshape(devices // 8, 2, 2, 2, rows, cols), "fsdp", 1, 3)
    one = scatter_bit(scatter_bit(x[..., : cols // 2], "fsdp", 2, 2), "dp", 1, 1)
    two = scatter_bit(scatter_bit(x[..., cols // 2 :], "dp", 1, 1), "fsdp", 2, 1)
    x = jnp.concatenate([one, two], -1)
    if len(bits) == 2:
        return scatter_two_bits(x, "dp", *bits)
    x = x.reshape((2,) * len(bits) + (rows, cols))
    for bit in bits:
        x = scatter_bit(x, "dp", bit, 0)
    return x.astype(f32)


def seats():
    dp, fsdp = lax.axis_index("dp"), lax.axis_index("fsdp")
    return dp // 2, dp % 2, fsdp // 2, fsdp % 2


def swap_all(x, dz=0, first=0, second=0, core=0):
    pairs = []
    for i in range(32):
        z, y, xx, c = i // 8, i // 4 % 2, i // 2 % 2, i % 2
        dy, dx = (first, second) if c == 0 else (second, first)
        pairs.append((i, (((z ^ dz) * 2 + (y ^ dy)) * 2 + (xx ^ dx)) * 2 + (c ^ core)))
    return lax.ppermute(x, AXES, pairs)


def after(x, *others):
    return lax.optimization_barrier((x, *others))[0]


def halves_kernel(core_ref, wq_ref, wk_ref, wv_ref, wo_ref, wi_ref, wb_ref, own_ref, send_ref):
    r, d = wq_ref.shape
    for core, out in ((core_ref[0], own_ref), (1 - core_ref[0], send_ref)):
        half = lambda base: pl.ds(pl.multiple_of(base + core * (d // 2), 128), d // 2)
        for j in range(4):
            out[j] = wi_ref[:, half(j * d)]
        back = wb_ref[:, half(0)].astype(f32)
        for j in range(4):
            out[4 + j] = back[j * r : (j + 1) * r].astype(bf16)
        for j, ref in enumerate((wo_ref, wq_ref, wk_ref, wv_ref)):
            out[8 + j] = ref[:, half(0)]


def halves(core, *weights):
    r, d = weights[0].shape
    return pl.pallas_call(
        halves_kernel,
        in_specs=[pl.BlockSpec(memory_space=pltpu.SMEM)]
        + [pl.BlockSpec(memory_space=pltpu.VMEM)] * 6,
        out_specs=[pl.BlockSpec(memory_space=pltpu.VMEM)] * 2,
        out_shape=[shape_of((12, r, d // 2), bf16)] * 2,
        compiler_params=PARAMS,
        name="halves",
        cost_estimate=lasts(2),
    )(core, *weights)


def chip_kernel(core_ref, own_ref, got_ref, *refs):
    small, (one_ref, two_ref, rows_ref) = refs[:-3], refs[-3:]
    swapped = core_ref[0] == 1

    def put(out_ref, tile, start, count):
        own = own_ref[start : start + count].astype(f32)
        got = got_ref[start : start + count].astype(f32)
        low, high = jnp.where(swapped, got, own), jnp.where(swapped, own, got)
        rows = jnp.concatenate([a[i] for a in (low, high) for i in range(count)], 0).astype(bf16)
        tiles = rows.shape[0] // 16
        out_ref[tile : tile + tiles] = rows.reshape(tiles, 16, rows.shape[1])

    for j in range(4):
        put(two_ref, 12 + 3 * j, j, 1)
    put(two_ref, 24, 8, 1)
    put(two_ref, 0, 4, 4)
    for j in range(3):
        put(one_ref, 3 * j, 9 + j, 1)
    rows_ref[...] = jnp.zeros_like(rows_ref)
    for i, ref in enumerate(small):
        rows_ref[i : i + 1, : ref.shape[1]] = ref[...].astype(f32)
    one_ref[9] = rows_ref[...].astype(bf16)


def chip_shards(core, own, got, small):
    width = own.shape[2]
    return pl.pallas_call(
        chip_kernel,
        in_specs=[pl.BlockSpec(memory_space=pltpu.SMEM)]
        + [pl.BlockSpec(memory_space=pltpu.VMEM)] * (2 + len(small)),
        out_specs=[pl.BlockSpec(memory_space=pltpu.VMEM)] * 2,
        out_shape=[shape_of((tiles, 16, width), bf16) for tiles in (10, 27)],
        scratch_shapes=[pltpu.VMEM((16, width), f32)],
        compiler_params=PARAMS,
        name="chip_shards",
        cost_estimate=lasts(2),
    )(core, own, got, *[a[None] for a in small])


def pair_up(x, dz, *late):
    return jnp.concatenate([x, after(swap_all(x, dz=dz), *late)])


def near_pieces(stack):
    return [stack, swap_all(stack, first=1), swap_all(stack, second=1)]


class Scatter:
    def __init__(self, small_slice, keep, send, direct=False):
        self.state = (keep, send)
        self.small_slice = small_slice
        self.steps = 0
        self.total = None
        self.direct = direct

    def hold(self, *late):
        self.state = tuple(after(part, *late) for part in self.state)

    def step(self, *late):
        if not self.small_slice:
            return ()
        self.steps += 1
        hops = [{"core": 1}, {"second": 1}, {"first": 1}]
        if not self.direct:
            hops += [{"dz": 1}, {"dz": 2}]
        if self.steps <= len(hops):
            keep, send = self.state
            got = after(swap_all(send, **hops[self.steps - 1]), *late)
            total = keep.astype(f32) + got.astype(f32)
            if self.steps == 5:
                self.total = total[0]
                return (self.total,)
            total = total.astype(bf16)
            half = total.shape[0] // 2
            self.state = (total,) if self.direct and self.steps == 3 else (total[:half], total[half:])
            return self.state
        (parts,) = self.state
        total = parts[0].astype(f32)
        for i, dz in ((1, 2), (2, 1), (3, 3)):
            total = total + after(swap_all(parts[i], dz=dz), *late).astype(f32)
        self.total = total
        return (total,)

    def result(self, devices):
        if self.small_slice:
            while self.total is None:
                self.step()
            return self.total
        keep, send = self.state
        stacked = jnp.stack([keep, send], 1)
        return scatter_sum(stacked.reshape(devices, -1, keep.shape[-1]))


def places(lengths, n):
    ends = jnp.cumsum(lengths)
    start = jnp.sum(jnp.where(lengths == n // 2, ends - n // 2, 0))
    position = (start + n // 2 + jnp.arange(n // 2, dtype=jnp.int32)) % n
    segment = jnp.sum((position[:, None] >= ends[None, :]).astype(jnp.int32), axis=1)
    return start, segment.astype(f32)


def vectors(small, r, d):
    vec = jnp.transpose(small[:, : 8 * r].reshape(-1, 8, r), (1, 0, 2)).reshape(8, d)
    return vec, small[:, 8 * r : 12 * r].reshape(4, d)


def body(
    tokens, lengths, cotangent, w_query, w_key, w_value, w_out, b_query, b_value, b_out,
    norm1_gain, norm1_shift, w_in, w_back, b_in, b_back, norm2_gain, norm2_shift,
):
    _, n, d = tokens.shape
    devices = lax.axis_size("dp") * lax.axis_size("fsdp")
    r = w_query.shape[0]
    small_slice = lax.axis_size("dp") == 8 and lax.axis_size("fsdp") == 4
    start, segment = places(lengths[0], n)
    seg_row, seg_col = segment[None, :], segment[:, None]
    rolled = lambda a: jnp.roll(a[0], -start, axis=0)
    small = [b_query, b_value, b_out, norm1_gain, norm1_shift, b_back, norm2_gain, norm2_shift, b_in]
    if small_slice:
        z, y, across, core = seats()
        i = jnp.arange(32, dtype=jnp.int32)
        first, second = i // 4 % 2, i // 8 % 2
        other = (core + i // 16) % 2
        chip = ((z ^ (i % 2 * 2 + i // 2 % 2)) * 2 + (y ^ jnp.where(other == 0, first, second))) * 2
        chip = chip + (across ^ jnp.where(other == 0, second, first))
        gather_at = jnp.concatenate([core[None], chip])
        i = jnp.arange(16, dtype=jnp.int32)
        dz, dy_, dx = z ^ i // 4, y ^ i // 2 % 2, across ^ i % 2
        dz = dz % 2 * 2 + dz // 2
        slot = lambda c: jnp.where(c == 0, dx, dy_) * 8 + jnp.where(c == 0, dy_, dx) * 4 + dz
        where = jnp.concatenate([core[None], slot(core), slot(1 - core)])
        own, send = halves(core[None], w_query, w_key, w_value, w_out, w_in, w_back)
        one, two = chip_shards(core[None], own, swap_all(send, core=1), small)
        x = rolled(after(tokens, one))
        hop2 = swap_all(two, first=1)
        pair1 = pair_up(one[None], 2, x, gather_at, where, hop2)
        diag2 = swap_all(hop2, second=1)
        dy = rolled(after(cotangent, pair1))
        pair2 = pair_up(after(two, pair1)[None], 2)
        stack1 = pair_up(pair1, 1, dy, diag2)
        first1 = jnp.concatenate([stack1, after(swap_all(stack1, first=1), pair2)])
        stack2 = pair_up(pair2, 1, first1)
        pieces1 = [first1, swap_all(first1, second=1)]
        near2 = near_pieces(after(stack2, first1))
        far2 = [swap_all(after(diag2, stack2), dz=dz)[None] for dz in (2, 1, 3)]
        early2 = [swap_all(near2[0], core=1), swap_all(diag2, core=1)[None]]
        pieces1 += [swap_all(piece, core=1) for piece in pieces1]
        x = after(x, *early2)
    else:
        x, dy = rolled(tokens), rolled(cotangent)
        step = jnp.arange(16, dtype=jnp.int32)
        where = jnp.concatenate([jnp.zeros((1,), jnp.int32), step, step])
        gather_at = where
        small = jnp.concatenate(small)
        small = jnp.pad(small, (0, 8 * d - small.shape[0])).reshape(8, d)
        pack1 = gather(jnp.concatenate([w_query, w_key, w_value, small]))
        vec, bi = vectors(pack1[:, 3 * r], r, d)
        rows = jnp.pad(vec.reshape(8, 16, 2, -1), ((0, 0), (0, 0), (0, 0), (0, d // 2 - d // 32)))
        row = jnp.pad(bi.reshape(1, 16, 2, -1), ((0, 7), (0, 0), (0, 0), (0, d // 2 - d // 8)))
        small = jnp.transpose(jnp.concatenate([rows, row]), (1, 0, 2, 3)).reshape(16, 1, 16, d)
        tiles = lambda w: w.reshape(CHUNKS, -1, 16, d)
        pack1 = [tiles(pack1[:, i * r : (i + 1) * r]) for i in range(3)] + [small]
        pack2 = gather(jnp.concatenate([w_in[:, j * d : (j + 1) * d] for j in range(4)] + [w_back, w_out]))
        cuts = [(4, 8), (0, 1), (1, 2), (2, 3), (3, 4), (8, 9)]
        pack2 = [tiles(pack2[:, a * r : b * r]) for a, b in cuts]
        cut = lambda p: [
            jnp.concatenate(p, 1)[4 * i : 4 * i + 4, :, :, j * (d // 2) : (j + 1) * (d // 2)]
            for j in range(2)
            for i in range(4)
        ]
        pieces1, pieces2 = cut(pack1), cut(pack2)

    q, k, v, o, lse, vec, bi, pack1 = attend(gather_at, x, seg_row, seg_col, pieces1)
    if small_slice:
        late2 = lax.optimization_barrier((*near2[1:], *far2, o))[:-1]
        swapped = [swap_all(a, core=1) for a in late2]
        pieces2 = [near2[0], *late2[:2], diag2[None], *late2[2:]]
        pieces2 += [early2[0], *swapped[:2], early2[1], *swapped[2:]]
    mixed, h, zhat, inv, g, slope, dr, df, sums2, pack2 = forward(
        gather_at, x, o, dy, vec, bi, pieces2
    )
    scatter1 = Scatter(small_slice, *back_outer(where, g, df))
    du, dr1, da, do, sums1, bsum = backward(
        after(df, *scatter1.state), slope, dr, zhat, inv, pack2, vec
    )
    h_late = after(h, du, *scatter1.step(du))
    scatter2 = Scatter(small_slice, *mid_outer(where, h_late, du, o, da, sums1, sums2, bsum))
    late = after(q, *scatter1.step(*scatter2.state))
    scatter2.hold(late)
    grads = [attend_back(late, k, v, do, lse, seg_row, seg_col, 0, 1)]
    late = after(q, *scatter1.step(grads[0]), *scatter2.step(grads[0]))
    grads.append(attend_back(late, k, v, do, lse, seg_row, seg_col, 1, 2))
    late = after(x, *scatter2.step(grads[1]))
    scatter3 = Scatter(small_slice, *qkv_outer(where, late, grads), True)
    late = scatter2.step(*scatter3.state) + scatter1.step(*scatter3.state)
    late = late + scatter3.step(*late)
    grad_tokens = input_grad(after(dr1, *late), grads, pack1)
    late = scatter3.step(grad_tokens) + scatter2.step(grad_tokens) + scatter1.step(grad_tokens)
    unroll = lambda a, *late: jnp.roll(after(a, *late), start, axis=0)[None]
    mixed, grad_tokens = unroll(mixed, *late), unroll(grad_tokens, *late)
    scatter3.step(mixed, grad_tokens)
    scatter2.step(mixed, grad_tokens)
    mid_grad = scatter2.result(devices)
    back_grad = scatter1.result(devices)
    rest = scatter3.result(devices)
    gq, gk, gv = [rest[:, i * d : (i + 1) * d] for i in range(3)]
    gbq, _, gbv = rest[:, 3 * d : 3 * d + 3].T
    in_grad, out_grad = mid_grad[:, : 4 * d], mid_grad[:, 4 * d : 5 * d]
    vecs = mid_grad[:, 5 * d : 5 * d + 11].T
    if small_slice:
        gbi = mid_grad[0, 5 * d + 16 : 5 * d + 16 + 4 * r]
    else:
        gbi = lax.psum_scatter(bsum.reshape(4 * d), AXES, scatter_dimension=0, tiled=True)
    return (
        mixed, grad_tokens, gq, gk, gv, out_grad,
        gbq, gbv, vecs[0], vecs[1], vecs[2],
        in_grad, back_grad, gbi, vecs[8], vecs[9], vecs[10],
    )


def solution(mesh):
    act, mat, vec = P(AXES, None, None), P(AXES, None), P(AXES)
    return jax.shard_map(
        body,
        mesh=mesh,
        in_specs=(act, mat, act, mat, mat, mat, mat, vec, vec, vec, vec, vec, mat, mat, vec, vec, vec, vec),
        out_specs=(act, act, mat, mat, mat, mat, vec, vec, vec, vec, vec, mat, mat, vec, vec, vec, vec),
        check_vma=False,
    )
```

```python
import functools

import jax
import jax.numpy as jnp
from jax import lax
from jax.experimental import pallas as pl
from jax.experimental.pallas import tpu as pltpu
from jax.sharding import PartitionSpec as P

HEAD_DIM = 64
MASKED = -1e30
AXES = ("dp", "fsdp")
CHUNKS = 16
f32 = jnp.float32
bf16 = jnp.bfloat16
NN = (((1,), (0,)), ((), ()))
NT = (((1,), (1,)), ((), ()))
TN = (((0,), (0,)), ((), ()))


def room(mib):
    return pltpu.CompilerParams(vmem_limit_bytes=mib << 20)


PARAMS = room(56)


def dot(left, right, dims=NN):
    return lax.dot_general(left, right, dims, preferred_element_type=f32)


def shape_of(shape, dtype=f32):
    return jax.ShapeDtypeStruct(shape, dtype)


def lasts(us):
    return pl.CostEstimate(flops=int(us * 1.1e9), bytes_accessed=0, transcendentals=0)


def whole(array):
    return pl.BlockSpec(array.shape, lambda i: (0,) * array.ndim)


def flat(weight):
    return weight.reshape(-1, weight.shape[-1])


def put_pieces(where_ref, pieces, pack_ref):
    width = pieces[0].shape[-1]
    at = 1
    for i, piece in enumerate(pieces):
        half = where_ref[0] if i < len(pieces) // 2 else 1 - where_ref[0]
        cols = pl.ds(pl.multiple_of(half * width, 128), width)
        for j in range(piece.shape[0]):
            pack_ref[where_ref[at], :, :, cols] = piece[j]
            at += 1


def once(array):
    rank = array.ndim
    return pl.BlockSpec(array.shape, lambda i, s: (0,) * rank, pipeline_mode=pl.Buffered(1))


def spread(small_ref, vec_ref, bias_ref):
    d = vec_ref.shape[1]
    r = d // 32
    vec = jnp.zeros((16, d), f32)
    bias = [jnp.zeros((1, d), f32) for _ in range(4)]
    for i in range(32):
        half = slice(i % 2 * (d // 2), (i % 2 + 1) * (d // 2))
        mine = small_ref[i // 2, small_ref.shape[1] - 1, :, half].astype(f32)
        mine = jnp.concatenate([mine, jnp.zeros_like(mine)], 1)
        vec = vec + (pltpu.roll(mine, i * r, 1) if i else mine)
        shift = i % 8 * 4 * r
        row = mine[8:9]
        bias[i // 8] = bias[i // 8] + (pltpu.roll(row, shift, 1) if shift else row)
    vec_ref[...] = vec[:8]
    bias_ref[...] = jnp.concatenate(bias, 0)


def second_specs(d):
    at = lambda tiles, j: pl.BlockSpec((CHUNKS, tiles, 16, d), lambda i: (0, j, 0, 0))
    return [at(3, 8), at(12, 1), at(12, 0)]


def attend_kernel(
    where_ref, x_ref, seg_row_ref, seg_col_ref, *refs
):
    pieces = refs[:-11]
    q_ref, k_ref, v_ref, o_ref, lse_ref, vec_ref, bi_ref, out_ref, pack_ref, bias_ref, sem = refs[-11:]
    half = x_ref.shape[0] // 2
    width = q_ref.shape[1]
    step = pl.program_id(0)
    keep_pack = pltpu.make_async_copy(pack_ref, out_ref, sem)

    @pl.when(step == 0)
    def _():
        bias_ref[...] = jnp.where(seg_col_ref[...] == seg_row_ref[...], 0.0, MASKED)
        put_pieces(where_ref, pieces, pack_ref)
        keep_pack.start()
        spread(pack_ref, vec_ref, bi_ref)

    x = x_ref[...]
    group = pl.ds(pl.multiple_of(step * width, 128), width)
    weight = lambda j: flat(pack_ref[:, 3 * j : 3 * j + 3, :, group])
    query = (dot(x, weight(0)) + vec_ref[0:1, group]).astype(bf16)
    q_ref[...] = query * jnp.asarray(HEAD_DIM**-0.5, bf16)
    k_ref[...] = dot(x, weight(1)).astype(bf16)
    v_ref[...] = (dot(x, weight(2)) + vec_ref[1:2, group]).astype(bf16)
    for part in range(2):
        rows = slice(part * half, (part + 1) * half)
        for pair in range(width // 128):
            cols = slice(pair * 128, (pair + 1) * 128)
            keys = k_ref[rows, cols]
            values_t = v_ref[rows, cols].T
            queries = q_ref[rows, cols]
            lane = lax.broadcasted_iota(jnp.int32, queries.shape, 1)
            outs = []
            for h in range(2):
                mine = (lane < HEAD_DIM) if h == 0 else (lane >= HEAD_DIM)
                scores = dot(keys, jnp.where(mine, queries, jnp.zeros_like(queries)), NT)
                if part == 1:
                    scores = scores + bias_ref[...]
                top = jnp.max(scores, axis=0, keepdims=True)
                terms = jnp.exp(scores - top)
                total = jnp.sum(terms, axis=0, keepdims=True)
                mixed = dot(values_t[h * HEAD_DIM : (h + 1) * HEAD_DIM, :], terms.astype(bf16))
                outs.append(mixed / total)
                lse_ref[0, pair * 2 + h : pair * 2 + h + 1, rows] = top + jnp.log(total)
            o_ref[rows, cols] = jnp.concatenate(outs, 0).T.astype(bf16)

    @pl.when(step == pl.num_programs(0) - 1)
    def _():
        keep_pack.wait()


def attend(where, x, seg_row, seg_col, pieces, width=256):
    n, d = x.shape
    groups = d // width
    tiles = pieces[0].shape[1]
    act = pl.BlockSpec((n, width), lambda i, s: (0, i))
    heads = width // HEAD_DIM
    still = lambda rows: pl.BlockSpec((rows, d), lambda i, s: (0, 0))
    return pl.pallas_call(
        attend_kernel,
        grid_spec=pltpu.PrefetchScalarGridSpec(
            num_scalar_prefetch=1,
            grid=(groups,),
            in_specs=[once(a) for a in (x, seg_row, seg_col, *pieces)],
            out_specs=[
                act, act, act, act, pl.BlockSpec((1, heads, n), lambda i, s: (i, 0, 0)),
                still(8), still(4), pl.BlockSpec(memory_space=pl.ANY),
            ],
            scratch_shapes=[
                pltpu.VMEM((CHUNKS, tiles, 16, d), bf16),
                pltpu.VMEM((n // 2, n // 2), f32),
                pltpu.SemaphoreType.DMA,
            ],
        ),
        out_shape=[shape_of((n, d), bf16)] * 4
        + [shape_of((groups, heads, n)), shape_of((8, d)), shape_of((4, d))]
        + [shape_of((CHUNKS, tiles, 16, d), bf16)],
        compiler_params=PARAMS,
        name="attend",
        cost_estimate=lasts(0),
    )(where, x, seg_row, seg_col, *pieces)


def attend_back_kernel(
    q_ref, k_ref, v_ref, do_ref, lse_ref, seg_row_ref, seg_col_ref, grads_ref, bias_ref
):
    n, width = q_ref.shape
    half = n // 2

    @pl.when(pl.program_id(0) == 0)
    def _():
        bias_ref[...] = jnp.where(seg_col_ref[...] == seg_row_ref[...], 0.0, MASKED)

    for part in range(2):
        rows = slice(part * half, (part + 1) * half)
        for pair in range(width // 128):
            cols = slice(pair * 128, (pair + 1) * 128)
            keys, values = k_ref[rows, cols], v_ref[rows, cols]
            queries, grads = q_ref[rows, cols], do_ref[rows, cols]
            keys_t = keys.T
            lane = lax.broadcasted_iota(jnp.int32, queries.shape, 1)
            dqs = []
            dk = dv = None
            for h in range(2):
                mine = (lane < HEAD_DIM) if h == 0 else (lane >= HEAD_DIM)
                query = jnp.where(mine, queries, jnp.zeros_like(queries))
                grad = jnp.where(mine, grads, jnp.zeros_like(grads))
                scores = dot(keys, query, NT)
                if part == 1:
                    scores = scores + bias_ref[...]
                prob = jnp.exp(scores - lse_ref[0, pair * 2 + h : pair * 2 + h + 1, rows])
                prob_grad = dot(values, grad, NT)
                delta = jnp.sum(prob * prob_grad, axis=0, keepdims=True)
                score_grad = (prob * (prob_grad - delta)).astype(bf16)
                dv_h = dot(prob.astype(bf16), grad)
                dk_h = dot(score_grad, query)
                dv = dv_h if h == 0 else dv + dv_h
                dk = dk_h if h == 0 else dk + dk_h
                dqs.append(dot(keys_t[h * HEAD_DIM : (h + 1) * HEAD_DIM, :], score_grad))
            dq = jnp.concatenate(dqs, 0).T * HEAD_DIM**-0.5
            grads_ref[0, rows, cols] = dq.astype(bf16)
            grads_ref[1, rows, cols] = dk.astype(bf16)
            grads_ref[2, rows, cols] = dv.astype(bf16)


def attend_back(q, k, v, do, lse, seg_row, seg_col, group, count, width=256):
    n, d = q.shape
    act = pl.BlockSpec((n, width), lambda i: (0, group + i))
    heads = width // HEAD_DIM
    return pl.pallas_call(
        attend_back_kernel,
        grid=(count,),
        in_specs=[
            act, act, act, act, pl.BlockSpec((1, heads, n), lambda i: (group + i, 0, 0)),
            whole(seg_row), whole(seg_col),
        ],
        out_specs=pl.BlockSpec((3, n, width), lambda i: (0, 0, i)),
        out_shape=shape_of((3, n, count * width), bf16),
        scratch_shapes=[pltpu.VMEM((n // 2, n // 2), f32)],
        compiler_params=room(50),
        name="attend_back",
        cost_estimate=lasts(9 * count),
    )(q, k, v, do, lse, seg_row, seg_col)


def gelu_and_slope(u):
    size = jnp.abs(u)
    t = 1.0 / (1.0 + (0.3275911 * 0.7071067811865476) * size)
    bell = jnp.exp(-0.5 * u * u)
    series = t * (
        0.127414796
        + t * (-0.142248368 + t * (0.7107068705 + t * (-0.7265760135 + t * 0.5307027145)))
    )
    tail = series * bell
    cdf = jnp.where(u >= 0, 1.0 - tail, tail)
    return u * cdf, cdf + u * (bell * 0.3989422804014327)


def normed(value):
    centre = value - jnp.mean(value, axis=-1, keepdims=True)
    inv = lax.rsqrt(jnp.mean(centre * centre, axis=-1, keepdims=True) + 1e-6)
    return centre * inv, inv


def normed_back(e, z, inv):
    mean_e = jnp.mean(e, axis=-1, keepdims=True)
    mean_ez = jnp.mean(e * z, axis=-1, keepdims=True)
    return (e - mean_e - z * mean_ez) * inv


def forward_kernel(where_ref, x_ref, o_ref, dy_ref, vec_ref, bi_ref, *refs):
    pieces = refs[:-12]
    mixed_ref, h_ref, z_ref, inv_ref, g_ref, slope_ref, dr_ref, df_ref, sums_ref = refs[-12:-3]
    out_ref, pack_ref, sem = refs[-3:]
    step = pl.program_id(0)
    keep_pack = pltpu.make_async_copy(pack_ref, out_ref, sem)

    @pl.when(step == 0)
    def _():
        put_pieces(where_ref, pieces, pack_ref)
        keep_pack.start()
        sums_ref[...] = jnp.zeros_like(sums_ref)

    b_out, gain1, shift1, b_back, gain2, shift2 = [vec_ref[i : i + 1, :] for i in range(2, 8)]
    r1 = x_ref[...].astype(f32) + dot(o_ref[...], flat(pack_ref[:, 24:27])) + b_out
    z1, inv1 = normed(r1)
    z_ref[...] = z1
    inv_ref[...] = inv1
    h1 = z1 * gain1 + shift1
    low = h1.astype(bf16)
    h_ref[...] = low
    r2 = h1 + b_back
    d = low.shape[1]
    for j in range(4):
        cols = slice(j * d, (j + 1) * d)
        wi = flat(pack_ref[:, 12 + 3 * j : 15 + 3 * j])
        g, slope = gelu_and_slope(dot(low, wi) + bi_ref[j : j + 1, :])
        g_low = g.astype(bf16)
        g_ref[:, cols] = g_low
        slope_ref[:, cols] = slope.astype(bf16)
        r2 = r2 + dot(g_low, flat(pack_ref[4 * j : 4 * j + 4, :12]))
    z2, inv2 = normed(r2)
    mixed_ref[...] = (z2 * gain2 + shift2).astype(bf16)
    dy = dy_ref[...].astype(f32)
    dr = normed_back(dy * gain2, z2, inv2)
    dr_ref[...] = dr
    df = dr.astype(bf16)
    df_ref[...] = df

    for i, term in enumerate((df.astype(f32), dy * z2, dy)):
        sums_ref[i : i + 1, :] += jnp.sum(term, axis=0, keepdims=True)

    @pl.when(step == pl.num_programs(0) - 1)
    def _():
        keep_pack.wait()


def forward(where, x, o, dy, vec, bi, pieces, rows=256):
    n, d = x.shape
    ff = 4 * d
    tiles = pieces[0].shape[1]
    tok = lambda w: pl.BlockSpec((rows, w), lambda i, s: (i, 0))
    return pl.pallas_call(
        forward_kernel,
        grid_spec=pltpu.PrefetchScalarGridSpec(
            num_scalar_prefetch=1,
            grid=(n // rows,),
            in_specs=[tok(d), tok(d), tok(d)] + [once(a) for a in (vec, bi, *pieces)],
            out_specs=[
                tok(d), tok(d), tok(d), tok(1), tok(ff), tok(ff), tok(d), tok(d),
                pl.BlockSpec((8, d), lambda i, s: (0, 0)), pl.BlockSpec(memory_space=pl.ANY),
            ],
            scratch_shapes=[
                pltpu.VMEM((CHUNKS, tiles, 16, d), bf16), pltpu.SemaphoreType.DMA,
            ],
        ),
        out_shape=[
            shape_of((n, d), bf16), shape_of((n, d), bf16), shape_of((n, d)), shape_of((n, 1)),
            shape_of((n, ff), bf16), shape_of((n, ff), bf16), shape_of((n, d)),
            shape_of((n, d), bf16), shape_of((8, d)), shape_of((CHUNKS, tiles, 16, d), bf16),
        ],
        compiler_params=PARAMS,
        name="forward",
        cost_estimate=lasts(30),
    )(where, x, o, dy, vec, bi, *pieces)


def backward_kernel(
    df_ref, slope_ref, dr_ref, z_ref, inv_ref, wo_ref, wi_ref, wb_ref, vec_ref,
    du_ref, dr1_ref, da_ref, do_ref, sums_ref, bsum_ref,
):
    @pl.when(pl.program_id(0) == 0)
    def _():
        sums_ref[...] = jnp.zeros_like(sums_ref)
        bsum_ref[...] = jnp.zeros_like(bsum_ref)

    df = df_ref[...]
    dh = dr_ref[...]
    d = df.shape[1]
    for j in range(4):
        cols = slice(j * d, (j + 1) * d)
        wi, wb = flat(wi_ref[:, 3 * j : 3 * j + 3]), flat(wb_ref[4 * j : 4 * j + 4])
        du = (dot(df, wb, NT) * slope_ref[:, cols].astype(f32)).astype(bf16)
        du_ref[:, cols] = du
        bsum_ref[j : j + 1, :] += jnp.sum(du.astype(f32), axis=0, keepdims=True)
        dh = dh + dot(du, wi, NT)
    z1 = z_ref[...]
    dr1 = normed_back(dh * vec_ref[3:4, :], z1, inv_ref[...])
    dr1_ref[...] = dr1
    da = dr1.astype(bf16)
    da_ref[...] = da
    do_ref[...] = dot(da, flat(wo_ref[...]), NT).astype(bf16)
    for i, term in enumerate((da.astype(f32), dh * z1, dh)):
        sums_ref[i : i + 1, :] += jnp.sum(term, axis=0, keepdims=True)


def backward(df, slope, dr, z, inv, pack, vec, rows=256):
    n, d = df.shape
    ff = 4 * d
    tok = lambda w: pl.BlockSpec((rows, w), lambda i: (i, 0))
    return pl.pallas_call(
        backward_kernel,
        grid=(n // rows,),
        in_specs=[tok(d), tok(ff), tok(d), tok(d), tok(1)] + second_specs(d) + [whole(vec)],
        out_specs=[
            tok(ff), tok(d), tok(d), tok(d),
            pl.BlockSpec((8, d), lambda i: (0, 0)), pl.BlockSpec((4, d), lambda i: (0, 0)),
        ],
        out_shape=[
            shape_of((n, ff), bf16), shape_of((n, d)), shape_of((n, d), bf16),
            shape_of((n, d), bf16), shape_of((8, d)), shape_of((4, d)),
        ],
        compiler_params=PARAMS,
        name="backward",
        cost_estimate=lasts(20),
    )(df, slope, dr, z, inv, pack, pack, pack, vec)


def put_slabs(where_ref, val_ref, keep_ref, send_ref, first, count, cols):
    r = keep_ref.shape[1]
    core = where_ref[0]
    for i in range(count):
        low = pl.multiple_of(2 * i * r + core * r, 8)
        high = pl.multiple_of(2 * i * r + (1 - core) * r, 8)
        keep_ref[where_ref[1 + first + i], :, cols] = val_ref[pl.ds(low, r), :].astype(bf16)
        send_ref[where_ref[1 + CHUNKS + first + i], :, cols] = val_ref[pl.ds(high, r), :].astype(bf16)


def outer_slabs(where_ref, left, right, val_ref, keep_ref, send_ref, first, count):
    width = right.shape[1]
    for cols in (slice(0, width * 2 // 3), slice(width * 2 // 3, width)):
        part = val_ref.at[:, cols]
        part[...] = dot(left, right[:, cols], TN)
        put_slabs(where_ref, part, keep_ref, send_ref, first, count, cols)


def slab_call(kernel, name, where, grid, in_specs, args, r, width, scratch, us, block):
    slabs = pl.BlockSpec((CHUNKS, r, block), lambda i, s: (0, 0, i))
    return pl.pallas_call(
        kernel,
        grid_spec=pltpu.PrefetchScalarGridSpec(
            num_scalar_prefetch=1,
            grid=grid,
            in_specs=in_specs,
            out_specs=[slabs, slabs],
            scratch_shapes=scratch,
        ),
        out_shape=[shape_of((CHUNKS, r, width), bf16)] * 2,
        compiler_params=room(36 if name == "qkv_outer" else 56),
        name=name,
        cost_estimate=lasts(us),
    )(where, *args)


def back_outer_kernel(where_ref, g_ref, df_ref, keep_out, send_out, val_ref, keep_ref, send_ref, sems):
    step = pl.program_id(0)

    def leaving(chunk):
        keep, send = where_ref[1 + chunk], where_ref[1 + CHUNKS + chunk]
        return (
            pltpu.make_async_copy(keep_ref.at[keep], keep_out.at[keep], sems.at[0, chunk]),
            pltpu.make_async_copy(send_ref.at[send], send_out.at[send], sems.at[1, chunk]),
        )

    outer_slabs(where_ref, g_ref[...], df_ref[...], val_ref, keep_ref, send_ref, step * 4, 4)
    for i in range(4):
        for copy in leaving(step * 4 + i):
            copy.start()

    @pl.when(step == 3)
    def _():
        for i in range(CHUNKS):
            for copy in leaving(i):
                copy.wait()


def back_outer(where, g, df):
    n, ff = g.shape
    d = df.shape[1]
    slabs = (CHUNKS, ff // 32, d)
    return pl.pallas_call(
        back_outer_kernel,
        grid_spec=pltpu.PrefetchScalarGridSpec(
            num_scalar_prefetch=1,
            grid=(4,),
            in_specs=[
                pl.BlockSpec((n, d), lambda i, s: (0, i)), pl.BlockSpec((n, d), lambda i, s: (0, 0)),
            ],
            out_specs=[pl.BlockSpec(memory_space=pl.ANY)] * 2,
            scratch_shapes=[
                pltpu.VMEM((d, d), f32), pltpu.VMEM(slabs, bf16), pltpu.VMEM(slabs, bf16),
                pltpu.SemaphoreType.DMA((2, CHUNKS)),
            ],
        ),
        out_shape=[shape_of(slabs, bf16)] * 2,
        compiler_params=PARAMS,
        name="back_outer",
        cost_estimate=lasts(11),
    )(where, g, df)


def put_sums(sums1_ref, sums2_ref, bsum_ref, val_ref):
    d = sums1_ref.shape[1]
    r = d // 32
    rows = [sums1_ref[...], sums2_ref[...], jnp.zeros((112, d), f32)]
    val_ref[:, :128] = jnp.concatenate(rows, 0).T
    lane = lax.broadcasted_iota(jnp.int32, (1, 128), 1)
    mine = (lane >= 16) & (lane < 16 + 4 * r)
    for i in range(32):
        row = bsum_ref[i // 8 : i // 8 + 1, :]
        part = pltpu.roll(row, (16 - i % 8 * 4 * r) % d, 1)[:, :128]
        val_ref[i * r : i * r + 1, :128] += jnp.where(mine, part, 0.0)


def mid_outer_kernel(
    where_ref, h_ref, du_ref, o_ref, da_ref, sums1_ref, sums2_ref, bsum_ref,
    keep_ref, send_ref, val_ref,
):
    step = pl.program_id(0)

    @pl.when(step < 4)
    def _():
        outer_slabs(where_ref, h_ref[...], du_ref[...], val_ref, keep_ref, send_ref, 0, CHUNKS)

    @pl.when(step == 4)
    def _():
        outer_slabs(where_ref, o_ref[...], da_ref[...], val_ref, keep_ref, send_ref, 0, CHUNKS)

    @pl.when(step == 5)
    def _():
        put_sums(sums1_ref, sums2_ref, bsum_ref, val_ref)
        put_slabs(where_ref, val_ref.at[:, :128], keep_ref, send_ref, 0, CHUNKS, slice(0, 128))


def mid_outer(where, h, du, o, da, sums1, sums2, bsum):
    n, d = h.shape
    keep = lambda a: pl.BlockSpec(a.shape, lambda i, s: (0, 0))
    block = pl.BlockSpec((n, d), lambda i, s: (0, jnp.minimum(i, 3)))
    specs = [keep(h), block, keep(o), keep(da), keep(sums1), keep(sums2), keep(bsum)]
    return slab_call(
        mid_outer_kernel, "mid_outer", where, (6,), specs, (h, du, o, da, sums1, sums2, bsum), d // 32,
        5 * d + 128, [pltpu.VMEM((d, d), f32)], 14, d,
    )


def qkv_outer_kernel(where_ref, x_ref, *refs):
    grad_refs, (keep_ref, send_ref, val_ref, sums_ref) = refs[:-4], refs[-4:]
    step = pl.program_id(0)

    @pl.when(step == 0)
    def _():
        sums_ref[...] = jnp.zeros_like(sums_ref)

    @pl.when(step < 3)
    def _():
        at = 0
        for ref in grad_refs:
            grads = ref[0]
            cols = slice(at, at + ref.shape[2])
            at += ref.shape[2]
            part = val_ref.at[:, cols]
            part[...] = dot(x_ref[...], grads, TN)
            put_slabs(where_ref, part, keep_ref, send_ref, 0, CHUNKS, cols)
            total = jnp.sum(grads.astype(f32), axis=0, keepdims=True)
            sums_ref[pl.ds(step, 1), cols] = total

    @pl.when(step == 3)
    def _():
        val_ref[:, :128] = sums_ref[...].T
        put_slabs(where_ref, val_ref.at[:, :128], keep_ref, send_ref, 0, CHUNKS, slice(0, 128))


def qkv_outer(where, x, grads):
    n, d = x.shape
    block = lambda a: pl.BlockSpec((1, n, a.shape[2]), lambda i, s: (jnp.minimum(i, 2), 0, 0))
    specs = [pl.BlockSpec((n, d), lambda i, s: (0, 0))] + [block(a) for a in grads]
    return slab_call(
        qkv_outer_kernel, "qkv_outer", where, (4,), specs, (x, *grads), d // 32, 3 * d + 128,
        [pltpu.VMEM((d, d), f32), pltpu.VMEM((128, d), f32)], 10, d,
    )


def input_grad_kernel(dr_ref, *refs):
    grad_refs, (wq_ref, wk_ref, wv_ref, out_ref) = refs[:-4], refs[-4:]
    total = dr_ref[...]
    for i, w_ref in enumerate((wq_ref, wk_ref, wv_ref)):
        at = 0
        for ref in grad_refs:
            w = flat(w_ref[:, :, :, at : at + ref.shape[2]])
            at += ref.shape[2]
            total = total + dot(ref[i], w, NT)
    out_ref[...] = total


def input_grad(dr, grads, pack, rows=256):
    n, d = dr.shape
    weight = lambda j: pl.BlockSpec((CHUNKS, 3, 16, d), lambda i: (0, j, 0, 0))
    return pl.pallas_call(
        input_grad_kernel,
        grid=(n // rows,),
        in_specs=[pl.BlockSpec((rows, d), lambda i: (i, 0))]
        + [pl.BlockSpec((3, rows, a.shape[2]), lambda i: (0, i, 0)) for a in grads]
        + [weight(0), weight(1), weight(2)],
        out_specs=pl.BlockSpec((rows, d), lambda i: (i, 0)),
        out_shape=shape_of((n, d)),
        compiler_params=room(36),
        name="input_grad",
        cost_estimate=lasts(9),
    )(dr, *grads, pack, pack, pack)


def bit_of(axis, bit):
    return (lax.axis_index(axis) // bit) % 2


def swap(x, axis, bits):
    size = lax.axis_size(axis)
    return lax.ppermute(x, axis, [(i, i ^ bits) for i in range(size)])


def ordered(mine, own, other):
    return jnp.where(mine == 0, own, other), jnp.where(mine == 0, other, own)


def gather_bit(x, axis, bit):
    first, second = ordered(bit_of(axis, bit), x, swap(x, axis, bit))
    return jnp.stack([first, second], 1).reshape((2 * x.shape[0],) + x.shape[1:])


def gather_two_bits(x, axis, high, low):
    a, b, c, d = x, swap(x, axis, low), swap(x, axis, high), swap(x, axis, high | low)
    a, b = ordered(bit_of(axis, low), a, b)
    c, d = ordered(bit_of(axis, low), c, d)
    a, c = ordered(bit_of(axis, high), a, c)
    b, d = ordered(bit_of(axis, high), b, d)
    return jnp.stack([a, b, c, d], 1).reshape((4 * x.shape[0],) + x.shape[1:])


def upper_bits():
    count = lax.axis_size("dp").bit_length() - 1
    return [1 << i for i in range(count - 1, 0, -1)]


def gather(x):
    rows, cols = x.shape
    x = x[None]
    bits = upper_bits()
    if len(bits) == 2:
        x = gather_two_bits(x, "dp", *bits)
    else:
        for bit in bits:
            x = gather_bit(x, "dp", bit)
    k = x.shape[0]
    one = gather_bit(gather_bit(x[:, :, : cols // 2], "dp", 1), "fsdp", 2)
    two = gather_bit(gather_bit(x[:, :, cols // 2 :], "fsdp", 2), "dp", 1)
    two = jnp.swapaxes(two.reshape(k, 2, 2, rows, cols // 2), 1, 2).reshape(one.shape)
    x = jnp.concatenate([one, two], -1)
    return gather_bit(x, "fsdp", 1)


def scatter_bit(x, axis, bit, dim):
    mine = bit_of(axis, bit)
    keep = lax.dynamic_index_in_dim(x, mine, dim, keepdims=False)
    send = lax.dynamic_index_in_dim(x, 1 - mine, dim, keepdims=False)
    return (keep.astype(f32) + swap(send, axis, bit).astype(f32)).astype(x.dtype)


def scatter_two_bits(x, axis, high, low):
    mine = bit_of(axis, high) * 2 + bit_of(axis, low)
    part = lambda i: lax.dynamic_index_in_dim(x, mine ^ i, 0, keepdims=False)
    total = part(0).astype(f32)
    for i, bits in ((1, low), (2, high), (3, high | low)):
        total = total + swap(part(i), axis, bits).astype(f32)
    return total


def scatter_sum(x):
    devices, rows, cols = x.shape
    bits = upper_bits()
    x = scatter_bit(x.reshape(devices // 8, 2, 2, 2, rows, cols), "fsdp", 1, 3)
    one = scatter_bit(scatter_bit(x[..., : cols // 2], "fsdp", 2, 2), "dp", 1, 1)
    two = scatter_bit(scatter_bit(x[..., cols // 2 :], "dp", 1, 1), "fsdp", 2, 1)
    x = jnp.concatenate([one, two], -1)
    if len(bits) == 2:
        return scatter_two_bits(x, "dp", *bits)
    x = x.reshape((2,) * len(bits) + (rows, cols))
    for bit in bits:
        x = scatter_bit(x, "dp", bit, 0)
    return x.astype(f32)


def seats():
    dp, fsdp = lax.axis_index("dp"), lax.axis_index("fsdp")
    return dp // 2, dp % 2, fsdp // 2, fsdp % 2


def swap_all(x, dz=0, first=0, second=0, core=0):
    pairs = []
    for i in range(32):
        z, y, xx, c = i // 8, i // 4 % 2, i // 2 % 2, i % 2
        dy, dx = (first, second) if c == 0 else (second, first)
        pairs.append((i, (((z ^ dz) * 2 + (y ^ dy)) * 2 + (xx ^ dx)) * 2 + (c ^ core)))
    return lax.ppermute(x, AXES, pairs)


def after(x, *others):
    return lax.optimization_barrier((x, *others))[0]


def halves_kernel(core_ref, wq_ref, wk_ref, wv_ref, wo_ref, wi_ref, wb_ref, own_ref, send_ref):
    r, d = wq_ref.shape
    for core, out in ((core_ref[0], own_ref), (1 - core_ref[0], send_ref)):
        half = lambda base: pl.ds(pl.multiple_of(base + core * (d // 2), 128), d // 2)
        for j in range(4):
            out[j] = wi_ref[:, half(j * d)]
        back = wb_ref[:, half(0)].astype(f32)
        for j in range(4):
            out[4 + j] = back[j * r : (j + 1) * r].astype(bf16)
        for j, ref in enumerate((wo_ref, wq_ref, wk_ref, wv_ref)):
            out[8 + j] = ref[:, half(0)]


def halves(core, *weights):
    r, d = weights[0].shape
    return pl.pallas_call(
        halves_kernel,
        in_specs=[pl.BlockSpec(memory_space=pltpu.SMEM)]
        + [pl.BlockSpec(memory_space=pltpu.VMEM)] * 6,
        out_specs=[pl.BlockSpec(memory_space=pltpu.VMEM)] * 2,
        out_shape=[shape_of((12, r, d // 2), bf16)] * 2,
        compiler_params=PARAMS,
        name="halves",
        cost_estimate=lasts(2),
    )(core, *weights)


def chip_kernel(core_ref, own_ref, got_ref, *refs):
    small, (one_ref, two_ref, rows_ref) = refs[:-3], refs[-3:]
    swapped = core_ref[0] == 1

    def put(out_ref, tile, start, count):
        own = own_ref[start : start + count].astype(f32)
        got = got_ref[start : start + count].astype(f32)
        low, high = jnp.where(swapped, got, own), jnp.where(swapped, own, got)
        rows = jnp.concatenate([a[i] for a in (low, high) for i in range(count)], 0).astype(bf16)
        tiles = rows.shape[0] // 16
        out_ref[tile : tile + tiles] = rows.reshape(tiles, 16, rows.shape[1])

    for j in range(4):
        put(two_ref, 12 + 3 * j, j, 1)
    put(two_ref, 24, 8, 1)
    put(two_ref, 0, 4, 4)
    for j in range(3):
        put(one_ref, 3 * j, 9 + j, 1)
    rows_ref[...] = jnp.zeros_like(rows_ref)
    for i, ref in enumerate(small):
        rows_ref[i : i + 1, : ref.shape[1]] = ref[...].astype(f32)
    one_ref[9] = rows_ref[...].astype(bf16)


def chip_shards(core, own, got, small):
    width = own.shape[2]
    return pl.pallas_call(
        chip_kernel,
        in_specs=[pl.BlockSpec(memory_space=pltpu.SMEM)]
        + [pl.BlockSpec(memory_space=pltpu.VMEM)] * (2 + len(small)),
        out_specs=[pl.BlockSpec(memory_space=pltpu.VMEM)] * 2,
        out_shape=[shape_of((tiles, 16, width), bf16) for tiles in (10, 27)],
        scratch_shapes=[pltpu.VMEM((16, width), f32)],
        compiler_params=PARAMS,
        name="chip_shards",
        cost_estimate=lasts(2),
    )(core, own, got, *[a[None] for a in small])


def pair_up(x, dz, *late):
    return jnp.concatenate([x, after(swap_all(x, dz=dz), *late)])


def near_pieces(stack):
    return [stack, swap_all(stack, first=1), swap_all(stack, second=1)]


class Scatter:
    def __init__(self, small_slice, keep, send, direct=False):
        self.state = (keep, send)
        self.small_slice = small_slice
        self.steps = 0
        self.total = None
        self.direct = direct

    def hold(self, *late):
        self.state = tuple(after(part, *late) for part in self.state)

    def step(self, *late):
        if not self.small_slice:
            return ()
        self.steps += 1
        hops = [{"core": 1}, {"second": 1}, {"first": 1}]
        if not self.direct:
            hops += [{"dz": 1}, {"dz": 2}]
        if self.steps <= len(hops):
            keep, send = self.state
            got = after(swap_all(send, **hops[self.steps - 1]), *late)
            total = keep.astype(f32) + got.astype(f32)
            if self.steps == 5:
                self.total = total[0]
                return (self.total,)
            total = total.astype(bf16)
            half = total.shape[0] // 2
            self.state = (total,) if self.direct and self.steps == 3 else (total[:half], total[half:])
            return self.state
        (parts,) = self.state
        total = parts[0].astype(f32)
        for i, dz in ((1, 2), (2, 1), (3, 3)):
            total = total + after(swap_all(parts[i], dz=dz), *late).astype(f32)
        self.total = total
        return (total,)

    def result(self, devices):
        if self.small_slice:
            while self.total is None:
                self.step()
            return self.total
        keep, send = self.state
        stacked = jnp.stack([keep, send], 1)
        return scatter_sum(stacked.reshape(devices, -1, keep.shape[-1]))


def places(lengths, n):
    ends = jnp.cumsum(lengths)
    start = jnp.sum(jnp.where(lengths == n // 2, ends - n // 2, 0))
    position = (start + n // 2 + jnp.arange(n // 2, dtype=jnp.int32)) % n
    segment = jnp.sum((position[:, None] >= ends[None, :]).astype(jnp.int32), axis=1)
    return start, segment.astype(f32)


def vectors(small, r, d):
    vec = jnp.transpose(small[:, : 8 * r].reshape(-1, 8, r), (1, 0, 2)).reshape(8, d)
    return vec, small[:, 8 * r : 12 * r].reshape(4, d)


def body(
    tokens, lengths, cotangent, w_query, w_key, w_value, w_out, b_query, b_value, b_out,
    norm1_gain, norm1_shift, w_in, w_back, b_in, b_back, norm2_gain, norm2_shift,
):
    _, n, d = tokens.shape
    devices = lax.axis_size("dp") * lax.axis_size("fsdp")
    r = w_query.shape[0]
    small_slice = lax.axis_size("dp") == 8 and lax.axis_size("fsdp") == 4
    start, segment = places(lengths[0], n)
    seg_row, seg_col = segment[None, :], segment[:, None]
    rolled = lambda a: jnp.roll(a[0], -start, axis=0)
    small = [b_query, b_value, b_out, norm1_gain, norm1_shift, b_back, norm2_gain, norm2_shift, b_in]
    if small_slice:
        z, y, across, core = seats()
        i = jnp.arange(32, dtype=jnp.int32)
        first, second = i // 4 % 2, i // 8 % 2
        other = (core + i // 16) % 2
        chip = ((z ^ (i % 2 * 2 + i // 2 % 2)) * 2 + (y ^ jnp.where(other == 0, first, second))) * 2
        chip = chip + (across ^ jnp.where(other == 0, second, first))
        gather_at = jnp.concatenate([core[None], chip])
        i = jnp.arange(16, dtype=jnp.int32)
        dz, dy_, dx = z ^ i // 4, y ^ i // 2 % 2, across ^ i % 2
        dz = dz % 2 * 2 + dz // 2
        slot = lambda c: jnp.where(c == 0, dx, dy_) * 8 + jnp.where(c == 0, dy_, dx) * 4 + dz
        where = jnp.concatenate([core[None], slot(core), slot(1 - core)])
        own, send = halves(core[None], w_query, w_key, w_value, w_out, w_in, w_back)
        one, two = chip_shards(core[None], own, swap_all(send, core=1), small)
        x = rolled(after(tokens, one))
        hop2 = swap_all(two, first=1)
        pair1 = pair_up(one[None], 2, x, gather_at, where, hop2)
        diag2 = swap_all(hop2, second=1)
        dy = rolled(after(cotangent, pair1))
        pair2 = pair_up(after(two, pair1)[None], 2)
        stack1 = pair_up(pair1, 1, dy, diag2)
        first1 = jnp.concatenate([stack1, after(swap_all(stack1, first=1), pair2)])
        stack2 = pair_up(pair2, 1, first1)
        pieces1 = [first1, swap_all(first1, second=1)]
        near2 = near_pieces(after(stack2, first1))
        far2 = [swap_all(after(diag2, stack2), dz=dz)[None] for dz in (2, 1, 3)]
        early2 = [swap_all(near2[0], core=1), swap_all(diag2, core=1)[None]]
        pieces1 += [swap_all(piece, core=1) for piece in pieces1]
        x = after(x, *early2)
    else:
        x, dy = rolled(tokens), rolled(cotangent)
        step = jnp.arange(16, dtype=jnp.int32)
        where = jnp.concatenate([jnp.zeros((1,), jnp.int32), step, step])
        gather_at = where
        small = jnp.concatenate(small)
        small = jnp.pad(small, (0, 8 * d - small.shape[0])).reshape(8, d)
        pack1 = gather(jnp.concatenate([w_query, w_key, w_value, small]))
        vec, bi = vectors(pack1[:, 3 * r], r, d)
        rows = jnp.pad(vec.reshape(8, 16, 2, -1), ((0, 0), (0, 0), (0, 0), (0, d // 2 - d // 32)))
        row = jnp.pad(bi.reshape(1, 16, 2, -1), ((0, 7), (0, 0), (0, 0), (0, d // 2 - d // 8)))
        small = jnp.transpose(jnp.concatenate([rows, row]), (1, 0, 2, 3)).reshape(16, 1, 16, d)
        tiles = lambda w: w.reshape(CHUNKS, -1, 16, d)
        pack1 = [tiles(pack1[:, i * r : (i + 1) * r]) for i in range(3)] + [small]
        pack2 = gather(jnp.concatenate([w_in[:, j * d : (j + 1) * d] for j in range(4)] + [w_back, w_out]))
        cuts = [(4, 8), (0, 1), (1, 2), (2, 3), (3, 4), (8, 9)]
        pack2 = [tiles(pack2[:, a * r : b * r]) for a, b in cuts]
        cut = lambda p: [
            jnp.concatenate(p, 1)[4 * i : 4 * i + 4, :, :, j * (d // 2) : (j + 1) * (d // 2)]
            for j in range(2)
            for i in range(4)
        ]
        pieces1, pieces2 = cut(pack1), cut(pack2)

    q, k, v, o, lse, vec, bi, pack1 = attend(gather_at, x, seg_row, seg_col, pieces1)
    if small_slice:
        late2 = lax.optimization_barrier((*near2[1:], *far2, o))[:-1]
        swapped = [swap_all(a, core=1) for a in late2]
        pieces2 = [near2[0], *late2[:2], diag2[None], *late2[2:]]
        pieces2 += [early2[0], *swapped[:2], early2[1], *swapped[2:]]
    mixed, h, zhat, inv, g, slope, dr, df, sums2, pack2 = forward(
        gather_at, x, o, dy, vec, bi, pieces2
    )
    scatter1 = Scatter(small_slice, *back_outer(where, g, df))
    du, dr1, da, do, sums1, bsum = backward(
        after(df, *scatter1.state), slope, dr, zhat, inv, pack2, vec
    )
    h_late = after(h, du, *scatter1.step(du))
    scatter2 = Scatter(small_slice, *mid_outer(where, h_late, du, o, da, sums1, sums2, bsum))
    late = after(q, *scatter1.step(*scatter2.state))
    scatter2.hold(late)
    grads = [attend_back(late, k, v, do, lse, seg_row, seg_col, 0, 1)]
    late = after(q, *scatter1.step(grads[0]), *scatter2.step(grads[0]))
    grads.append(attend_back(late, k, v, do, lse, seg_row, seg_col, 1, 2))
    late = after(x, *scatter2.step(grads[1]))
    scatter3 = Scatter(small_slice, *qkv_outer(where, late, grads), True)
    late = scatter2.step(*scatter3.state) + scatter1.step(*scatter3.state)
    late = late + scatter3.step(*late)
    grad_tokens = input_grad(after(dr1, *late), grads, pack1)
    late = scatter3.step(grad_tokens) + scatter2.step(grad_tokens) + scatter1.step(grad_tokens)
    unroll = lambda a, *late: jnp.roll(after(a, *late), start, axis=0)[None]
    mixed, grad_tokens = unroll(mixed, *late), unroll(grad_tokens, *late)
    scatter3.step(mixed, grad_tokens)
    scatter2.step(mixed, grad_tokens)
    mid_grad = scatter2.result(devices)
    back_grad = scatter1.result(devices)
    rest = scatter3.result(devices)
    gq, gk, gv = [rest[:, i * d : (i + 1) * d] for i in range(3)]
    gbq, _, gbv = rest[:, 3 * d : 3 * d + 3].T
    in_grad, out_grad = mid_grad[:, : 4 * d], mid_grad[:, 4 * d : 5 * d]
    vecs = mid_grad[:, 5 * d : 5 * d + 11].T
    if small_slice:
        gbi = mid_grad[0, 5 * d + 16 : 5 * d + 16 + 4 * r]
    else:
        gbi = lax.psum_scatter(bsum.reshape(4 * d), AXES, scatter_dimension=0, tiled=True)
    return (
        mixed, grad_tokens, gq, gk, gv, out_grad,
        gbq, gbv, vecs[0], vecs[1], vecs[2],
        in_grad, back_grad, gbi, vecs[8], vecs[9], vecs[10],
    )


def solution(mesh):
    act, mat, vec = P(AXES, None, None), P(AXES, None), P(AXES)
    return jax.shard_map(
        body,
        mesh=mesh,
        in_specs=(act, mat, act, mat, mat, mat, mat, vec, vec, vec, vec, vec, mat, mat, vec, vec, vec, vec),
        out_specs=(act, act, mat, mat, mat, mat, vec, vec, vec, vec, vec, mat, mat, vec, vec, vec, vec),
        check_vma=False,
    )
```
